32 devices in a mesh: img: 4 (over x, core), strip: 8 (over z, y).
Axes of the slice: x: 2, y: 2, z: 4, core: 2. Of those that a mesh axis runs over, the one named last changes fastest.
Arguments:
- images: bfloat16 [2, 4, 64, 64, 512], P(None, 'img', 'strip'), may hold values from -6 to 6
- cotangent: bfloat16 [2, 4, 64, 64, 512], P(None, 'img', 'strip'), may hold values from -6 to 6
- extent: int32 [2, 4, 2], P(None, 'img'), may hold values from 32 to 64, as said below
- w_qkv: bfloat16 [512, 1536], P(('img', 'strip')), may hold values from -0.25 to 0.25
- w_out: bfloat16 [512, 512], P(('img', 'strip')), may hold values from -0.25 to 0.25
- w_up: bfloat16 [512, 2048], P(('img', 'strip')), may hold values from -0.25 to 0.25
- w_down: bfloat16 [2048, 512], P(('img', 'strip')), may hold values from -0.125 to 0.125
- pos_weight: float32 [3, 3, 512], replicated, may hold values from -2 to 2
- win_three: float32 [3, 3, 128], replicated, may hold values from -2 to 2
- win_five: float32 [5, 5, 192], replicated, may hold values from -1.25 to 1.25
- win_seven: float32 [7, 7, 192], replicated, may hold values from -0.875 to 0.875
- gain_one: float32 [512], replicated, may hold values from 0.5 to 1.5
- gain_two: float32 [512], replicated, may hold values from 0.5 to 1.5
Outputs:
- out_images: bfloat16 [2, 4, 64, 64, 512], P(None, 'img', 'strip')
- grad_images: float32 [2, 4, 64, 64, 512], P(None, 'img', 'strip')
- grad_w_qkv: float32 [512, 1536], P(('img', 'strip'))
- grad_w_out: float32 [512, 512], P(('img', 'strip'))
- grad_w_up: float32 [512, 2048], P(('img', 'strip'))
- grad_w_down: float32 [2048, 512], P(('img', 'strip'))
- grad_pos: float32 [3, 3, 512], replicated
- grad_three: float32 [3, 3, 128], replicated
- grad_five: float32 [5, 5, 192], replicated
- grad_seven: float32 [7, 7, 192], replicated
- grad_gain_one: float32 [512], replicated
- grad_gain_two: float32 [512], replicated
The draws below stay inside these ranges and needn't reach their ends.
Inputs may be any that keep to these rules, and one draw needn't show every extreme that they name: `extent`: in each image column one micro-batch, drawn from the seed, has all 64 rows and all 64 columns valid; other images have more than 32 valid rows and 32 or more valid columns.
All inputs are finite; a program needn't handle non-finite values.
Results may differ from the reference program's by a relative error of at most 0.0091.
Values may be sent and summed in bfloat16 or wider, within the bound.
No kernel may reach another device: no remote copies, remote signals or barrier semaphores. Data moves between devices by JAX's collectives and lax.ppermute only.
A program may use at most 192 MiB of HBM per device.

```python
import jax
import jax.numpy as jnp
from jax import lax

D = 512
FF = 2048
HEADS = 8
HEAD_DIM = 64
COLS = 64
MICRO = 2
NROWS = 64
IMAGES = 4


def draw_extent(key, part):
    key = jax.random.fold_in(key, 11)
    first_key, second_key, third_key = jax.random.split(key, 3)
    valid_rows = jax.random.randint(first_key, (MICRO, IMAGES), NROWS // 2 + 1, NROWS + 1)
    valid_cols = jax.random.randint(second_key, (MICRO, IMAGES), COLS // 2, COLS + 1)
    chosen = jax.random.randint(third_key, (IMAGES,), 0, MICRO)
    picked = lax.broadcasted_iota(jnp.int32, (MICRO, IMAGES), 0) == chosen[None, :]
    valid_rows = jnp.where(picked, NROWS, valid_rows)
    valid_cols = jnp.where(picked, COLS, valid_cols)
    return jnp.stack([valid_rows, valid_cols], axis=-1).astype(jnp.int32)


def levels(stream_key, shape, cuts, least, high):
    def one(position, blocks):
        steps = jax.random.uniform(jax.random.fold_in(jax.random.fold_in(stream_key, 6), position), (blocks,), jnp.float32, least / len(cuts), high / len(cuts))
        return jnp.repeat(jnp.exp(steps), shape[position] // blocks).reshape((-1,) + (1,) * (len(shape) - position - 1))

    level = one(*cuts[0])
    for cut in cuts[1:]:
        level = level * one(*cut)
    return level


def normal_values(stream_key, shape, deviation, most, shards=(), held_as=jnp.bfloat16):
    entries = deviation * jax.random.normal(stream_key, shape, jnp.float32)
    if shards:
        entries = entries * levels(stream_key, shape, shards, -0.22, 0.18)
    return jnp.clip(entries, -most, most).astype(held_as)


def setup_inputs(seed: int = 0) -> dict:
    arg_keys = jax.random.split(jax.random.key(seed), 14)
    return {
        "images": normal_values(arg_keys[0], (MICRO, IMAGES, NROWS, COLS, D), 1.0, 6.0, ((1, 4), (2, 8))),
        "cotangent": normal_values(arg_keys[1], (MICRO, IMAGES, NROWS, COLS, D), 1.0, 6.0, ((1, 4), (2, 8))),
        "extent": draw_extent(jax.random.fold_in(arg_keys[13], 71), 0),
        "w_qkv": normal_values(arg_keys[3], (D, 3 * D), D ** -0.5, 0.25, ((0, 32),)),
        "w_out": normal_values(arg_keys[4], (D, D), D ** -0.5, 0.25, ((0, 32),)),
        "w_up": normal_values(arg_keys[5], (D, FF), D ** -0.5, 0.25, ((0, 32),)),
        "w_down": normal_values(arg_keys[6], (FF, D), FF ** -0.5, 0.125, ((0, 32),)),
        "pos_weight": normal_values(arg_keys[7], (3, 3, D), 9 ** -0.5, 2.0, (), jnp.float32),
        "win_three": normal_values(arg_keys[8], (3, 3, 2 * HEAD_DIM), 9 ** -0.5, 2.0, (), jnp.float32),
        "win_five": normal_values(arg_keys[9], (5, 5, 3 * HEAD_DIM), 25 ** -0.5, 1.25, (), jnp.float32),
        "win_seven": normal_values(arg_keys[10], (7, 7, 3 * HEAD_DIM), 49 ** -0.5, 0.875, (), jnp.float32),
        "gain_one": jnp.clip(1.0 + 0.1 * jax.random.normal(arg_keys[11], (D,), jnp.float32), 0.5, 1.5),
        "gain_two": jnp.clip(1.0 + 0.1 * jax.random.normal(arg_keys[12], (D,), jnp.float32), 0.5, 1.5),
    }


@jax.custom_vjp
def low(v):
    return lax.optimization_barrier(v.astype(jnp.bfloat16)).astype(jnp.float32)

@jax.custom_vjp
def low_back(v):
    return v

def low_keep(v):
    return (low(v), None)

def low_pass(kept, grad):
    return (grad,)

def back_keep(v):
    return (v, None)

def back_low(kept, grad):
    return (low(grad),)
low.defvjp(low_keep, low_pass)
low_back.defvjp(back_keep, back_low)
norm_eps = 1e-06
highest = lax.Precision.HIGHEST
masked_low = -1e+30

def layer_norm(fields, gain):
    average = lax.optimization_barrier(jnp.mean(fields, axis=-1, keepdims=True))
    centred = fields - average
    return centred * lax.rsqrt(lax.optimization_barrier(jnp.mean(centred * centred, axis=-1, keepdims=True)) + norm_eps) * gain

@jax.checkpoint
def depthwise(fields, weight):
    reach = weight.shape[0] // 2
    padded = jnp.pad(fields, ((reach, reach), (reach, reach), (0, 0)))
    height, breadth = (fields.shape[0], fields.shape[1])
    totals = jnp.zeros(fields.shape, jnp.float32)
    for tap_row in range(weight.shape[0]):
        for tap_col in range(weight.shape[1]):
            totals = totals + weight[tap_row, tap_col] * padded[tap_row:tap_row + height, tap_col:tap_col + breadth]
    return totals

def forward(picture, validity, w_qkv, w_out, w_up, w_down, pos_weight, win_three, win_five, win_seven, gain_one, gain_two):
    height, breadth, width = picture.shape
    tokens_all = height * breadth
    keep_mask = validity[:, :, None]
    flat_mask = validity.reshape(tokens_all, 1)
    masked_in = picture * keep_mask
    residual = ((masked_in + depthwise(masked_in, pos_weight)) * keep_mask).reshape(tokens_all, width)
    normed = low(layer_norm(residual, gain_one))
    qkv_all = low(low_back(jnp.dot(normed, w_qkv, precision=highest)))
    queries = qkv_all[:, :width]
    keys_flat = jnp.where(flat_mask > 0, qkv_all[:, width:2 * width], masked_low)
    values_flat = qkv_all[:, 2 * width:]
    key_top = lax.optimization_barrier(jnp.max(keys_flat, axis=0))
    exp_weights = jnp.exp(keys_flat - key_top) * flat_mask
    totals = lax.optimization_barrier(jnp.sum(exp_weights, axis=0)).reshape(HEADS, HEAD_DIM)
    summary = jnp.einsum('thc,the->hce', exp_weights.reshape(tokens_all, HEADS, HEAD_DIM), values_flat.reshape(tokens_all, HEADS, HEAD_DIM), precision=highest)
    normal_kv = summary / totals[:, :, None]
    factor = jnp.einsum('thc,hce->the', queries.reshape(tokens_all, HEADS, HEAD_DIM), normal_kv, precision=highest) * HEAD_DIM ** (-0.5)
    values_map = values_flat.reshape(height, breadth, width)
    edge_three = 2 * HEAD_DIM
    edge_five = 5 * HEAD_DIM
    conv_value = jnp.concatenate([depthwise(values_map[:, :, :edge_three], win_three), depthwise(values_map[:, :, edge_three:edge_five], win_five), depthwise(values_map[:, :, edge_five:], win_seven)], axis=-1)
    attended = low(factor.reshape(tokens_all, width) + queries * conv_value.reshape(tokens_all, width))
    middle = residual + low_back(jnp.dot(attended, w_out, precision=highest))
    normed_two = low(layer_norm(middle, gain_two))
    hidden = low_back(jnp.dot(normed_two, w_up, precision=highest))
    activated = low(jax.nn.gelu(hidden, approximate=False))
    ffn_out = low_back(jnp.dot(activated, w_down, precision=highest))
    return ((middle + ffn_out) * flat_mask).reshape(height, breadth, width)

def reference(images, cotangent, extent, w_qkv, w_out, w_up, w_down, pos_weight, win_three, win_five, win_seven, gain_one, gain_two):
    params = (w_qkv.astype(jnp.float32), w_out.astype(jnp.float32), w_up.astype(jnp.float32), w_down.astype(jnp.float32), pos_weight, win_three, win_five, win_seven, gain_one, gain_two)
    image_count = MICRO * IMAGES
    pictures = images.reshape(image_count, NROWS, COLS, D)
    cotangents = cotangent.reshape(image_count, NROWS, COLS, D)
    extents = extent.reshape(image_count, 2)
    row_ids = lax.broadcasted_iota(jnp.int32, (NROWS, COLS), 0)
    col_ids = lax.broadcasted_iota(jnp.int32, (NROWS, COLS), 1)

    def one_image(carry, item):
        picture, grad_top, bounds = item
        validity = ((row_ids < bounds[0]) & (col_ids < bounds[1])).astype(jnp.float32)

        def closed(picture_in, *weights):
            return forward(picture_in, validity, *weights)
        result, pull = jax.vjp(closed, picture.astype(jnp.float32), *params)
        grads = pull(grad_top.astype(jnp.float32))
        summed = tuple((running + fresh for running, fresh in zip(carry, grads[1:])))
        return (summed, (result.astype(jnp.bfloat16), grads[0]))
    start = tuple((jnp.zeros(param.shape, jnp.float32) for param in params))
    totals, (outputs, grad_in) = lax.scan(one_image, start, (pictures, cotangents, extents))
    shape_all = (MICRO, IMAGES, NROWS, COLS, D)
    return (outputs.reshape(shape_all), grad_in.reshape(shape_all), totals[0], totals[1], totals[2], totals[3], totals[4], totals[5], totals[6], totals[7], totals[8], totals[9])
```

```python
import math

import jax
import jax.numpy as jnp
from jax import lax
from jax.sharding import PartitionSpec as P

HEADS = 8


norm_eps = 1e-06
highest = lax.Precision.HIGHEST
masked_low = -1e30


def extended(cells, sides, width):
    for axis, dim in sides:
        count = lax.axis_size(axis)
        ends = count - 1
        head = lax.slice_in_dim(cells, 0, width, axis=dim)
        tail = lax.slice_in_dim(cells, cells.shape[dim] - width, cells.shape[dim], axis=dim)
        cells = jnp.concatenate(
            [
                lax.ppermute(tail, axis, [(i, (i + 1) % count) for i in range(ends)]),
                cells,
                lax.ppermute(head, axis, [((i + 1) % count, i) for i in range(ends)]),
            ],
            axis=dim,
        )
    return cells


def positions():
    count = lax.axis_size("strip")
    return lax.axis_index("img") * count + lax.axis_index("strip")


def flipped(cells, mask):
    count = lax.axis_size("img") * lax.axis_size("strip")
    return lax.ppermute(cells, ("img", "strip"), [(i, i ^ mask) for i in range(count)])


def plan(shard_rows):
    strip_bits = int(math.log2(lax.axis_size("strip")))
    img_bits = int(math.log2(lax.axis_size("img")))
    lead = 0
    while (shard_rows << lead) < 16:
        lead += 1
    free = [1 << b for b in range(lead, strip_bits)]
    first = free[-2:]
    second = free[:-2] + [1 << (strip_bits + b) for b in range(1, img_bits)]
    return [1 << b for b in range(lead)], first, second, [1 << strip_bits]


def spans(masks):
    out = [0]
    for mask in masks:
        out = out + [o ^ mask for o in out]
    return out


def gather_blocks(shards):
    lead, first, second, third = plan(shards[0].shape[0])
    me = positions()
    for mask in lead:
        bit = (me & mask) != 0
        others = [flipped(s, mask) for s in shards]
        shards = [
            jnp.where(bit, jnp.concatenate([o, s]), jnp.concatenate([s, o]))
            for s, o in zip(shards, others)
        ]
    cur = [s[None] for s in shards]
    for stage in (first, second, third):
        parts = [[c] for c in cur]
        for mask in spans(stage)[1:]:
            for part, c in zip(parts, cur):
                part.append(flipped(c, mask))
        cur = [jnp.concatenate(part) for part in parts]
    order = [0]
    for stage in (first, second, third):
        order = [o ^ m for m in spans(stage) for o in order]
    return cur, order, len(lead)


def gather_rows(shards):
    blocks, order, lead = gather_blocks(shards)
    me = positions() >> lead
    where = [0] * len(order)
    for slot, mask in enumerate(order):
        where[mask >> lead] = slot
    slots = jnp.asarray(where)[jnp.arange(len(order)) ^ me]
    return [b[slots].reshape(-1, b.shape[-1]) for b in blocks]


def scatter_rows(grads, shard_rows):
    lead, first, second, third = plan(16)
    strip_bits = int(math.log2(lax.axis_size("strip")))
    first = [1 << b for b in range(max(0, strip_bits - 2), strip_bits)]
    rest = [1 << b for b in range(0, max(0, strip_bits - 2))]
    high = [m for m in second if m >= (1 << strip_bits)]
    stages = [third, high + rest[-1:], first] + ([rest[:-1]] if rest[:-1] else [])
    order = [0]
    for stage in reversed(stages):
        order = [o ^ m for m in spans(stage) for o in order]
    me = positions()
    slots = jnp.asarray(order) ^ me
    cur = []
    for g, rows in zip(grads, shard_rows):
        cur.append(g.reshape(len(order), rows, g.shape[-1])[slots])
    for stage in stages:
        masks = spans(stage)
        nxt = []
        for c in cur:
            size = c.shape[0] // len(masks)
            total = c[:size]
            for k, mask in enumerate(masks[1:], 1):
                got = flipped(c[k * size : (k + 1) * size].astype(jnp.bfloat16), mask)
                total = total + got.astype(jnp.float32)
            nxt.append(total)
        cur = nxt
    return [c[0] for c in cur]


def strip_sum(cells):
    count = lax.axis_size("strip")
    mask = 1
    while mask < count:
        low = cells.astype(jnp.bfloat16)
        got = lax.ppermute(low, "strip", [(i, i ^ mask) for i in range(count)])
        cells = low.astype(jnp.float32) + got.astype(jnp.float32)
        mask *= 2
    return cells


def all_sum(cells):
    _, first, second, third = plan(16)
    for stage in (third, second, first):
        masks = spans(stage)
        got = [cells] + [flipped(cells, m) for m in masks[1:]]
        while len(got) > 1:
            got = [a + b for a, b in zip(got[::2], got[1::2])]
        cells = got[0]
    return cells


def transposed_product(left_side, right_side):
    return lax.dot_general(
        left_side, right_side, (((0,), (0,)), ((), ())), preferred_element_type=jnp.float32
    )


def product_back(left_side, right_side):
    return lax.dot_general(
        left_side, right_side, (((1,), (1,)), ((), ())), preferred_element_type=jnp.float32
    )


def norm_forward(fields, gain):
    average = jnp.mean(fields, axis=-1, keepdims=True)
    centred = fields - average
    inverse_std = lax.rsqrt(jnp.mean(centred * centred, axis=-1, keepdims=True) + norm_eps)
    unit_rows = centred * inverse_std
    return (unit_rows * gain, unit_rows, inverse_std)


def norm_backward(grad_norm, unit_rows, inverse_std, gain):
    grad_unit = grad_norm * gain
    grad_fields = inverse_std * (
        grad_unit
        - jnp.mean(grad_unit, axis=-1, keepdims=True)
        - unit_rows * jnp.mean(grad_unit * unit_rows, axis=-1, keepdims=True)
    )
    return (grad_fields, jnp.sum(grad_norm * unit_rows, axis=0))


def gelu_slope(hidden):
    return 0.5 * (1.0 + lax.erf(hidden / math.sqrt(2.0))) + hidden * jnp.exp(
        -0.5 * hidden * hidden
    ) / math.sqrt(2.0 * math.pi)


def apply_taps(padded, weight, strip_rows, strip_cols):
    window_size = weight.shape[0]
    totals = jnp.zeros((strip_rows, strip_cols, weight.shape[2]), jnp.float32)
    for tap_row in range(window_size):
        for tap_col in range(window_size):
            totals = (
                totals
                + weight[tap_row, tap_col]
                * padded[tap_row : tap_row + strip_rows, tap_col : tap_col + strip_cols]
            )
    return totals


def tap_grads(grad_map, padded, window_size):
    strip_rows, strip_cols = (grad_map.shape[0], grad_map.shape[1])
    tap_table = []
    for tap_row in range(window_size):
        tap_line = []
        for tap_col in range(window_size):
            tap_line.append(
                jnp.sum(
                    grad_map
                    * padded[tap_row : tap_row + strip_rows, tap_col : tap_col + strip_cols],
                    axis=(0, 1),
                )
            )
        tap_table.append(jnp.stack(tap_line))
    return jnp.stack(tap_table)


def window_input(rim_rows, low_edge, high_edge, window_size, strip_rows):
    reach = window_size // 2
    part_rows = rim_rows[3 - reach : 3 + strip_rows + reach, :, low_edge:high_edge].astype(
        jnp.float32
    )
    return jnp.pad(part_rows, ((0, 0), (reach, reach), (0, 0)))


def local(
    images,
    cotangent,
    extent,
    w_qkv,
    w_out,
    w_up,
    w_down,
    pos_weight,
    win_three,
    win_five,
    win_seven,
    gain_one,
    gain_two,
):
    micro_count, _, strip_rows, strip_cols, width = images.shape
    head_count = HEADS
    head_size = width // head_count
    edge_three = 2 * head_size
    edge_five = 5 * head_size
    attn_scale = head_size ** (-0.5)
    tokens_here = strip_rows * strip_cols
    row_global = lax.axis_index("strip") * strip_rows + lax.broadcasted_iota(
        jnp.int32, (strip_rows, strip_cols), 0
    )
    col_global = lax.broadcasted_iota(jnp.int32, (strip_rows, strip_cols), 1)
    windows = (
        (0, edge_three, win_three),
        (edge_three, edge_five, win_five),
        (edge_five, width, win_seven),
    )
    grad_qkv = 0.0
    grad_out = 0.0
    grad_up = 0.0
    grad_down = 0.0
    grad_pos = 0.0
    grad_wins = [0.0, 0.0, 0.0]
    grad_gain_one = 0.0
    grad_gain_two = 0.0
    outputs = []
    grads_in = []
    (full_qkv,) = gather_rows([w_qkv])
    full_out, full_up = gather_rows([w_out, w_up])
    (full_down,) = gather_rows([w_down])
    back_qkv, back_out, back_up, back_down = full_qkv, full_out, full_up, full_down
    for micro_index in range(micro_count):
        bounds = extent[micro_index, 0]
        validity = ((row_global < bounds[0]) & (col_global < bounds[1])).astype(jnp.float32)
        keep_mask = validity[:, :, None]
        flat_mask = validity.reshape(tokens_here, 1)
        masked_in = images[micro_index, 0].astype(jnp.float32) * keep_mask
        pos_rim = extended(masked_in.astype(jnp.bfloat16), (("strip", 0),), 1).astype(
            masked_in.dtype
        )
        pos_padded = jnp.pad(pos_rim, ((0, 0), (1, 1), (0, 0)))
        residual = (
            (masked_in + apply_taps(pos_padded, pos_weight, strip_rows, strip_cols)) * keep_mask
        ).reshape(tokens_here, width)
        normed, unit_one, inverse_one = norm_forward(residual, gain_one)
        normed_low = normed.astype(jnp.bfloat16)
        qkv_low = jnp.dot(normed_low, full_qkv, preferred_element_type=jnp.float32).astype(
            jnp.bfloat16
        )
        queries = qkv_low[:, :width].astype(jnp.float32)
        keys_flat = jnp.where(
            flat_mask > 0, qkv_low[:, width : 2 * width].astype(jnp.float32), masked_low
        )
        value_heads = (
            qkv_low[:, 2 * width :].astype(jnp.float32).reshape(tokens_here, head_count, head_size)
        )
        key_top = jnp.max(keys_flat, axis=0)
        exp_weights = jnp.exp(keys_flat - key_top) * flat_mask
        local_kv = jnp.einsum(
            "thc,the->hce",
            exp_weights.reshape(tokens_here, head_count, head_size),
            value_heads,
            precision=highest,
        )
        top_all = key_top
        for mask in [1 << b for b in range(int(math.log2(lax.axis_size("strip"))))]:
            count = lax.axis_size("strip")
            top_all = jnp.maximum(
                top_all, lax.ppermute(top_all, "strip", [(i, i ^ mask) for i in range(count)])
            )
        rescale = jnp.exp(key_top - top_all)
        exp_weights = exp_weights * rescale
        packed = jnp.concatenate(
            [
                local_kv * rescale.reshape(head_count, head_size, 1),
                jnp.broadcast_to(
                    jnp.sum(exp_weights, axis=0).reshape(head_count, head_size, 1),
                    (head_count, head_size, head_size),
                ),
            ],
            axis=-1,
        )
        packed = strip_sum(packed)
        summary = packed[..., :head_size]
        totals = packed[..., head_size].reshape(width)
        normal_kv = summary / totals.reshape(head_count, head_size, 1)
        query_heads = queries.reshape(tokens_here, head_count, head_size)
        factor = jnp.einsum("thc,hce->the", query_heads, normal_kv, precision=highest) * attn_scale
        value_rim = extended(
            qkv_low[:, 2 * width :].reshape(strip_rows, strip_cols, width), (("strip", 0),), 3
        )
        value_inputs = [
            window_input(value_rim, low_edge, high_edge, weight.shape[0], strip_rows)
            for low_edge, high_edge, weight in windows
        ]
        conv_value = jnp.concatenate(
            [
                apply_taps(padded, window_spec[2], strip_rows, strip_cols)
                for padded, window_spec in zip(value_inputs, windows)
            ],
            axis=-1,
        ).reshape(tokens_here, width)
        att_low = (factor.reshape(tokens_here, width) + queries * conv_value).astype(jnp.bfloat16)
        middle = residual + jnp.dot(att_low, full_out, preferred_element_type=jnp.float32)
        normed_two, unit_two, inverse_two = norm_forward(middle, gain_two)
        two_low = normed_two.astype(jnp.bfloat16)
        hidden = jnp.dot(two_low, full_up, preferred_element_type=jnp.float32)
        act_low = jax.nn.gelu(hidden, approximate=False).astype(jnp.bfloat16)
        result = (
            middle + jnp.dot(act_low, full_down, preferred_element_type=jnp.float32)
        ) * flat_mask
        outputs.append(result.astype(jnp.bfloat16).reshape(1, strip_rows, strip_cols, width))
        grad_top = (
            cotangent[micro_index, 0].astype(jnp.float32).reshape(tokens_here, width) * flat_mask
        )
        ffn_low = grad_top.astype(jnp.bfloat16)
        grad_down = grad_down + transposed_product(act_low, ffn_low)
        hidden_low = (product_back(ffn_low, back_down) * gelu_slope(hidden)).astype(jnp.bfloat16)
        grad_up = grad_up + transposed_product(two_low, hidden_low)
        grad_middle, gain_term = norm_backward(
            product_back(hidden_low, back_up), unit_two, inverse_two, gain_two
        )
        grad_middle = grad_middle + grad_top
        grad_gain_two = grad_gain_two + gain_term
        middle_low = grad_middle.astype(jnp.bfloat16)
        grad_out = grad_out + transposed_product(att_low, middle_low)
        grad_att = product_back(middle_low, back_out)
        grad_conv = (grad_att * queries).reshape(strip_rows, strip_cols, width)
        grad_heads = grad_att.reshape(tokens_here, head_count, head_size)
        grad_queries = (
            grad_att * conv_value
            + jnp.einsum("the,hce->thc", grad_heads, normal_kv, precision=highest).reshape(
                tokens_here, width
            )
            * attn_scale
        )
        grad_kv = strip_sum(
            jnp.einsum("thc,the->hce", query_heads, grad_heads, precision=highest) * attn_scale
        )
        key_probs = (exp_weights / totals).reshape(tokens_here, head_count, head_size)
        inner_kv = jnp.sum(grad_kv * normal_kv, axis=-1)
        grad_keys = key_probs * (
            jnp.einsum("the,hce->thc", value_heads, grad_kv, precision=highest) - inner_kv
        )
        grad_values = jnp.einsum("thc,hce->the", key_probs, grad_kv, precision=highest).reshape(
            tokens_here, width
        )
        conv_rim = extended(grad_conv.astype(jnp.bfloat16), (("strip", 0),), 3).astype(
            grad_conv.dtype
        )
        back_parts = []
        for window_index in range(3):
            low_edge, high_edge, weight = windows[window_index]
            window_size = weight.shape[0]
            back_parts.append(
                apply_taps(
                    window_input(conv_rim, low_edge, high_edge, window_size, strip_rows),
                    weight[::-1, ::-1],
                    strip_rows,
                    strip_cols,
                )
            )
            grad_wins[window_index] = grad_wins[window_index] + tap_grads(
                grad_conv[:, :, low_edge:high_edge], value_inputs[window_index], window_size
            )
        grad_values = grad_values + jnp.concatenate(back_parts, axis=-1).reshape(tokens_here, width)
        grad_qkv_low = jnp.concatenate(
            [grad_queries, grad_keys.reshape(tokens_here, width), grad_values], axis=1
        ).astype(jnp.bfloat16)
        grad_qkv = grad_qkv + transposed_product(normed_low, grad_qkv_low)
        grad_norm_in, gain_term = norm_backward(
            product_back(grad_qkv_low, back_qkv), unit_one, inverse_one, gain_one
        )
        grad_gain_one = grad_gain_one + gain_term
        grad_inner = ((grad_norm_in + grad_middle) * flat_mask).reshape(
            strip_rows, strip_cols, width
        )
        inner_rim = extended(grad_inner.astype(jnp.bfloat16), (("strip", 0),), 1).astype(
            grad_inner.dtype
        )
        grad_start = (
            grad_inner
            + apply_taps(
                jnp.pad(inner_rim, ((0, 0), (1, 1), (0, 0))),
                pos_weight[::-1, ::-1],
                strip_rows,
                strip_cols,
            )
        ) * keep_mask
        grad_pos = grad_pos + tap_grads(grad_inner, pos_padded, 3)
        grads_in.append(grad_start.reshape(1, strip_rows, strip_cols, width))
    grad_out, grad_up, grad_down = scatter_rows(
        [grad_out, grad_up, grad_down], [w_out.shape[0], w_up.shape[0], w_down.shape[0]]
    )
    (grad_qkv,) = scatter_rows([grad_qkv], [w_qkv.shape[0]])
    small = [grad_pos, grad_wins[0], grad_wins[1], grad_wins[2], grad_gain_one, grad_gain_two]
    flat = jnp.concatenate([s.reshape(-1) for s in small])
    flat = all_sum(flat.reshape(-1, 128)).reshape(-1)
    small_sums = []
    at = 0
    for s in small:
        rows = s.size
        small_sums.append(flat[at : at + rows].reshape(s.shape))
        at += rows
    return (
        jnp.stack(outputs),
        jnp.stack(grads_in),
        grad_qkv,
        grad_out,
        grad_up,
        grad_down,
        small_sums[0],
        small_sums[1],
        small_sums[2],
        small_sums[3],
        small_sums[4],
        small_sums[5],
    )


def solution(mesh):
    in_specs = (
        P(None, "img", "strip", None, None),
        P(None, "img", "strip", None, None),
        P(None, "img", None),
        P(("img", "strip"), None),
        P(("img", "strip"), None),
        P(("img", "strip"), None),
        P(("img", "strip"), None),
        P(),
        P(),
        P(),
        P(),
        P(),
        P(),
    )
    out_specs = (
        P(None, "img", "strip", None, None),
        P(None, "img", "strip", None, None),
        P(("img", "strip"), None),
        P(("img", "strip"), None),
        P(("img", "strip"), None),
        P(("img", "strip"), None),
        P(),
        P(),
        P(),
        P(),
        P(),
        P(),
    )
    return jax.shard_map(local, mesh=mesh, in_specs=in_specs, out_specs=out_specs, check_vma=False)
```

```python
import functools
import math

import jax
import jax.numpy as jnp
from jax import lax
from jax.experimental import pallas as pl
from jax.experimental.pallas import tpu as pltpu
from jax.sharding import PartitionSpec as P

HEADS = 8
norm_eps = 1e-06
masked_low = -1e30
RIM = 3
EDGE = 8
BF = jnp.bfloat16
F32 = jnp.float32
MIB = 2**20


def positions():
    return lax.axis_index("img") * lax.axis_size("strip") + lax.axis_index("strip")


def flipped(cells, mask):
    count = lax.axis_size("img") * lax.axis_size("strip")
    return lax.ppermute(cells, ("img", "strip"), [(i, i ^ mask) for i in range(count)])


def plan(shard_rows):
    strip_bits = int(math.log2(lax.axis_size("strip")))
    img_bits = int(math.log2(lax.axis_size("img")))
    lead = 0
    while (shard_rows << lead) < 16:
        lead += 1
    free = [1 << b for b in range(lead, strip_bits)]
    first = free[-2:]
    second = free[:-2] + [1 << (strip_bits + b) for b in range(1, img_bits)]
    return [1 << b for b in range(lead)], first, second, [1 << strip_bits]


def spans(masks):
    out = [0]
    for mask in masks:
        out = out + [o ^ mask for o in out]
    return out


def join_lead(shard, lead):
    me = positions()
    for mask in lead:
        other = flipped(shard, mask)
        shard = jnp.where(
            (me & mask) != 0, jnp.concatenate([other, shard]), jnp.concatenate([shard, other])
        )
    return shard


def gather_pieces(block, stages):
    first, second, third = stages
    own = jnp.concatenate([block[None]] + [flipped(block, m)[None] for m in spans(first)[1:]])
    pieces = [own] + [flipped(own, m) for m in spans(second)[1:]]
    marks = spans(second)
    for mask in third:
        pieces = pieces + [flipped(p, mask) for p in pieces]
        marks = marks + [m ^ mask for m in marks]
    return pieces, [[m ^ f for f in spans(first)] for m in marks]


def all_sum(cells, stages):
    for stage in stages:
        masks = spans(stage)
        got = [cells] + [flipped(cells, m) for m in masks[1:]]
        while len(got) > 1:
            got = [a + b for a, b in zip(got[::2], got[1::2])]
        cells = got[0]
    return cells


def strip_swap(cells, mask):
    count = lax.axis_size("strip")
    return lax.ppermute(cells, "strip", [(i, i ^ mask) for i in range(count)])


def strip_masks():
    return [1 << b for b in range(int(math.log2(lax.axis_size("strip"))))]


def strip_sum(cells):
    for mask in strip_masks():
        low = cells.astype(BF)
        cells = low.astype(F32) + strip_swap(low, mask).astype(F32)
    return cells


def rims(cells, width):
    count = lax.axis_size("strip")
    above = lax.ppermute(
        cells[:, -width:], "strip", [(i, i + 1) for i in range(count - 1)]
    )
    below = lax.ppermute(cells[:, :width], "strip", [(i + 1, i) for i in range(count - 1)])
    return above, below


def dot(a, b):
    return jnp.dot(a, b, preferred_element_type=F32)


def dot_nt(a, b):
    return lax.dot_general(a, b, (((1,), (1,)), ((), ())), preferred_element_type=F32)


def dot_tn(a, b):
    return lax.dot_general(a, b, (((0,), (0,)), ((), ())), preferred_element_type=F32)


def valid_rows(sc, micro, first_row, rows, cols):
    n = rows * cols
    flat = lax.broadcasted_iota(jnp.int32, (n, 1), 0)
    row = flat // cols + (sc[1] + first_row)
    col = flat % cols
    ok = (row >= 0) & (row < sc[4 + 2 * micro]) & (col < sc[5 + 2 * micro])
    return jnp.where(ok, 1.0, 0.0).astype(F32)


def unit_rows(fields):
    average = jnp.mean(fields, axis=-1, keepdims=True)
    centred = fields - average
    inverse = lax.rsqrt(jnp.mean(centred * centred, axis=-1, keepdims=True) + norm_eps)
    return centred * inverse, inverse


def norm_back(dy, unit, inverse, gain):
    dyg = dy * gain
    first = jnp.mean(dyg, axis=-1, keepdims=True)
    second = jnp.mean(dyg * unit, axis=-1, keepdims=True)
    return inverse * (dyg - first - unit * second)


def clear_edges(pad):
    groups, rows, cols, _ = pad.shape
    zeros = jnp.zeros((rows, EDGE, 128), F32)
    for g in range(groups):
        pad[g, :, :EDGE, :] = zeros
        pad[g, :, cols - EDGE :, :] = zeros


def put_row(pad, row, cells):
    for g in range(pad.shape[0]):
        pad[g, row, EDGE : EDGE + cells.shape[0], :] = cells[:, g * 128 : (g + 1) * 128]


def tap_row(pad, w_ref, lanes, group, row, cols, size, centre, flip):
    reach = size // 2
    total = jnp.zeros((cols, 128), F32)
    for i in range(size):
        for j in range(size):
            at = i * size + j
            if flip:
                at = size * size - 1 - at
            w = w_ref[at : at + 1, lanes : lanes + 128]
            total = total + w * pad[
                group, row + i - reach, EDGE + j - reach : EDGE + j - reach + cols, :
            ]
    return total


def tap_sums(pad, grad_ref, out_ref, lanes, group, rows, cols, size, above):
    reach = size // 2
    blocks = cols // 8

    def step(t, sums):
        r = t // blocks
        c = pl.multiple_of((t % blocks) * 8, 8)
        g = grad_ref[0, r, pl.ds(c, 8), group * 128 : (group + 1) * 128]
        out = []
        for i in range(size):
            for j in range(size):
                f = pad[group, r + above + i - reach, pl.ds(c + EDGE + j - reach, 8), :]
                out.append(sums[i * size + j] + g * f)
        return tuple(out)

    start = tuple(jnp.zeros((8, 128), F32) for _ in range(size * size))
    sums = lax.fori_loop(0, rows * blocks, step, start)
    for at in range(size * size):
        out_ref[at : at + 1, lanes : lanes + 128] += jnp.sum(sums[at], axis=0, keepdims=True)


def block_diagonal(wide, head):
    lane = lax.broadcasted_iota(jnp.int32, wide.shape, 1) // head
    return jnp.concatenate(
        [jnp.where(lane == h, wide, 0.0) for h in range(wide.shape[1] // head)], axis=0
    )


def diagonal_blocks(full, head):
    lane = lax.broadcasted_iota(jnp.int32, (head, full.shape[1]), 1) // head
    total = jnp.zeros((head, full.shape[1]), F32)
    for h in range(full.shape[1] // head):
        total = total + jnp.where(lane == h, full[h * head : (h + 1) * head], 0.0)
    return total


def fetch(sc, pieces, marks, lead, targets, sem):
    place = sc[0] >> lead
    for piece, mark in zip(pieces, marks):
        for k, mask in enumerate(mark):
            block = place ^ (mask >> lead)
            for whole, lane, lanes, parts in targets:
                for part in range(parts):
                    at = pl.multiple_of(block * (16 * parts) + 16 * part, 16)
                    pltpu.make_async_copy(
                        piece.at[k, :, pl.ds(lane + part * lanes, lanes)],
                        whole.at[pl.ds(at, 16), :],
                        sem,
                    ).start()


def norm_kernel(sc, x_ref, top_ref, bot_ref, w_ref, gain_ref, normed_ref, resid_ref, pad):
    micro = pl.program_id(0)
    rows, cols = x_ref.shape[2], x_ref.shape[3]
    halo = top_ref.shape[1]
    clear_edges(pad)

    def fill(source, count, first):
        def one(r, carry):
            cells = source(r).astype(F32)
            ok = valid_rows(sc, micro, first + r, 1, cols)
            put_row(pad, first + halo + r, cells * ok)
            return carry

        lax.fori_loop(0, count, one, 0)

    fill(lambda r: top_ref[0, r], halo, -halo)
    fill(lambda r: x_ref[0, 0, r], rows, 0)
    fill(lambda r: bot_ref[0, r], halo, rows)
    gain = gain_ref[...]

    def one(r, carry):
        ok = valid_rows(sc, micro, r - RIM, 1, cols)
        at = r + halo - RIM
        parts = []
        for g in range(pad.shape[0]):
            taps = tap_row(pad, w_ref, g * 128, g, at, cols, 3, None, False)
            parts.append((taps + pad[g, at, EDGE : EDGE + cols, :]) * ok)
        resid = jnp.concatenate(parts, axis=1)
        unit, _ = unit_rows(resid)
        normed_ref[0, r] = (unit * gain).astype(BF)

        @pl.when((r >= RIM) & (r < RIM + rows))
        def _():
            resid_ref[0, r - RIM] = resid

        return carry

    lax.fori_loop(0, rows + 2 * RIM, one, 0)


def qkv_kernel(marks, lead, sc, n_ref, *refs):
    pieces = refs[: len(marks)]
    q_ref, k_ref, v_ref, sums_ref, whole, sem = refs[len(marks) :]
    micro = pl.program_id(0)
    rows, cols, width = n_ref.shape[1] - 2 * RIM, n_ref.shape[2], n_ref.shape[3]
    head = width // HEADS
    tokens = rows * cols

    @pl.when(micro == 0)
    def _():
        fetch(sc, pieces, marks, lead, [(whole, 0, 3 * width, 1)], sem)
        pltpu.make_async_copy(whole, whole, sem).wait()

    normed = n_ref[0, RIM : RIM + rows].reshape(tokens, width)
    q_ref[0] = dot(normed, whole[:, :width]).astype(BF)
    k = dot(normed, whole[:, width : 2 * width]).astype(BF)
    k_ref[0] = k
    w_v = whole[:, 2 * width :]
    v = dot(normed, w_v).astype(BF)
    v_ref[0, RIM : RIM + rows] = v.reshape(rows, cols, width)
    rim = n_ref[0, :RIM].reshape(RIM * cols, width)
    v_ref[0, :RIM] = dot(rim, w_v).astype(BF).reshape(RIM, cols, width)
    rim = n_ref[0, RIM + rows :].reshape(RIM * cols, width)
    v_ref[0, RIM + rows :] = dot(rim, w_v).astype(BF).reshape(RIM, cols, width)
    ok = valid_rows(sc, micro, 0, rows, cols)
    keys = jnp.where(ok > 0, k.astype(F32), masked_low)
    top = jnp.max(keys, axis=0, keepdims=True)
    ew = jnp.exp(keys - top) * ok
    total = jnp.sum(ew, axis=0, keepdims=True)
    low = ew.astype(BF)
    half = 4 * head
    for b in range(width // half):
        full = dot_tn(v[:, b * half : (b + 1) * half], low[:, b * half : (b + 1) * half])
        sums_ref[0, :head, b * half : (b + 1) * half] = diagonal_blocks(full, head).astype(BF)
    line = lax.broadcasted_iota(jnp.int32, (16, width), 0)
    sums_ref[0, head:, :] = jnp.where(line == 0, total, jnp.where(line == 1, top, 0.0)).astype(BF)


def window_kernel(v_ref, w3, w5, w7, o_ref, pad):
    rows, cols = o_ref.shape[1], o_ref.shape[2]
    clear_edges(pad)

    def fill(r, carry):
        put_row(pad, r, v_ref[0, r].astype(F32))
        return carry

    lax.fori_loop(0, rows + 2 * RIM, fill, 0)

    def one(r, carry):
        for g, (w, lanes, size) in enumerate(((w3, 0, 3), (w5, 0, 5), (w7, 0, 7), (w7, 128, 7))):
            o_ref[0, r, :, g * 128 : (g + 1) * 128] = tap_row(
                pad, w, lanes, g, r + RIM, cols, size, None, False
            )
        return carry

    lax.fori_loop(0, rows, one, 0)


def main_kernel(marks, lead, sc, sums_ref, q_ref, conv_ref, resid_ref, cot_ref, gain_ref, *refs):
    pieces = refs[: len(marks)]
    (
        out_ref,
        act_ref,
        gh_ref,
        n2_ref,
        att_ref,
        gffn_ref,
        gproj_ref,
        gconv_ref,
        gq_ref,
        gm_ref,
        gkv_ref,
        ggain_ref,
        w_out,
        w_up,
        w_down,
        kvn,
        gacc,
        sem,
    ) = refs[len(marks) :]
    micro, tile = pl.program_id(0), pl.program_id(1)
    tokens, width = q_ref.shape[1], q_ref.shape[2]
    cols = 64
    rows = tokens // cols
    head = width // HEADS
    half = 4 * head
    scale = head**-0.5
    hidden_width = w_up.shape[1]

    @pl.when((micro == 0) & (tile == 0))
    def _():
        fetch(
            sc,
            pieces,
            marks,
            lead,
            [
                (w_out, 0, width, 1),
                (w_up, width, hidden_width, 1),
                (w_down, width + hidden_width, width, 4),
            ],
            sem,
        )
        ggain_ref[...] = jnp.zeros_like(ggain_ref)

    @pl.when(tile == 0)
    def _():
        normal = sums_ref[0, :head] / sums_ref[0, head : head + 1] * scale
        for b in range(width // half):
            kvn[b] = block_diagonal(normal[:, b * half : (b + 1) * half], head).astype(BF)
        gacc[...] = jnp.zeros_like(gacc)

    ok = valid_rows(sc, micro, tile * rows, rows, cols)
    q = q_ref[0]
    qf = q.astype(F32)
    conv = conv_ref[0]
    factor = jnp.concatenate(
        [dot_nt(q[:, b * half : (b + 1) * half], kvn[b]) for b in range(width // half)], axis=1
    )
    att = (factor + qf * conv).astype(BF)
    att_ref[0] = att

    @pl.when((micro == 0) & (tile == 0))
    def _():
        pltpu.make_async_copy(w_out, w_out, sem).wait()
        pltpu.make_async_copy(w_up, w_up, sem).wait()
        pltpu.make_async_copy(w_down, w_down, sem).wait()

    middle = resid_ref[0] + dot(att, w_out[...])
    unit, inverse = unit_rows(middle)
    gain = gain_ref[...]
    n2 = (unit * gain).astype(BF)
    n2_ref[0] = n2
    g_top = cot_ref[0].astype(F32) * ok
    g_ffn = g_top.astype(BF)
    gffn_ref[0] = g_ffn
    ffn = jnp.zeros((tokens, width), F32)
    back = jnp.zeros((tokens, width), F32)
    step = 512
    for c in range(0, hidden_width, step):
        hidden = dot(n2, w_up[:, c : c + step])
        cdf = 0.5 * (1.0 + lax.erf(hidden * (1.0 / math.sqrt(2.0))))
        act = (hidden * cdf).astype(BF)
        slope = cdf + hidden * jnp.exp(-0.5 * hidden * hidden) * (1.0 / math.sqrt(2.0 * math.pi))
        act_ref[0, :, c : c + step] = act
        ffn = ffn + dot(act, w_down[c : c + step, :])
        g_hidden = (dot_nt(g_ffn, w_down[c : c + step, :]) * slope).astype(BF)
        gh_ref[0, :, c : c + step] = g_hidden
        back = back + dot_nt(g_hidden, w_up[:, c : c + step])
    out_ref[0] = ((middle + ffn) * ok).astype(BF)
    ggain_ref[...] += jnp.sum(back * unit, axis=0, keepdims=True)
    g_middle = g_top + norm_back(back, unit, inverse, gain)
    gm_ref[0] = g_middle
    g_proj = g_middle.astype(BF)
    gproj_ref[0] = g_proj
    g_att = dot_nt(g_proj, w_out[...])
    gconv_ref[0] = g_att * qf
    low = g_att.astype(BF)
    for b in range(width // half):
        lanes = slice(b * half, (b + 1) * half)
        gq_ref[0, :, lanes] = (
            g_att[:, lanes] * conv[:, lanes] + dot(low[:, lanes], kvn[b])
        ).astype(BF)
        gacc[b] += dot_tn(low[:, lanes], q[:, lanes])

    @pl.when(tile == pl.num_programs(1) - 1)
    def _():
        for b in range(width // half):
            gkv_ref[0, :, b * half : (b + 1) * half] = (
                diagonal_blocks(gacc[b], head) * scale
            ).astype(BF)


def place_blocks(sc, lead, order, value, keep_ref, send_ref, lane, parts):
    place = sc[0] >> lead
    lanes = value.shape[1]
    half = len(order) // 2
    for slot, mask in enumerate(order):
        block = place ^ (mask >> lead)
        target = keep_ref if slot < half else send_ref
        for part in range(parts):
            at = pl.multiple_of(block * (16 * parts) + 16 * part, 16)
            target[slot % half, :, lane + part * lanes : lane + (part + 1) * lanes] = value[
                pl.ds(at, 16), :
            ].astype(BF)


def up_kernel(order, lead, sc, n2_ref, gh_ref, act_ref, gffn_ref, att_ref, gproj_ref, keep_ref, send_ref, acc_up, acc_down):
    width = n2_ref.shape[1]
    hidden = gh_ref.shape[1]
    step = 512
    acc = acc_down.at[:width, :]
    acc[...] = dot_tn(att_ref[...], gproj_ref[...])
    place_blocks(sc, lead, order, acc, keep_ref, send_ref, 0, 1)
    for c in range(0, hidden, step):
        acc_up[:, c : c + step] = dot_tn(n2_ref[...], gh_ref[:, c : c + step])
    place_blocks(sc, lead, order, acc_up, keep_ref, send_ref, width, 1)
    for c in range(0, hidden, step):
        acc_down[c : c + step, :] = dot_tn(act_ref[:, c : c + step], gffn_ref[...])
    place_blocks(sc, lead, order, acc_down, keep_ref, send_ref, width + hidden, 4)


def taps_kernel(v_ref, g_ref, o3, o5, o7, pad):
    rows, cols = g_ref.shape[1], g_ref.shape[2]
    clear_edges(pad)

    @pl.when(pl.program_id(0) == 0)
    def _():
        o3[...] = jnp.zeros_like(o3)
        o5[...] = jnp.zeros_like(o5)
        o7[...] = jnp.zeros_like(o7)

    def fill(r, carry):
        put_row(pad, r, v_ref[0, r].astype(F32))
        return carry

    lax.fori_loop(0, rows + 2 * RIM, fill, 0)
    for g, (o, lanes, size) in enumerate(((o3, 0, 3), (o5, 0, 5), (o7, 0, 7), (o7, 128, 7))):
        tap_sums(pad, g_ref, o, lanes, g, rows, cols, size, RIM)


def back_kernel(
    marks, lead, sc, k_ref, v_ref, sums_ref, gkv_ref, gc_ref, top_ref, bot_ref, gq_ref, resid_ref,
    gm_ref, gain_ref, w3, w5, w7, *refs
):
    pieces = refs[: len(marks)]
    gqkv_ref, gu_ref, ggain_ref, whole, pad, gv_buf, sem = refs[len(marks) :]
    micro = pl.program_id(0)
    rows, cols = gc_ref.shape[1], gc_ref.shape[2]
    tokens, width = k_ref.shape[1], k_ref.shape[2]
    head = width // HEADS
    half = 4 * head

    @pl.when(micro == 0)
    def _():
        fetch(sc, pieces, marks, lead, [(whole, 0, 3 * width, 1)], sem)
        ggain_ref[...] = jnp.zeros_like(ggain_ref)

    clear_edges(pad)

    def fill(r, carry):
        put_row(pad, RIM + r, gc_ref[0, r])
        return carry

    lax.fori_loop(0, rows, fill, 0)
    for r in range(RIM):
        put_row(pad, r, top_ref[0, r].astype(F32))
        put_row(pad, RIM + rows + r, bot_ref[0, r].astype(F32))

    def one(r, carry):
        for g, (w, lanes, size) in enumerate(((w3, 0, 3), (w5, 0, 5), (w7, 0, 7), (w7, 128, 7))):
            gv_buf[r, :, g * 128 : (g + 1) * 128] = tap_row(
                pad, w, lanes, g, r + RIM, cols, size, None, True
            )
        return carry

    lax.fori_loop(0, rows, one, 0)

    ok = valid_rows(sc, micro, 0, rows, cols)
    total = sums_ref[0, head : head + 1]
    top = sums_ref[0, head + 1 : head + 2]
    normal = sums_ref[0, :head] / total
    gkv = gkv_ref[0]
    inner = jnp.sum(normal * gkv, axis=0, keepdims=True)
    probs = jnp.where(ok > 0, jnp.exp(k_ref[0].astype(F32) - top) / total, 0.0)
    low = probs.astype(BF)
    v = v_ref[0, RIM : RIM + rows].reshape(tokens, width)
    gqkv_ref[0, :, :width] = gq_ref[0]
    for b in range(width // half):
        lanes = slice(b * half, (b + 1) * half)
        diag = block_diagonal(gkv[:, lanes], head).astype(BF)
        gk = probs[:, lanes] * (dot(v[:, lanes], diag) - inner[:, lanes])
        gqkv_ref[0, :, width + b * half : width + (b + 1) * half] = gk.astype(BF)
        gv = dot_nt(low[:, lanes], diag) + gv_buf[:, :, lanes].reshape(tokens, half)
        gqkv_ref[0, :, 2 * width + b * half : 2 * width + (b + 1) * half] = gv.astype(BF)

    @pl.when(micro == 0)
    def _():
        pltpu.make_async_copy(whole, whole, sem).wait()

    dy = dot_nt(gqkv_ref[0], whole[...])
    unit, inverse = unit_rows(resid_ref[0])
    ggain_ref[...] += jnp.sum(dy * unit, axis=0, keepdims=True)
    gu = (gm_ref[0] + norm_back(dy, unit, inverse, gain_ref[...])) * ok
    gu_ref[0] = gu.reshape(rows, cols, width)


def qkv_grad_kernel(order, lead, sc, n_ref, g_ref, keep_ref, send_ref, acc):
    micros, rows, cols, width = n_ref.shape
    rows = rows - 2 * RIM
    n = n_ref[:, RIM : RIM + rows].reshape(micros * rows * cols, width)
    step = 512
    for c in range(0, g_ref.shape[1], step):
        acc[:, c : c + step] = dot_tn(n, g_ref[:, c : c + step])
    place_blocks(sc, lead, order, acc, keep_ref, send_ref, 0, 1)


def pos_grad_kernel(sc, x_ref, top_ref, bot_ref, gu_ref, o_ref, pad):
    micro = pl.program_id(0)
    rows, cols = x_ref.shape[2], x_ref.shape[3]
    halo = top_ref.shape[1]
    clear_edges(pad)

    @pl.when(micro == 0)
    def _():
        o_ref[...] = jnp.zeros_like(o_ref)

    def put(r, cells):
        put_row(pad, r + 1, cells.astype(F32) * valid_rows(sc, micro, r, 1, cols))

    def fill(r, carry):
        put(r, x_ref[0, 0, r])
        return carry

    lax.fori_loop(0, rows, fill, 0)
    put(-1, top_ref[0, halo - 1])
    put(rows, bot_ref[0, 0])
    for g in range(pad.shape[0]):
        tap_sums(pad, gu_ref, o_ref, g * 128, g, rows, cols, 3, 1)


def start_grad_kernel(sc, gu_ref, top_ref, bot_ref, w_ref, o_ref, pad):
    micro = pl.program_id(0)
    rows, cols = gu_ref.shape[1], gu_ref.shape[2]
    clear_edges(pad)

    def fill(r, carry):
        put_row(pad, 1 + r, gu_ref[0, r])
        return carry

    lax.fori_loop(0, rows, fill, 0)
    put_row(pad, 0, top_ref[0, 0].astype(F32))
    put_row(pad, rows + 1, bot_ref[0, 0].astype(F32))

    def one(r, carry):
        ok = valid_rows(sc, micro, r, 1, cols)
        for g in range(pad.shape[0]):
            taps = tap_row(pad, w_ref, g * 128, g, r + 1, cols, 3, None, True)
            o_ref[0, 0, r, :, g * 128 : (g + 1) * 128] = (
                taps + pad[g, r + 1, EDGE : EDGE + cols, :]
            ) * ok
        return carry

    lax.fori_loop(0, rows, one, 0)


SMEM = pl.BlockSpec(memory_space=pltpu.SMEM)
ANY = pl.BlockSpec(memory_space=pl.ANY)


def by_micro(shape):
    rest = tuple(shape[1:])
    return pl.BlockSpec((1,) + rest, lambda m: (m,) + (0,) * len(rest))


def whole_spec(shape):
    return pl.BlockSpec(tuple(shape), lambda *_: (0,) * len(shape))


def shaped(shape, dtype):
    return jax.ShapeDtypeStruct(tuple(shape), dtype)


def call(kernel, grid, ins, outs, scratch, flops, limit=48):
    nbytes = sum(a.size * a.dtype.itemsize for _, a in ins)
    nbytes += sum(math.prod(s) * jnp.dtype(d).itemsize for _, s, d in outs)
    return pl.pallas_call(
        kernel,
        grid=grid,
        in_specs=[s for s, _ in ins],
        out_specs=[s for s, _, _ in outs],
        out_shape=[shaped(s, d) for _, s, d in outs],
        scratch_shapes=scratch,
        cost_estimate=pl.CostEstimate(
            flops=int(flops), bytes_accessed=int(nbytes), transcendentals=0
        ),
        compiler_params=pltpu.CompilerParams(
            vmem_limit_bytes=limit * MIB, dimension_semantics=("arbitrary",) * len(grid)
        ),
    )(*[a for _, a in ins])


def local(
    images,
    cotangent,
    extent,
    w_qkv,
    w_out,
    w_up,
    w_down,
    pos_weight,
    win_three,
    win_five,
    win_seven,
    gain_one,
    gain_two,
):
    micros, _, rows, cols, width = images.shape
    head = width // HEADS
    hidden = w_up.shape[1]
    tokens = rows * cols
    halo = RIM + 1
    me = positions()
    lead_masks, first, second, third = plan(w_up.shape[0])
    lead = len(lead_masks)
    stages = (first, second, third)
    scalars = jnp.concatenate(
        [
            jnp.stack([me, lax.axis_index("strip") * rows, me, me]).astype(jnp.int32),
            extent[:, 0].reshape(-1).astype(jnp.int32),
        ]
    )
    sc = (SMEM, scalars)
    taps3 = pos_weight.reshape(9, width)
    n5 = 128
    w3 = win_three.reshape(9, 128)
    w5 = win_five[:, :, :n5].reshape(25, n5)
    w7 = jnp.concatenate(
        [jnp.pad(win_five[:, :, n5:], ((1, 1), (1, 1), (0, 0))), win_seven], axis=-1
    ).reshape(49, 256)
    gain1, gain2 = gain_one.reshape(1, width), gain_two.reshape(1, width)
    windows = [(whole_spec(w.shape), w) for w in (w3, w5, w7)]
    pad_rim = pltpu.VMEM((width // 128, rows + 2 * RIM, cols + 2 * EDGE, 128), F32)
    pad_one = pltpu.VMEM((width // 128, rows + 2, cols + 2 * EDGE, 128), F32)

    x_top, x_bot = rims(images[:, 0], halo)
    qkv_pieces, marks = gather_pieces(join_lead(w_qkv, lead_masks), stages)
    joined = [join_lead(w, lead_masks) for w in (w_out, w_up, w_down)]
    down = joined[2].reshape(4, 16, width)
    block = jnp.concatenate([joined[0], joined[1], down[0], down[1], down[2], down[3]], axis=1)
    rest_pieces, _ = gather_pieces(block, stages)

    x_in = (pl.BlockSpec((1, 1, rows, cols, width), lambda m: (m, 0, 0, 0, 0)), images)
    normed, resid = call(
        norm_kernel,
        (micros,),
        [
            sc,
            x_in,
            (by_micro(x_top.shape), x_top),
            (by_micro(x_bot.shape), x_bot),
            (whole_spec(taps3.shape), taps3),
            (whole_spec(gain1.shape), gain1),
        ],
        [
            (by_micro((micros, rows + 2 * RIM, cols, width)), (micros, rows + 2 * RIM, cols, width), BF),
            (by_micro((micros, rows, cols, width)), (micros, rows, cols, width), F32),
        ],
        [pltpu.VMEM((width // 128, rows + 2 * halo, cols + 2 * EDGE, 128), F32)],
        5e6,
    )
    flat = (micros, tokens, width)
    rimmed = (micros, rows + 2 * RIM, cols, width)
    sums_shape = (micros, head + 16, width)
    q, k, v, sums = call(
        functools.partial(qkv_kernel, marks, lead),
        (micros,),
        [sc, (by_micro(rimmed), normed)] + [(ANY, p) for p in qkv_pieces],
        [
            (by_micro(flat), flat, BF),
            (by_micro(flat), flat, BF),
            (by_micro(rimmed), rimmed, BF),
            (by_micro(sums_shape), sums_shape, BF),
        ],
        [pltpu.VMEM((width, 3 * width), BF), pltpu.SemaphoreType.DMA],
        2e9,
    )
    (conv,) = call(
        window_kernel,
        (micros,),
        [(by_micro(rimmed), v)] + windows,
        [(by_micro((micros, rows, cols, width)), (micros, rows, cols, width), F32)],
        [pad_rim],
        3e7,
    )
    for mask in strip_masks():
        low = sums.astype(BF)
        got = strip_swap(low, mask).astype(F32)
        low = low.astype(F32)
        top = jnp.maximum(low[:, head + 1 : head + 2], got[:, head + 1 : head + 2])
        body = low[:, : head + 1] * jnp.exp(low[:, head + 1 : head + 2] - top) + got[
            :, : head + 1
        ] * jnp.exp(got[:, head + 1 : head + 2] - top)
        sums = jnp.concatenate([body, top, jnp.zeros((micros, 14, width), F32)], axis=1)

    tile_rows = 4
    tile = tile_rows * cols
    tiles = rows // tile_rows

    def tiled(lanes):
        return pl.BlockSpec((1, tile, lanes), lambda m, t: (m, t, 0))

    def per_micro(shape):
        return pl.BlockSpec((1,) + tuple(shape[1:]), lambda m, t: (m,) + (0,) * (len(shape) - 1))

    wide = (micros, tokens, hidden)
    gkv_shape = (micros, head, width)
    outs = call(
        functools.partial(main_kernel, marks, lead),
        (micros, tiles),
        [
            sc,
            (per_micro(sums_shape), sums),
            (tiled(width), q),
            (tiled(width), conv.reshape(flat)),
            (tiled(width), resid.reshape(flat)),
            (tiled(width), cotangent.reshape(flat)),
            (whole_spec(gain2.shape), gain2),
        ]
        + [(ANY, p) for p in rest_pieces],
        [
            (tiled(width), flat, BF),
            (tiled(hidden), wide, BF),
            (tiled(hidden), wide, BF),
            (tiled(width), flat, BF),
            (tiled(width), flat, BF),
            (tiled(width), flat, BF),
            (tiled(width), flat, BF),
            (tiled(width), flat, F32),
            (tiled(width), flat, BF),
            (tiled(width), flat, F32),
            (per_micro(gkv_shape), gkv_shape, BF),
            (whole_spec((1, width)), (1, width), F32),
        ],
        [
            pltpu.VMEM((width, width), BF),
            pltpu.VMEM((width, hidden), BF),
            pltpu.VMEM((hidden, width), BF),
            pltpu.VMEM((width // (4 * head), 4 * head, 4 * head), BF),
            pltpu.VMEM((width // (4 * head), 4 * head, 4 * head), F32),
            pltpu.SemaphoreType.DMA,
        ],
        1.2e10,
    )
    out, act, g_hidden, n2, att, g_ffn, g_proj, g_conv, gq, g_middle, gkv, ggain2 = outs
    gkv = strip_sum(gkv)
    map_shape = (micros, rows, cols, width)
    g_conv = g_conv.reshape(map_shape)
    gc_top, gc_bot = rims(g_conv.astype(BF), RIM)

    marked = [0]
    for stage in (first, second, third):
        marked = [o ^ m for m in spans(stage) for o in marked]
    slots = len(marked) // 2
    lanes = width + 2 * hidden

    def flat2(a):
        return a.reshape(-1, a.shape[-1])

    def rows_sum(keep, send):
        total = keep.astype(F32) + flipped(send, third[0]).astype(F32)
        for stage in (second, first):
            masks = spans(stage)
            size = total.shape[0] // len(masks)
            got = total[:size]
            for n, mask in enumerate(masks[1:], 1):
                got = got + flipped(total[n * size : (n + 1) * size].astype(BF), mask).astype(F32)
            total = got
        return total[0]

    half_shape = (slots, 16, lanes)
    ops = [flat2(a) for a in (n2, g_hidden, act, g_ffn, att, g_proj)]
    keep, send = call(
        functools.partial(up_kernel, marked, lead),
        (1,),
        [sc] + [(whole_spec(a.shape), a) for a in ops],
        [(whole_spec(half_shape), half_shape, BF)] * 2,
        [pltpu.VMEM((width, hidden), F32), pltpu.VMEM((hidden, width), F32)],
        5e9,
        56,
    )
    o3, o5, o7 = call(
        taps_kernel,
        (micros,),
        [(by_micro(rimmed), v), (by_micro(map_shape), g_conv)],
        [
            (whole_spec((9, 128)), (9, 128), F32),
            (whole_spec((25, 128)), (25, 128), F32),
            (whole_spec((49, 256)), (49, 256), F32),
        ],
        [pad_rim],
        3e7,
    )
    rest = rows_sum(keep, send)

    g_qkv, g_u, ggain1 = call(
        functools.partial(back_kernel, marks, lead),
        (micros,),
        [
            sc,
            (by_micro(flat), k),
            (by_micro(rimmed), v),
            (by_micro(sums_shape), sums),
            (by_micro(gkv_shape), gkv),
            (by_micro(map_shape), g_conv),
            (by_micro(gc_top.shape), gc_top),
            (by_micro(gc_bot.shape), gc_bot),
            (by_micro(flat), gq),
            (by_micro(flat), resid.reshape(flat)),
            (by_micro(flat), g_middle),
            (whole_spec(gain1.shape), gain1),
        ]
        + windows
        + [(ANY, p) for p in qkv_pieces],
        [
            (by_micro((micros, tokens, 3 * width)), (micros, tokens, 3 * width), BF),
            (by_micro(map_shape), map_shape, F32),
            (whole_spec((1, width)), (1, width), F32),
        ],
        [
            pltpu.VMEM((width, 3 * width), BF),
            pad_rim,
            pltpu.VMEM((rows, cols, width), F32),
            pltpu.SemaphoreType.DMA,
        ],
        2.5e9,
        56,
    )
    gu_top, gu_bot = rims(g_u.astype(BF), 1)
    half_shape = (slots, 16, 3 * width)
    g2 = flat2(g_qkv)
    keep, send = call(
        functools.partial(qkv_grad_kernel, marked, lead),
        (1,),
        [sc, (whole_spec(normed.shape), normed), (whole_spec(g2.shape), g2)],
        [(whole_spec(half_shape), half_shape, BF)] * 2,
        [pltpu.VMEM((width, 3 * width), F32)],
        1.6e9,
    )
    (o_pos,) = call(
        pos_grad_kernel,
        (micros,),
        [
            sc,
            x_in,
            (by_micro(x_top.shape), x_top),
            (by_micro(x_bot.shape), x_bot),
            (by_micro(map_shape), g_u),
        ],
        [(whole_spec((9, width)), (9, width), F32)],
        [pad_one],
        1e7,
    )
    qkv_sum = rows_sum(keep, send)
    (grad_in,) = call(
        start_grad_kernel,
        (micros,),
        [
            sc,
            (by_micro(map_shape), g_u),
            (by_micro(gu_top.shape), gu_top),
            (by_micro(gu_bot.shape), gu_bot),
            (whole_spec(taps3.shape), taps3),
        ],
        [
            (
                pl.BlockSpec((1, 1, rows, cols, width), lambda m: (m, 0, 0, 0, 0)),
                (micros, 1, rows, cols, width),
                F32,
            )
        ],
        [pad_one],
        1e7,
    )

    own_rows = w_up.shape[0]

    def lead_sum(total, rows_own):
        for mask in reversed(lead_masks):
            size = total.shape[0] // 2
            low, high = total[:size], total[size:]
            bit = (me & mask) != 0
            kept, sent = jnp.where(bit, high, low), jnp.where(bit, low, high)
            total = kept + flipped(sent, mask)
        return total

    grad_out = lead_sum(rest[:, :width], own_rows)
    grad_up = lead_sum(rest[:, width : width + hidden], own_rows)
    down = rest[:, width + hidden :].reshape(16, 4, width).transpose(1, 0, 2).reshape(64, width)
    grad_down = lead_sum(down, w_down.shape[0])
    grad_qkv = lead_sum(qkv_sum, own_rows)

    early = jnp.concatenate([o.reshape(-1) for o in (o3, o5, o7, ggain2)]).reshape(-1, 128)
    late = jnp.concatenate([o_pos.reshape(-1), ggain1.reshape(-1)]).reshape(-1, 128)
    order = ([1 << b for b in range(max(lead, 0))],) if lead else ()
    small_stages = (third, second, first) + order
    early = all_sum(early, small_stages).reshape(-1)
    late = all_sum(late, small_stages).reshape(-1)
    sizes = [9 * 128, 25 * 128, 49 * 256, width]
    at = [0]
    for s in sizes:
        at.append(at[-1] + s)
    o3, o5, o7, ggain2 = (early[a:b] for a, b in zip(at, at[1:]))
    o5 = o5.reshape(5, 5, 128)
    o7 = o7.reshape(7, 7, 256)
    return (
        out.reshape(micros, 1, rows, cols, width),
        grad_in,
        grad_qkv,
        grad_out,
        grad_up,
        grad_down,
        late[: 9 * width].reshape(3, 3, width),
        o3.reshape(3, 3, 128),
        jnp.concatenate([o5, o7[1:6, 1:6, :64]], axis=-1),
        o7[:, :, 64:],
        late[9 * width :],
        ggain2,
    )


def solution(mesh):
    in_specs = (
        P(None, "img", "strip", None, None),
        P(None, "img", "strip", None, None),
        P(None, "img", None),
        P(("img", "strip"), None),
        P(("img", "strip"), None),
        P(("img", "strip"), None),
        P(("img", "strip"), None),
        P(),
        P(),
        P(),
        P(),
        P(),
        P(),
    )
    out_specs = (
        P(None, "img", "strip", None, None),
        P(None, "img", "strip", None, None),
        P(("img", "strip"), None),
        P(("img", "strip"), None),
        P(("img", "strip"), None),
        P(("img", "strip"), None),
        P(),
        P(),
        P(),
        P(),
        P(),
        P(),
    )
    return jax.shard_map(local, mesh=mesh, in_specs=in_specs, out_specs=out_specs, check_vma=False)
```

```python
import functools
import math

import jax
import jax.numpy as jnp
from jax import lax
from jax.experimental import pallas as pl
from jax.experimental.pallas import tpu as pltpu
from jax.sharding import PartitionSpec as P

HEADS = 8
norm_eps = 1e-06
masked_low = -1e30
RIM = 3
EDGE = 8
BF = jnp.bfloat16
F32 = jnp.float32
MIB = 2**20
VMEM_MIB = 58


def positions():
    return lax.axis_index("img") * lax.axis_size("strip") + lax.axis_index("strip")


def flipped(cells, mask):
    count = lax.axis_size("img") * lax.axis_size("strip")
    return lax.ppermute(cells, ("img", "strip"), [(i, i ^ mask) for i in range(count)])


def plan(shard_rows):
    strip_bits = int(math.log2(lax.axis_size("strip")))
    img_bits = int(math.log2(lax.axis_size("img")))
    lead = 0
    while (shard_rows << lead) < 16:
        lead += 1
    free = [1 << b for b in range(lead, strip_bits)]
    img = [1 << (strip_bits + b) for b in range(1, img_bits)]
    if len(free) > 2:
        first, second = [free[0], free[2]], [free[1]] + img
    else:
        first, second = free, img
    return [1 << b for b in range(lead)], first, second, [1 << strip_bits]


def spans(masks):
    out = [0]
    for mask in masks:
        out = out + [o ^ mask for o in out]
    return out


def join_lead(shard, lead):
    me = positions()
    for mask in lead:
        other = flipped(shard, mask)
        shard = jnp.where(
            (me & mask) != 0, jnp.concatenate([other, shard]), jnp.concatenate([shard, other])
        )
    return shard


def strip_swap(cells, mask):
    count = lax.axis_size("strip")
    return lax.ppermute(cells, "strip", [(i, i ^ mask) for i in range(count)])


def strip_stages():
    masks = [1 << b for b in range(int(math.log2(lax.axis_size("strip"))))]
    return [masks[:2], masks[2:]]


def rims(first, last):
    count = lax.axis_size("strip")
    above = lax.ppermute(last, "strip", [(i, i + 1) for i in range(count - 1)])
    below = lax.ppermute(first, "strip", [(i + 1, i) for i in range(count - 1)])
    return above, below


class Here:
    def __init__(self, extent_ref, strip_rows):
        self.extent = extent_ref
        self.strip_rows = strip_rows

    def place(self):
        return positions()

    def first_row(self):
        return lax.axis_index("strip") * self.strip_rows

    def valid(self, micro, which):
        return self.extent[micro, 0, which]


def dot(a, b):
    return jnp.dot(a, b, preferred_element_type=F32)


def dot_nt(a, b):
    return lax.dot_general(a, b, (((1,), (1,)), ((), ())), preferred_element_type=F32)


def dot_tn(a, b):
    return lax.dot_general(a, b, (((0,), (0,)), ((), ())), preferred_element_type=F32)


def valid_rows(sc, micro, first_row, rows, cols):
    n = rows * cols
    shift = int(math.log2(cols))
    flat = lax.broadcasted_iota(jnp.int32, (n, 1), 0)
    row = lax.shift_right_logical(flat, shift) + (sc.first_row() + first_row)
    ok = (row < sc.valid(micro, 0)) & ((flat & (cols - 1)) < sc.valid(micro, 1))
    return jnp.where(ok, 1.0, 0.0).astype(F32)


def valid_cols(sc, micro, cols):
    col = lax.broadcasted_iota(jnp.int32, (cols, 128), 0)
    return jnp.where(col < sc.valid(micro, 1), 1.0, 0.0).astype(F32)


def valid_row(sc, micro, row):
    at = sc.first_row() + row
    return jnp.where((at >= 0) & (at < sc.valid(micro, 0)), 1.0, 0.0).astype(F32)


def unit_rows(fields):
    average = jnp.mean(fields, axis=-1, keepdims=True)
    centred = fields - average
    inverse = lax.rsqrt(jnp.mean(centred * centred, axis=-1, keepdims=True) + norm_eps)
    return centred * inverse, inverse


def norm_back(dy, unit, inverse, gain):
    dyg = dy * gain
    first = jnp.mean(dyg, axis=-1, keepdims=True)
    second = jnp.mean(dyg * unit, axis=-1, keepdims=True)
    return inverse * (dyg - first - unit * second)


def clear_edges(pad):
    groups, rows, cols, _ = pad.shape
    zeros = jnp.zeros((rows, EDGE, 128), F32)
    for g in range(groups):
        pad[g, :, :EDGE, :] = zeros
        pad[g, :, cols - EDGE :, :] = zeros


def put_row(pad, row, cells, ok=None):
    for g in range(pad.shape[0]):
        part = cells[:, g * 128 : (g + 1) * 128]
        pad[g, row, EDGE : EDGE + cells.shape[0], :] = part if ok is None else part * ok


def rim_lanes(width):
    out, lane = [], 0
    for row in range(RIM):
        out.append((row, lane))
        lane += width - 128 * row
    return out, lane


def pack_rim(rim_ref, lines):
    spans_, _ = rim_lanes(lines[0].shape[1])
    for line, (group, lane) in zip(lines, spans_):
        part = line[:, 128 * group :]
        rim_ref[0, :, lane : lane + part.shape[1]] = part.astype(BF)


def put_rims(pad, top_ref, bot_ref, rows):
    width = 128 * pad.shape[0]
    cols = top_ref.shape[1]
    for near, (group, lane) in enumerate(rim_lanes(width)[0]):
        for ref, line in ((top_ref, RIM - 1 - near), (bot_ref, RIM + rows + near)):
            for g in range(group, pad.shape[0]):
                at = lane + 128 * (g - group)
                pad[g, line, EDGE : EDGE + cols, :] = ref[0, :, at : at + 128].astype(F32)


def tap_row(pad, w_ref, lanes, group, row, cols, size, lines, flip):
    reach = size // 2
    total = jnp.zeros((cols, 128), F32)
    for i in lines or range(size):
        for j in range(size):
            at = i * size + j
            if flip:
                at = size * size - 1 - at
            w = w_ref[at : at + 1, lanes : lanes + 128]
            total = total + w * pad[
                group, row + i - reach, EDGE + j - reach : EDGE + j - reach + cols, :
            ]
    return total


def tap_sums(pad, grad_ref, out_ref, sums, lanes, group, size, above):
    reach = size // 2
    rows, cols = grad_ref.shape[1], grad_ref.shape[2]
    taps = size * size
    sums[:taps] = jnp.zeros((taps, 8, 128), F32)

    def step(t, carry):
        c = pl.multiple_of(t * 8, 8)
        grads = [
            grad_ref[0, r, pl.ds(c, 8), group * 128 : (group + 1) * 128].astype(F32)
            for r in range(rows)
        ]
        for j in range(size):
            got = [None] * size
            for line in range(rows + 2 * reach):
                f = pad[group, line + above - reach, pl.ds(c + EDGE + j - reach, 8), :]
                for i in range(size):
                    r = line - i
                    if 0 <= r < rows:
                        term = grads[r] * f
                        got[i] = term if got[i] is None else got[i] + term
            for i in range(size):
                sums[i * size + j] += got[i]
        return carry

    lax.fori_loop(0, cols // 8, step, 0)
    for at in range(taps):
        out_ref[at : at + 1, lanes : lanes + 128] += jnp.sum(sums[at], axis=0, keepdims=True)


def block_diagonal(wide, head):
    lane = lax.broadcasted_iota(jnp.int32, wide.shape, 1) // head
    return jnp.concatenate(
        [jnp.where(lane == h, wide, 0.0) for h in range(wide.shape[1] // head)], axis=0
    )


def diagonal_blocks(full, head):
    lane = lax.broadcasted_iota(jnp.int32, (head, full.shape[1]), 1) // head
    total = jnp.zeros((head, full.shape[1]), F32)
    for h in range(full.shape[1] // head):
        total = total + jnp.where(lane == h, full[h * head : (h + 1) * head], 0.0)
    return total


def fetch(sc, pieces, marks, lead, targets, sem):
    place = sc.place() >> lead
    for piece, mark in zip(pieces, marks):
        for k, mask in enumerate(mark):
            block = place ^ (mask >> lead)
            for whole, lane, lanes, parts in targets:
                for part in range(parts):
                    at = pl.multiple_of(block * (16 * parts) + 16 * part, 16)
                    pltpu.make_async_copy(
                        piece.at[k, :, pl.ds(lane + part * lanes, lanes)],
                        whole.at[pl.ds(at, 16), :],
                        sem,
                    ).start()


def taps_prep(pos_ref, three_ref, five_ref, seven_ref, taps3, w3, w5, w7):
    for i in range(3):
        for j in range(3):
            taps3[3 * i + j : 3 * i + j + 1, :] = pos_ref[i, j : j + 1, :]
            w3[3 * i + j : 3 * i + j + 1, :] = three_ref[i, j : j + 1, :]
    for i in range(5):
        for j in range(5):
            w5[5 * i + j : 5 * i + j + 1, :] = five_ref[i, j : j + 1, :128]
    for i in range(7):
        for j in range(7):
            seven = seven_ref[i, j : j + 1, :]
            low = jnp.zeros((1, 64), F32)
            if 1 <= i <= 5 and 1 <= j <= 5:
                low = five_ref[i - 1, j - 1 : j, 128:192]
            w7[7 * i + j : 7 * i + j + 1, :] = jnp.concatenate([low, seven], axis=1)


def prep_kernel(pos_ref, three_ref, five_ref, seven_ref, out_ref, up_ref, down_ref, *refs):
    taps_prep(pos_ref, three_ref, five_ref, seven_ref, *refs[:4])
    o_ref = refs[4]
    width = out_ref.shape[1]
    o_ref[:, :width] = out_ref[...]
    lane = width + up_ref.shape[1]
    o_ref[:, width:lane] = up_ref[...]
    for part in range(4):
        o_ref[:, lane + part * width : lane + (part + 1) * width] = down_ref[
            16 * part : 16 * part + 16, :
        ]


def stack_kernel(*refs):
    for n, ref in enumerate(refs[:-1]):
        refs[-1][n] = ref[...]


def first_kernel(count, *refs):
    x_first, x_last, o_ref, first_ref, last_ref = refs[count:]
    for n in range(count):
        o_ref[n] = refs[n][...]
    first_ref[...] = x_first[:, 0]
    last_ref[...] = x_last[:, 0]


def join_kernel(head, *refs):
    o_ref = refs[-1]
    parts = [ref[...].astype(F32) for ref in refs[:-1]]
    tops = [p[:, head + 1 : head + 2] for p in parts]
    top = functools.reduce(jnp.maximum, tops)
    total = functools.reduce(
        jnp.add, [p[:, : head + 1] * jnp.exp(t - top) for p, t in zip(parts, tops)]
    )
    o_ref[:, :head] = total[:, :head].astype(o_ref.dtype)
    line = lax.broadcasted_iota(jnp.int32, parts[0][:, head:].shape, 1)
    o_ref[:, head:] = jnp.where(
        line == 0, total[:, head:], jnp.where(line == 1, top, 0.0)
    ).astype(o_ref.dtype)


def sum_kernel(*refs):
    total = refs[0][...].astype(F32)
    for ref in refs[1:-1]:
        total = total + ref[...].astype(F32)
    refs[-1][...] = total.astype(refs[-1].dtype)


def norm_kernel(sc, x_ref, top_ref, bot_ref, w_ref, gain_ref, normed_ref, resid_ref, pad):
    micro = pl.program_id(0)
    rows, cols = x_ref.shape[2], x_ref.shape[3]
    clear_edges(pad)
    cols_ok = valid_cols(sc, micro, cols)
    put_row(pad, 0, top_ref[0, 0].astype(F32), cols_ok * valid_row(sc, micro, -1))
    put_row(pad, rows + 1, bot_ref[0, 0].astype(F32), cols_ok * valid_row(sc, micro, rows))

    def fill(r, carry):
        put_row(pad, r + 1, x_ref[0, 0, r].astype(F32), cols_ok * valid_row(sc, micro, r))
        return carry

    lax.fori_loop(0, rows, fill, 0)
    gain = gain_ref[...]

    def one(r, carry):
        ok = cols_ok * valid_row(sc, micro, r)
        parts = []
        for g in range(pad.shape[0]):
            taps = tap_row(pad, w_ref, g * 128, g, r + 1, cols, 3, None, False)
            parts.append((taps + pad[g, r + 1, EDGE : EDGE + cols, :]) * ok)
        resid = jnp.concatenate(parts, axis=1)
        unit, _ = unit_rows(resid)
        normed_ref[0, r] = (unit * gain).astype(BF)
        resid_ref[0, r] = resid
        return carry

    lax.fori_loop(0, rows, one, 0)


def qkv_kernel(marks, lead, sc, n_ref, *refs):
    pieces = refs[: len(marks)]
    q_ref, k_ref, v_ref, sums_ref, first_ref, last_ref, whole, sem = refs[len(marks) :]
    micro = pl.program_id(0)
    rows, cols, width = n_ref.shape[1:]
    head = width // HEADS
    tokens = rows * cols

    @pl.when(micro == 0)
    def _():
        fetch(sc, pieces, marks, lead, [(whole, 0, 3 * width, 1)], sem)
        pltpu.make_async_copy(whole, whole, sem).wait()

    normed = n_ref[0].reshape(tokens, width)
    q_ref[0] = dot(normed, whole[:, :width]).astype(BF)
    k = dot(normed, whole[:, width : 2 * width]).astype(BF)
    k_ref[0] = k
    v = dot(normed, whole[:, 2 * width :]).astype(BF)
    v_ref[0] = v.reshape(rows, cols, width)
    pack_rim(first_ref, [v[r * cols : (r + 1) * cols] for r in range(RIM)])
    pack_rim(last_ref, [v[(rows - 1 - r) * cols : (rows - r) * cols] for r in range(RIM)])
    ok = valid_rows(sc, micro, 0, rows, cols)
    keys = jnp.where(ok > 0, k.astype(F32), masked_low)
    top = jnp.max(keys, axis=0, keepdims=True)
    ew = jnp.exp(keys - top) * ok
    total = jnp.sum(ew, axis=0, keepdims=True)
    low = ew.astype(BF)
    half = 4 * head
    for b in range(width // half):
        full = dot_tn(v[:, b * half : (b + 1) * half], low[:, b * half : (b + 1) * half])
        sums_ref[0, :head, b * half : (b + 1) * half] = diagonal_blocks(full, head).astype(BF)
    line = lax.broadcasted_iota(jnp.int32, (16, width), 0)
    sums_ref[0, head:, :] = jnp.where(line == 0, total, jnp.where(line == 1, top, 0.0)).astype(BF)


def fill_rimmed(pad, source, rows, top_ref, bot_ref):
    clear_edges(pad)

    def fill(r, carry):
        put_row(pad, RIM + r, source(r).astype(F32))
        return carry

    lax.fori_loop(0, rows, fill, 0)
    put_rims(pad, top_ref, bot_ref, rows)


WINDOWS = ((0, 0, 3), (1, 0, 5), (2, 0, 7), (2, 128, 7))


def window_kernel(v_ref, *refs):
    weights, (o_ref, pad) = refs[:3], refs[3:]
    rows, cols = o_ref.shape[1], o_ref.shape[2]
    clear_edges(pad)

    def fill(r, carry):
        put_row(pad, r, v_ref[0, r].astype(F32))
        return carry

    lax.fori_loop(0, rows, fill, 0)
    for r in range(rows):
        for g, (which, lanes, size) in enumerate(WINDOWS):
            reach = size // 2
            lines = range(max(0, reach - r), min(size, rows + reach - r))
            o_ref[0, r, :, g * 128 : (g + 1) * 128] = tap_row(
                pad, weights[which], lanes, g, r, cols, size, lines, False
            )


def window_rim_kernel(part_ref, top_ref, bot_ref, *refs):
    weights, (o_ref, pad) = refs[:3], refs[3:]
    rows, cols = 2 * RIM, part_ref.shape[2]
    clear_edges(pad)
    put_rims(pad, top_ref, bot_ref, 0)
    last = part_ref.shape[1]
    for r in range(RIM):
        for row, centre in ((r, RIM + r), (last - 1 - r, RIM - 1 - r)):
            for g, (which, lanes, size) in enumerate(WINDOWS):
                reach = size // 2
                if row < RIM:
                    lines = range(0, reach - r)
                else:
                    lines = range(reach + 1 + r, size)
                part = part_ref[0, row, :, g * 128 : (g + 1) * 128]
                if lines:
                    part = part + tap_row(
                        pad, weights[which], lanes, g, centre, cols, size, lines, False
                    )
                o_ref[0, row, :, g * 128 : (g + 1) * 128] = part
    for row in range(RIM, last - RIM):
        o_ref[0, row] = part_ref[0, row]


def main_kernel(
    marks, lead, sc, sums_ref, q_ref, conv_ref, resid_ref, cot_ref, gain_ref, *refs
):
    pieces = refs[: len(marks)]
    (
        out_ref,
        act_ref,
        gh_ref,
        n2_ref,
        att_ref,
        gffn_ref,
        gproj_ref,
        gconv_ref,
        gq_ref,
        gm_ref,
        gkv_ref,
        first_ref,
        last_ref,
        ggain_ref,
        w_out,
        w_up,
        w_down,
        kvn,
        gacc,
        sem,
        down_sem,
    ) = refs[len(marks) :]
    micro, tile = pl.program_id(0), pl.program_id(1)
    tokens, width = q_ref.shape[1], q_ref.shape[2]
    cols = 64
    rows = tokens // cols
    head = width // HEADS
    half = 4 * head
    scale = head**-0.5
    hidden_width = w_up.shape[1]

    @pl.when((micro == 0) & (tile == 0))
    def _():
        fetch(
            sc,
            pieces,
            marks,
            lead,
            [
                (w_out, 0, width, 1),
                (w_up, width, hidden_width, 1),
            ],
            sem,
        )
        fetch(sc, pieces, marks, lead, [(w_down, width + hidden_width, width, 4)], down_sem)
        ggain_ref[...] = jnp.zeros_like(ggain_ref)

    @pl.when(tile == 0)
    def _():
        normal = sums_ref[0, :head] / sums_ref[0, head : head + 1] * scale
        for b in range(width // half):
            kvn[b] = block_diagonal(normal[:, b * half : (b + 1) * half], head).astype(BF)
        gacc[...] = jnp.zeros_like(gacc)

    ok = valid_rows(sc, micro, tile * rows, rows, cols)
    q = q_ref[0]
    qf = q.astype(F32)
    conv = conv_ref[0]
    factor = jnp.concatenate(
        [dot_nt(q[:, b * half : (b + 1) * half], kvn[b]) for b in range(width // half)], axis=1
    )
    att = (factor + qf * conv).astype(BF)
    att_ref[0] = att

    @pl.when((micro == 0) & (tile == 0))
    def _():
        pltpu.make_async_copy(w_out, w_out, sem).wait()
        pltpu.make_async_copy(w_up, w_up, sem).wait()
        pltpu.make_async_copy(w_down, w_down, down_sem).wait()

    middle = resid_ref[0] + dot(att, w_out[...])
    unit, inverse = unit_rows(middle)
    gain = gain_ref[...]
    n2 = (unit * gain).astype(BF)
    n2_ref[0] = n2
    g_top = cot_ref[0].astype(F32) * ok
    g_ffn = g_top.astype(BF)
    gffn_ref[0] = g_ffn
    ffn = jnp.zeros((tokens, width), F32)
    back = jnp.zeros((tokens, width), F32)
    step = 512
    for c in range(0, hidden_width, step):
        hidden = dot(n2, w_up[:, c : c + step])
        cdf = 0.5 * (1.0 + lax.erf(hidden * (1.0 / math.sqrt(2.0))))
        act = (hidden * cdf).astype(BF)
        slope = cdf + hidden * jnp.exp(-0.5 * hidden * hidden) * (1.0 / math.sqrt(2.0 * math.pi))
        act_ref[0, :, c : c + step] = act
        ffn = ffn + dot(act, w_down[c : c + step, :])
        g_hidden = (dot_nt(g_ffn, w_down[c : c + step, :]) * slope).astype(BF)
        gh_ref[0, :, c : c + step] = g_hidden
        back = back + dot_nt(g_hidden, w_up[:, c : c + step])
    out_ref[0] = ((middle + ffn) * ok).astype(BF)
    ggain_ref[...] += jnp.sum(back * unit, axis=0, keepdims=True)
    g_middle = g_top + norm_back(back, unit, inverse, gain)
    gm_ref[0] = g_middle
    g_proj = g_middle.astype(BF)
    gproj_ref[0] = g_proj
    g_att = dot_nt(g_proj, w_out[...])
    g_conv = g_att * qf
    gconv_ref[0] = g_conv

    @pl.when(tile == 0)
    def _():
        pack_rim(first_ref, [g_conv[r * cols : (r + 1) * cols] for r in range(RIM)])

    @pl.when(tile == pl.num_programs(1) - 1)
    def _():
        pack_rim(last_ref, [g_conv[(rows - 1 - r) * cols : (rows - r) * cols] for r in range(RIM)])

    low = g_att.astype(BF)
    for b in range(width // half):
        lanes = slice(b * half, (b + 1) * half)
        gq_ref[0, :, lanes] = (
            g_att[:, lanes] * conv[:, lanes] + dot(low[:, lanes], kvn[b])
        ).astype(BF)
        gacc[b] += dot_tn(low[:, lanes], q[:, lanes])

    @pl.when(tile == pl.num_programs(1) - 1)
    def _():
        for b in range(width // half):
            gkv_ref[0, :, b * half : (b + 1) * half] = (
                diagonal_blocks(gacc[b], head) * scale
            ).astype(BF)


def place_blocks(sc, lead, order, value, keep_ref, send_ref, lane, parts):
    place = sc.place() >> lead
    lanes = value.shape[1]
    half = len(order) // 2
    for slot, mask in enumerate(order):
        block = place ^ (mask >> lead)
        target = keep_ref if slot < half else send_ref
        for part in range(parts):
            at = pl.multiple_of(block * (16 * parts) + 16 * part, 16)
            target[slot % half, :, pl.ds(lane + part * lanes, lanes)] = value[
                pl.ds(at, 16), :
            ].astype(BF)


def up_kernel(
    order, lead, sc, n2_ref, gh_ref, act_ref, gffn_ref, att_ref, gproj_ref, keep_ref, send_ref,
    acc, acc_down
):
    step, steps = pl.program_id(0), pl.num_programs(0)
    width, chunk = n2_ref.shape[1], gh_ref.shape[1]

    @pl.when(step == 0)
    def _():
        acc[...] = dot_tn(att_ref[...], gproj_ref[...])
        place_blocks(sc, lead, order, acc, keep_ref, send_ref, 0, 1)

    acc[...] = dot_tn(n2_ref[...], gh_ref[...])
    lane = pl.multiple_of(width + step * chunk, 128)
    place_blocks(sc, lead, order, acc, keep_ref, send_ref, lane, 1)
    acc_down[pl.ds(pl.multiple_of(step * chunk, chunk), chunk), :] = dot_tn(
        act_ref[...], gffn_ref[...]
    )

    @pl.when(step == steps - 1)
    def _():
        lane = width + chunk * steps
        place_blocks(sc, lead, order, acc_down, keep_ref, send_ref, lane, 4)


def taps_kernel(v_ref, top_ref, bot_ref, g_ref, o3, o5, o7, pad, sums):
    rows, cols = g_ref.shape[1], g_ref.shape[2]

    @pl.when(pl.program_id(0) == 0)
    def _():
        o3[...] = jnp.zeros_like(o3)
        o5[...] = jnp.zeros_like(o5)
        o7[...] = jnp.zeros_like(o7)

    fill_rimmed(pad, lambda r: v_ref[0, r], rows, top_ref, bot_ref)
    for g, (o, lanes, size) in enumerate(((o3, 0, 3), (o5, 0, 5), (o7, 0, 7), (o7, 128, 7))):
        tap_sums(pad, g_ref, o, sums, lanes, g, size, RIM)


def back_kernel(
    marks, lead, sc, k_ref, v_ref, sums_ref, gkv_ref, gc_ref, top_ref, bot_ref, gq_ref, resid_ref,
    gm_ref, gain_ref, w3, w5, w7, *refs
):
    pieces = refs[: len(marks)]
    gqkv_ref, gu_ref, first_ref, last_ref, ggain_ref, whole, pad, gv_buf, sem = refs[len(marks) :]
    micro = pl.program_id(0)
    rows, cols = gc_ref.shape[1], gc_ref.shape[2]
    tokens, width = k_ref.shape[1], k_ref.shape[2]
    head = width // HEADS
    half = 4 * head

    @pl.when(micro == 0)
    def _():
        fetch(sc, pieces, marks, lead, [(whole, 0, 3 * width, 1)], sem)
        ggain_ref[...] = jnp.zeros_like(ggain_ref)

    fill_rimmed(pad, lambda r: gc_ref[0, r], rows, top_ref, bot_ref)

    def one(r, carry):
        for g, (w, lanes, size) in enumerate(((w3, 0, 3), (w5, 0, 5), (w7, 0, 7), (w7, 128, 7))):
            gv_buf[r, :, g * 128 : (g + 1) * 128] = tap_row(
                pad, w, lanes, g, r + RIM, cols, size, None, True
            )
        return carry

    lax.fori_loop(0, rows, one, 0)

    ok = valid_rows(sc, micro, 0, rows, cols)
    total = sums_ref[0, head : head + 1]
    top = sums_ref[0, head + 1 : head + 2]
    normal = sums_ref[0, :head] / total
    gkv = gkv_ref[0]
    inner = jnp.sum(normal * gkv, axis=0, keepdims=True)
    probs = jnp.where(ok > 0, jnp.exp(k_ref[0].astype(F32) - top) / total, 0.0)
    low = probs.astype(BF)
    v = v_ref[0].reshape(tokens, width)
    gqkv_ref[0, :, :width] = gq_ref[0]
    for b in range(width // half):
        lanes = slice(b * half, (b + 1) * half)
        diag = block_diagonal(gkv[:, lanes], head).astype(BF)
        gk = probs[:, lanes] * (dot(v[:, lanes], diag) - inner[:, lanes])
        gqkv_ref[0, :, width + b * half : width + (b + 1) * half] = gk.astype(BF)
        gv = dot_nt(low[:, lanes], diag) + gv_buf[:, :, lanes].reshape(tokens, half)
        gqkv_ref[0, :, 2 * width + b * half : 2 * width + (b + 1) * half] = gv.astype(BF)

    @pl.when(micro == 0)
    def _():
        pltpu.make_async_copy(whole, whole, sem).wait()

    dy = dot_nt(gqkv_ref[0], whole[...])
    unit, inverse = unit_rows(resid_ref[0])
    ggain_ref[...] += jnp.sum(dy * unit, axis=0, keepdims=True)
    gu = (gm_ref[0] + norm_back(dy, unit, inverse, gain_ref[...])) * ok
    gu_ref[0] = gu.reshape(rows, cols, width)
    first_ref[0, 0] = gu[:cols].astype(BF)
    last_ref[0, 0] = gu[tokens - cols :].astype(BF)


def place_seven(at, width):
    return at % 16, width + 256 * (at // 16)


def place_three(at):
    return 11 + at // 4, 128 * (at % 4)


def place_five(at, width):
    return 1 + at % 13, width + 768 + 128 * (at // 13)


def last_grads_kernel(
    order, lead, sc, x_ref, top_ref, bot_ref, gu_ref, n_ref, g_ref, o3, o5, o7, gain1, gain2,
    keep_ref, send_ref, small_ref, pad, sums, pos, acc, small
):
    micro = pl.program_id(0)
    rows, cols = x_ref.shape[2], x_ref.shape[3]
    width = n_ref.shape[-1]
    clear_edges(pad)
    cols_ok = valid_cols(sc, micro, cols)

    @pl.when(micro == 0)
    def _():
        pos[...] = jnp.zeros_like(pos)

    def put(r, cells):
        put_row(pad, r + 1, cells.astype(F32), cols_ok * valid_row(sc, micro, r))

    def fill(r, carry):
        put(r, x_ref[0, 0, r])
        return carry

    lax.fori_loop(0, rows, fill, 0)
    put(-1, top_ref[0, 0])
    put(rows, bot_ref[0, 0])
    for g in range(pad.shape[0]):
        tap_sums(pad, gu_ref, pos, sums, g * 128, g, 3, 1)
    tokens = rows * cols
    n = n_ref[0].reshape(tokens, width)
    for c in range(0, g_ref.shape[2], width):
        part = dot_tn(n, g_ref[0, :, c : c + width])

        @pl.when(micro == 0)
        def _():
            acc[:, c : c + width] = part

        @pl.when(micro > 0)
        def _():
            acc[:, c : c + width] += part

    @pl.when(micro == pl.num_programs(0) - 1)
    def _():
        place_blocks(sc, lead, order, acc, keep_ref, send_ref, 0, 1)
        small[...] = jnp.zeros_like(small)
        small[:9, :width] = pos[...]
        small[9:10, :width] = gain1[...]
        small[10:11, :width] = gain2[...]
        for at in range(49):
            line, lane = place_seven(at, width)
            small[line : line + 1, lane : lane + 256] = o7[at : at + 1, :]
        for at in range(9):
            line, lane = place_three(at)
            small[line : line + 1, lane : lane + 128] = o3[at : at + 1, :]
        for at in range(25):
            line, lane = place_five(at, width)
            small[line : line + 1, lane : lane + 128] = o5[at : at + 1, :]
        small_ref[...] = small[...].astype(BF)


def start_grad_kernel(sc, gu_ref, top_ref, bot_ref, w_ref, o_ref, pad):
    micro = pl.program_id(0)
    rows, cols = gu_ref.shape[1], gu_ref.shape[2]
    clear_edges(pad)
    cols_ok = valid_cols(sc, micro, cols)

    def fill(r, carry):
        put_row(pad, 1 + r, gu_ref[0, r])
        return carry

    lax.fori_loop(0, rows, fill, 0)
    put_row(pad, 0, top_ref[0, 0].astype(F32))
    put_row(pad, rows + 1, bot_ref[0, 0].astype(F32))

    def one(r, carry):
        ok = cols_ok * valid_row(sc, micro, r)
        for g in range(pad.shape[0]):
            taps = tap_row(pad, w_ref, g * 128, g, r + 1, cols, 3, None, True)
            o_ref[0, 0, r, :, g * 128 : (g + 1) * 128] = (
                taps + pad[g, r + 1, EDGE : EDGE + cols, :]
            ) * ok
        return carry

    lax.fori_loop(0, rows, one, 0)


def add_kernel(parts, *refs):
    outs = refs[-parts:]
    ins = refs[:-parts]
    total = ins[0][...].astype(F32)
    for ref in ins[1:]:
        total = total + ref[...].astype(F32)
    for n in range(parts):
        outs[n][...] = total[n].astype(outs[n].dtype)


def sum_small(refs):
    sums = [ref[...].astype(F32) for ref in refs]
    while len(sums) > 1:
        sums = [a + b for a, b in zip(sums[::2], sums[1::2])]
    return sums[0]


def add_small_kernel(parts, count, *refs):
    ins, small, outs = refs[:count], refs[count:-parts], refs[-parts:]
    size = outs[0].shape[0] - 1
    for n in range(parts):
        for b in range(size):
            total = ins[0][n * size + b].astype(F32)
            for ref in ins[1:]:
                total = total + ref[n * size + b].astype(F32)
            outs[n][b] = total.astype(outs[n].dtype)
    if not small:
        small = [ref.at[parts * size] for ref in ins]
    low = sum_small(small).astype(BF)
    for n in range(parts):
        outs[n][size] = low.astype(outs[n].dtype)


def rest_kernel(*refs):
    out_ref, up_ref, down_ref = refs[-3:]
    total = refs[0][0]
    for ref in refs[1:-3]:
        total = total + ref[0].astype(F32)
    width, hidden = out_ref.shape[1], up_ref.shape[1]
    out_ref[...] = total[:, :width]
    up_ref[...] = total[:, width : width + hidden]
    for part in range(4):
        lane = width + hidden + part * width
        down_ref[16 * part : 16 * part + 16, :] = total[:, lane : lane + width]


def small_kernel(s_ref, pos, three, five, seven, gain1, gain2):
    width = gain1.shape[1]
    for i in range(3):
        for j in range(3):
            at = 3 * i + j
            pos[i, j : j + 1, :] = s_ref[at : at + 1, :width]
            line, lane = place_three(at)
            three[i, j : j + 1, :] = s_ref[line : line + 1, lane : lane + 128]
    for i in range(5):
        for j in range(5):
            line, lane = place_five(5 * i + j, width)
            five[i, j : j + 1, :128] = s_ref[line : line + 1, lane : lane + 128]
            line, lane = place_seven(7 * i + j + 8, width)
            five[i, j : j + 1, 128:192] = s_ref[line : line + 1, lane : lane + 64]
    for i in range(7):
        for j in range(7):
            line, lane = place_seven(7 * i + j, width)
            seven[i, j : j + 1, :] = s_ref[line : line + 1, lane + 64 : lane + 256]
    gain1[...] = s_ref[9:10, :width]
    gain2[...] = s_ref[10:11, :width]


def ends_kernel(split, *refs):
    ins, qkv_ref, outs = refs[:4], refs[4], refs[5:]
    total = ins[0][0]
    for ref in ins[1:]:
        total = total + ref[0].astype(F32)
    qkv_ref[...] = total
    outs[-1][...] = sum_small([ref.at[1] for ref in ins])
    if split:
        small_kernel(outs[-1], *outs[:-1])


SMEM = pl.BlockSpec(memory_space=pltpu.SMEM)
ANY = pl.BlockSpec(memory_space=pl.ANY)


def by_micro(shape):
    rest = tuple(shape[1:])
    return pl.BlockSpec((1,) + rest, lambda m: (m,) + (0,) * len(rest))


def whole_spec(shape):
    return pl.BlockSpec(tuple(shape), lambda *_: (0,) * len(shape))


def shaped(shape, dtype):
    return jax.ShapeDtypeStruct(tuple(shape), dtype)


def call(
    kernel, name, grid, ins, outs, scratch, micros_long, deps=(), alias=None, carry=(), rows_here=8
):
    nbytes = sum(a.size * a.dtype.itemsize for _, a in ins)
    nbytes += sum(math.prod(s) * jnp.dtype(d).itemsize for _, s, d in outs)
    first, last = len(ins), len(ins) + len(deps) + len(carry)
    results = last + len(outs)

    def body(*refs):
        if ins and ins[0][0] is SMEM:
            refs = (Here(refs[0], rows_here),) + refs[1:]
        kernel(*refs[:first], *refs[last:results], *refs[results + len(carry) :])

    alias = dict(alias or {})
    for n in range(len(carry)):
        alias[first + len(deps) + n] = len(outs) + n
    return pl.pallas_call(
        body,
        name=name,
        grid=grid,
        in_specs=[s for s, _ in ins] + [ANY] * (len(deps) + len(carry)),
        out_specs=[s for s, _, _ in outs] + [ANY] * len(carry),
        out_shape=[shaped(s, d) for _, s, d in outs] + [shaped(c.shape, c.dtype) for c in carry],
        scratch_shapes=scratch,
        input_output_aliases=alias,
        cost_estimate=pl.CostEstimate(
            flops=int(micros_long * 1.15e9), bytes_accessed=int(nbytes), transcendentals=0
        ),
        compiler_params=pltpu.CompilerParams(
            vmem_limit_bytes=VMEM_MIB * MIB, dimension_semantics=("arbitrary",) * len(grid)
        ),
    )(*[a for _, a in ins], *deps, *carry)


def gate_kernel(*refs):
    pass


def gate(values, deps):
    return call(gate_kernel, "gate", (), [], [], [], 0, deps=deps, carry=values)


def add_parts(arrays, parts, deps=(), carry=()):
    n, rows, lanes = arrays[0].shape[1:]
    return call(
        functools.partial(add_kernel, parts),
        "add_parts",
        (n,),
        [(pl.BlockSpec((parts, 1, rows, lanes), lambda i: (0, i, 0, 0)), a) for a in arrays],
        [
            (
                pl.BlockSpec((1, rows, lanes), lambda i: (i, 0, 0)),
                (n, rows, lanes),
                F32 if p == 0 else BF,
            )
            for p in range(parts)
        ],
        [],
        2,
        deps,
        carry=carry,
    )


def add_small(arrays, small, parts, deps=()):
    blocks, rows, lanes = arrays[0].shape
    shape = ((blocks if small else blocks - 1) // parts + 1, rows, lanes)
    every = list(arrays) + list(small)
    return call(
        functools.partial(add_small_kernel, parts, len(arrays)),
        "add_small",
        (1,),
        [(whole_spec(a.shape), a) for a in every],
        [(whole_spec(shape), shape, F32 if p == 0 else BF) for p in range(parts)],
        [],
        2,
        deps,
    )


def local(
    images,
    cotangent,
    extent,
    w_qkv,
    w_out,
    w_up,
    w_down,
    pos_weight,
    win_three,
    win_five,
    win_seven,
    gain_one,
    gain_two,
):
    micros, _, rows, cols, width = images.shape
    head = width // HEADS
    hidden = w_up.shape[1]
    tokens = rows * cols
    me = positions()
    lead_masks, first, second, third = plan(w_up.shape[0])
    lead = len(lead_masks)
    stages = (first, second, third)
    sc = (SMEM, extent)
    n5 = 128
    gain1, gain2 = gain_one.reshape(1, width), gain_two.reshape(1, width)
    pad_rim = pltpu.VMEM((width // 128, rows + 2 * RIM, cols + 2 * EDGE, 128), F32)
    pad_one = pltpu.VMEM((width // 128, rows + 2, cols + 2 * EDGE, 128), F32)

    flat = (micros, tokens, width)
    map_shape = (micros, rows, cols, width)
    rim_shape = (micros, cols, rim_lanes(width)[1])
    q_block = join_lead(w_qkv, lead_masks)
    joined = [join_lead(w, lead_masks) for w in (w_out, w_up, w_down)]
    lanes = width + 2 * hidden
    taps3, w3, w5, w7, r_block = call(
        prep_kernel,
        "prep",
        (1,),
        [
            (whole_spec(w.shape), w)
            for w in (pos_weight, win_three, win_five, win_seven, *joined)
        ],
        [
            (whole_spec(shape), shape, F32)
            for shape in ((9, width), (9, 128), (25, n5), (49, 256))
        ]
        + [(whole_spec((16, lanes)), (16, lanes), BF)],
        [],
        2,
    )
    windows = [(whole_spec(w.shape), w) for w in (w3, w5, w7)]

    def gather_second(own):
        return [own] + [flipped(own, m) for m in spans(second)[1:]]

    def gather_third(pieces):
        return pieces + [flipped(p, third[0]) for p in pieces]

    marks = spans(second)
    marks = marks + [m ^ third[0] for m in marks]
    marks = [[m ^ f for f in spans(first)] for m in marks]

    def single(shape, micro):
        rest = tuple(shape[1:])
        return pl.BlockSpec((1,) + rest, lambda m: (micro,) + (0,) * len(rest))

    q_blocks = [q_block] + [flipped(q_block, m) for m in spans(first)[1:]]
    edge = (micros, 1, cols, width)

    def edge_spec(row):
        return pl.BlockSpec((micros, 1, 1, cols, width), lambda _: (0, 0, row, 0, 0))

    own_shape = (len(q_blocks),) + q_block.shape
    q_own, x_first, x_last = call(
        functools.partial(first_kernel, len(q_blocks)),
        "first",
        (1,),
        [(whole_spec(b.shape), b) for b in q_blocks]
        + [(edge_spec(0), images), (edge_spec(rows - 1), images)],
        [
            (whole_spec(own_shape), own_shape, BF),
            (whole_spec(edge), edge, BF),
            (whole_spec(edge), edge, BF),
        ],
        [],
        1,
        deps=[r_block],
    )
    x_top, x_bot = rims(x_first, x_last)
    q_pieces = gather_second(q_own)
    x_in = pl.BlockSpec((1, 1, rows, cols, width), lambda m: (m, 0, 0, 0, 0))
    r_blocks = [r_block] + [flipped(r_block, m) for m in spans(first)[1:]]
    r_shape = (len(r_blocks),) + r_block.shape
    (r_own,) = call(
        stack_kernel,
        "stack",
        (1,),
        [(whole_spec(b.shape), b) for b in r_blocks],
        [(whole_spec(r_shape), r_shape, BF)],
        [],
        1,
        deps=[x_top, x_bot],
    )
    normed, resid = call(
        norm_kernel,
        "norm",
        (micros,),
        [
            sc,
            (x_in, images),
            (by_micro(edge), x_top),
            (by_micro(edge), x_bot),
            (whole_spec(taps3.shape), taps3),
            (whole_spec(gain1.shape), gain1),
        ],
        [(by_micro(map_shape), map_shape, BF), (by_micro(map_shape), map_shape, F32)],
        [pad_one],
        8,
        deps=q_pieces[1:],
    )
    qkv_pieces = gather_third(q_pieces)
    r_pieces = list(gate([r_own] + [flipped(r_own, m) for m in second], [normed]))
    r_pieces = r_pieces + [flipped(r_pieces[1], second[1])]
    sums_shape = (micros, head + 16, width)
    q, k, v, sums, v_first, v_last = call(
        functools.partial(qkv_kernel, marks, lead),
        "qkv",
        (micros,),
        [sc, (by_micro(map_shape), normed)] + [(ANY, p) for p in qkv_pieces],
        [
            (by_micro(flat), flat, BF),
            (by_micro(flat), flat, BF),
            (by_micro(map_shape), map_shape, BF),
            (by_micro(sums_shape), sums_shape, BF),
            (by_micro(rim_shape), rim_shape, BF),
            (by_micro(rim_shape), rim_shape, BF),
        ],
        [pltpu.VMEM((width, 3 * width), BF), pltpu.SemaphoreType.DMA],
        6,
        deps=[r_own],
    )

    def join_strips(kernel, cells, stage, dtype, deps, carry=()):
        parts = [cells] + [strip_swap(cells, m) for m in spans(stage)[1:]]
        spec = whole_spec(cells.shape)
        return call(
            kernel,
            "join",
            (1,),
            [(spec, p) for p in parts],
            [(spec, cells.shape, dtype)],
            [],
            1,
            deps=deps,
            carry=carry,
        )

    near, far = strip_stages()
    v_top, v_bot = rims(v_first, v_last)
    (conv,) = call(
        window_kernel,
        "window",
        (micros,),
        [(by_micro(map_shape), v)] + windows,
        [(by_micro(map_shape), map_shape, F32)],
        [pltpu.VMEM((width // 128, rows, cols + 2 * EDGE, 128), F32)],
        6,
    )
    join = functools.partial(join_kernel, head)
    (sums,) = join_strips(join, sums, near, BF, [v_top, v_bot, conv])
    (conv,) = call(
        window_rim_kernel,
        "window_rim",
        (micros,),
        [
            (by_micro(map_shape), conv),
            (by_micro(rim_shape), v_top),
            (by_micro(rim_shape), v_bot),
        ]
        + windows,
        [(by_micro(map_shape), map_shape, F32)],
        [pltpu.VMEM((width // 128, 2 * RIM, cols + 2 * EDGE, 128), F32)],
        3,
        deps=[sums],
    )
    r_pieces = list(gate(r_pieces, [sums]))
    (sums,) = join_strips(join, sums, far, F32, [conv])
    rest_pieces = gather_third(r_pieces)

    tile_rows = rows
    tile = tile_rows * cols
    tiles = rows // tile_rows

    def tiled(lanes):
        return pl.BlockSpec((1, tile, lanes), lambda m, t: (m, t, 0))

    def per_micro(shape):
        return pl.BlockSpec((1,) + tuple(shape[1:]), lambda m, t: (m,) + (0,) * (len(shape) - 1))

    wide = (micros, tokens, hidden)
    gkv_shape = (micros, head, width)
    outs = call(
        functools.partial(main_kernel, marks, lead),
        "main",
        (micros, tiles),
        [
            sc,
            (per_micro(sums_shape), sums),
            (tiled(width), q),
            (tiled(width), conv.reshape(flat)),
            (tiled(width), resid.reshape(flat)),
            (tiled(width), cotangent.reshape(flat)),
            (whole_spec(gain2.shape), gain2),
        ]
        + [(ANY, p) for p in rest_pieces],
        [
            (tiled(width), flat, BF),
            (tiled(hidden), wide, BF),
            (tiled(hidden), wide, BF),
            (tiled(width), flat, BF),
            (tiled(width), flat, BF),
            (tiled(width), flat, BF),
            (tiled(width), flat, BF),
            (tiled(width), flat, F32),
            (tiled(width), flat, BF),
            (tiled(width), flat, F32),
            (per_micro(gkv_shape), gkv_shape, BF),
            (per_micro(rim_shape), rim_shape, BF),
            (per_micro(rim_shape), rim_shape, BF),
            (whole_spec((1, width)), (1, width), F32),
        ],
        [
            pltpu.VMEM((width, width), BF),
            pltpu.VMEM((width, hidden), BF),
            pltpu.VMEM((hidden, width), BF),
            pltpu.VMEM((width // (4 * head), 4 * head, 4 * head), BF),
            pltpu.VMEM((width // (4 * head), 4 * head, 4 * head), F32),
            pltpu.SemaphoreType.DMA,
            pltpu.SemaphoreType.DMA,
        ],
        24,
    )
    out, act, g_hidden, n2, att, g_ffn, g_proj, g_conv, gq, g_middle, gkv = outs[:11]
    gc_first, gc_last, ggain2 = outs[11:]
    g_conv = g_conv.reshape(map_shape)
    gc_top, gc_bot = rims(gc_first, gc_last)

    marked = [0]
    for stage in (first, second, third):
        marked = [o ^ m for m in spans(stage) for o in marked]
    slots = len(marked) // 2

    def flat2(a):
        return a.reshape(-1, a.shape[-1])

    def staged(block, parts):
        return block.reshape((parts, block.shape[0] // parts) + block.shape[1:])

    half_shape = (slots, 16, lanes)
    ops = [flat2(a) for a in (n2, g_hidden, act, g_ffn, att, g_proj)]
    chunk = 512

    def columns(a):
        return pl.BlockSpec((a.shape[0], chunk), lambda c: (0, c))

    keep, send = call(
        functools.partial(up_kernel, marked, lead),
        "mlp_grads",
        (hidden // chunk,),
        [sc]
        + [
            (columns(a) if a.shape[1] == hidden else whole_spec(a.shape), a)
            for a in ops
        ],
        [(whole_spec(half_shape), half_shape, BF)] * 2,
        [pltpu.VMEM((width, chunk), F32), pltpu.VMEM((hidden, width), F32)],
        12,
    )
    gkv, send = join_strips(sum_kernel, gkv, near, BF, [gc_top, gc_bot, keep], [send])
    got = flipped(send, third[0])
    o3, o5, o7 = call(
        taps_kernel,
        "window_grads",
        (micros,),
        [
            (by_micro(map_shape), v),
            (by_micro(rim_shape), v_top),
            (by_micro(rim_shape), v_bot),
            (by_micro(map_shape), g_conv),
        ],
        [
            (whole_spec((9, 128)), (9, 128), F32),
            (whole_spec((25, 128)), (25, 128), F32),
            (whole_spec((49, 256)), (49, 256), F32),
        ],
        [pad_rim, pltpu.VMEM((49, 8, 128), F32)],
        6,
        deps=[gkv],
    )
    parts2, parts1 = len(spans(second)), len(spans(first))
    (gkv,) = join_strips(sum_kernel, gkv, far, F32, [o3])
    rest = add_parts([staged(keep, parts2), staged(got, parts2)], parts2, [gkv])
    rest_got = [flipped(o, m) for o, m in zip(rest[1:], spans(second)[1:])]

    g_qkv, g_u, gu_first, gu_last, ggain1 = call(
        functools.partial(back_kernel, marks, lead),
        "back",
        (micros,),
        [
            sc,
            (by_micro(flat), k),
            (by_micro(map_shape), v),
            (by_micro(sums_shape), sums),
            (by_micro(gkv_shape), gkv),
            (by_micro(map_shape), g_conv),
            (by_micro(rim_shape), gc_top),
            (by_micro(rim_shape), gc_bot),
            (by_micro(flat), gq),
            (by_micro(flat), resid.reshape(flat)),
            (by_micro(flat), g_middle),
            (whole_spec(gain1.shape), gain1),
        ]
        + windows
        + [(ANY, p) for p in qkv_pieces],
        [
            (by_micro((micros, tokens, 3 * width)), (micros, tokens, 3 * width), BF),
            (by_micro(map_shape), map_shape, F32),
            (by_micro(edge), edge, BF),
            (by_micro(edge), edge, BF),
            (whole_spec((1, width)), (1, width), F32),
        ],
        [
            pltpu.VMEM((width, 3 * width), BF),
            pad_rim,
            pltpu.VMEM((rows, cols, width), F32),
            pltpu.SemaphoreType.DMA,
        ],
        15,
        deps=[rest[0]],
    )
    gu_top, gu_bot = rims(gu_first, gu_last)
    half_shape = (slots, 16, 3 * width)
    small_shape = (16, 3 * width)
    keep, send, small = call(
        functools.partial(last_grads_kernel, marked, lead),
        "last_grads",
        (micros,),
        [
            sc,
            (x_in, images),
            (by_micro(x_top.shape), x_top),
            (by_micro(x_bot.shape), x_bot),
            (by_micro(map_shape), g_u),
            (by_micro(map_shape), normed),
            (by_micro(g_qkv.shape), g_qkv),
        ]
        + [(whole_spec(a.shape), a) for a in (o3, o5, o7, ggain1, ggain2)],
        [
            (whole_spec(half_shape), half_shape, BF),
            (whole_spec(half_shape), half_shape, BF),
            (whole_spec(small_shape), small_shape, BF),
        ],
        [
            pad_one,
            pltpu.VMEM((9, 8, 128), F32),
            pltpu.VMEM((9, width), F32),
            pltpu.VMEM((width, 3 * width), F32),
            pltpu.VMEM(small_shape, F32),
        ],
        1,
    )
    *rest, send, small = add_parts(
        [staged(p, parts1) for p in [rest[0]] + rest_got],
        parts1,
        [keep, gu_top, gu_bot],
        [send, small],
    )
    got, small_got = flipped(send, third[0]), flipped(small, third[0])
    rest_got = [flipped(o, m) for o, m in zip(rest[1:], spans(first)[1:])]
    own = add_small([keep, got], [small, small_got], parts2, [rest[0]])
    own_got = [flipped(o, m) for o, m in zip(own[1:], spans(second)[1:])]
    (grad_in,) = call(
        start_grad_kernel,
        "input_grad",
        (micros,),
        [
            sc,
            (by_micro(map_shape), g_u),
            (by_micro(gu_top.shape), gu_top),
            (by_micro(gu_bot.shape), gu_bot),
            (whole_spec(taps3.shape), taps3),
        ],
        [(x_in, (micros, 1, rows, cols, width), F32)],
        [pad_one],
        3,
        deps=[own[0]],
    )
    own = [own[0]] + own_got
    own = add_small(own, [], parts1, [grad_in])
    own_got = [flipped(o, m) for o, m in zip(own[1:], spans(first)[1:])]
    own = [own[0]] + own_got
    rest = [rest[0]] + rest_got

    def lead_sum(total):
        for mask in reversed(lead_masks):
            size = total.shape[0] // 2
            low, high = total[:size], total[size:]
            bit = (me & mask) != 0
            kept, sent = jnp.where(bit, high, low), jnp.where(bit, low, high)
            total = kept + flipped(sent, mask)
        return total

    def call_whole(kernel, name, arrays, shapes, deps=()):
        return call(
            kernel,
            name,
            (1,),
            [(whole_spec(a.shape), a) for a in arrays],
            [(whole_spec(shape), shape, F32) for shape in shapes],
            [],
            1,
            deps=deps,
        )

    rest_shapes = [(16, width), (16, hidden), (64, width)]
    grad_out, grad_up, grad_down = call_whole(rest_kernel, "rest_sum", rest, rest_shapes, own[:1])
    small_shapes = [w.shape for w in (pos_weight, win_three, win_five, win_seven)]
    small_shapes = small_shapes + [gain1.shape] * 2
    if lead_masks:
        grad_out, grad_up, grad_down = (lead_sum(g) for g in (grad_out, grad_up, grad_down))
        grad_qkv, small = call_whole(
            functools.partial(ends_kernel, False), "last_sum", own, [small_shape] * 2
        )
        grad_qkv = lead_sum(grad_qkv)
        low = small.astype(BF)
        got = [low.astype(F32)] + [flipped(low, m).astype(F32) for m in spans(lead_masks)[1:]]
        while len(got) > 1:
            got = [a + b for a, b in zip(got[::2], got[1::2])]
        smalls = call_whole(small_kernel, "small_grads", got, small_shapes)
    else:
        grad_qkv, *smalls, _ = call_whole(
            functools.partial(ends_kernel, True),
            "last_sum",
            own,
            [small_shape] + small_shapes + [small_shape],
        )
    g_pos, g_three, g_five, g_seven, ggain1, ggain2 = smalls
    return (
        out.reshape(micros, 1, rows, cols, width),
        grad_in,
        grad_qkv,
        grad_out,
        grad_up,
        grad_down,
        g_pos,
        g_three,
        g_five,
        g_seven,
        ggain1.reshape(width),
        ggain2.reshape(width),
    )


def solution(mesh):
    in_specs = (
        P(None, "img", "strip", None, None),
        P(None, "img", "strip", None, None),
        P(None, "img", None),
        P(("img", "strip"), None),
        P(("img", "strip"), None),
        P(("img", "strip"), None),
        P(("img", "strip"), None),
        P(),
        P(),
        P(),
        P(),
        P(),
        P(),
    )
    out_specs = (
        P(None, "img", "strip", None, None),
        P(None, "img", "strip", None, None),
        P(("img", "strip"), None),
        P(("img", "strip"), None),
        P(("img", "strip"), None),
        P(("img", "strip"), None),
        P(),
        P(),
        P(),
        P(),
        P(),
        P(),
    )
    return jax.shard_map(local, mesh=mesh, in_specs=in_specs, out_specs=out_specs, check_vma=False)
```

```python
import functools
import math

import jax
import jax.numpy as jnp
from jax import lax
from jax.experimental import pallas as pl
from jax.experimental.pallas import tpu as pltpu
from jax.sharding import PartitionSpec as P

HEADS = 8
norm_eps = 1e-06
masked_low = -1e30
RIM = 3
EDGE = 8
BF = jnp.bfloat16
F32 = jnp.float32
MIB = 2**20
VMEM_MIB = 63


def positions():
    return lax.axis_index("img") * lax.axis_size("strip") + lax.axis_index("strip")


def flipped(cells, mask):
    count = lax.axis_size("img") * lax.axis_size("strip")
    return lax.ppermute(cells, ("img", "strip"), [(i, i ^ mask) for i in range(count)])


def plan(shard_rows):
    strip_bits = int(math.log2(lax.axis_size("strip")))
    img_bits = int(math.log2(lax.axis_size("img")))
    lead = 0
    while (shard_rows << lead) < 16:
        lead += 1
    free = [1 << b for b in range(lead, strip_bits)]
    img = [1 << (strip_bits + b) for b in range(1, img_bits)]
    if len(free) > 2:
        first, second = [free[0], free[2]], [free[1]] + img
    else:
        first, second = free, img
    return [1 << b for b in range(lead)], first, second, [1 << strip_bits]


def sum_stages(first, second):
    masks = sorted(first + second)
    return (masks[1:3], [masks[0]] + masks[3:]) if len(masks) == 4 else (first, second)


def spans(masks):
    out = [0]
    for mask in masks:
        out = out + [o ^ mask for o in out]
    return out


def join_lead(shard, lead):
    me = positions()
    for mask in lead:
        other = flipped(shard, mask)
        shard = jnp.where(
            (me & mask) != 0, jnp.concatenate([other, shard]), jnp.concatenate([shard, other])
        )
    return shard


def strip_swap(cells, mask):
    count = lax.axis_size("strip")
    return lax.ppermute(cells, "strip", [(i, i ^ mask) for i in range(count)])


def strip_stages():
    masks = [1 << b for b in range(int(math.log2(lax.axis_size("strip"))))]
    return [masks[:2], masks[2:]]


def rims(first, last):
    count = lax.axis_size("strip")
    above = lax.ppermute(last, "strip", [(i, i + 1) for i in range(count - 1)])
    below = lax.ppermute(first, "strip", [(i + 1, i) for i in range(count - 1)])
    return above, below


class Here:
    def __init__(self, extent_ref, strip_rows):
        self.extent = extent_ref
        self.strip_rows = strip_rows

    def place(self):
        return positions()

    def first_row(self):
        return lax.axis_index("strip") * self.strip_rows

    def valid(self, micro, which):
        return self.extent[micro, 0, which]


def dot(a, b):
    return jnp.dot(a, b, preferred_element_type=F32)


def dot_nt(a, b):
    return lax.dot_general(a, b, (((1,), (1,)), ((), ())), preferred_element_type=F32)


def dot_tn(a, b):
    return lax.dot_general(a, b, (((0,), (0,)), ((), ())), preferred_element_type=F32)


def valid_rows(sc, micro, first_row, rows, cols):
    n = rows * cols
    shift = int(math.log2(cols))
    flat = lax.broadcasted_iota(jnp.int32, (n, 1), 0)
    row = lax.shift_right_logical(flat, shift) + (sc.first_row() + first_row)
    ok = (row < sc.valid(micro, 0)) & ((flat & (cols - 1)) < sc.valid(micro, 1))
    return jnp.where(ok, 1.0, 0.0).astype(F32)


def valid_cols(sc, micro, cols):
    col = lax.broadcasted_iota(jnp.int32, (cols, 128), 0)
    return jnp.where(col < sc.valid(micro, 1), 1.0, 0.0).astype(F32)


def valid_row(sc, micro, row):
    at = sc.first_row() + row
    return jnp.where((at >= 0) & (at < sc.valid(micro, 0)), 1.0, 0.0).astype(F32)


def unit_rows(fields):
    average = jnp.mean(fields, axis=-1, keepdims=True)
    centred = fields - average
    inverse = lax.rsqrt(jnp.mean(centred * centred, axis=-1, keepdims=True) + norm_eps)
    return centred * inverse, inverse


def norm_back(dy, unit, inverse, gain):
    dyg = dy * gain
    first = jnp.mean(dyg, axis=-1, keepdims=True)
    second = jnp.mean(dyg * unit, axis=-1, keepdims=True)
    return inverse * (dyg - first - unit * second)


def clear_edges(pad):
    groups, rows, cols, _ = pad.shape
    zeros = jnp.zeros((rows, EDGE, 128), F32)
    for g in range(groups):
        pad[g, :, :EDGE, :] = zeros
        pad[g, :, cols - EDGE :, :] = zeros


def put_row(pad, row, cells, ok=None):
    for g in range(pad.shape[0]):
        part = cells[:, g * 128 : (g + 1) * 128]
        pad[g, row, EDGE : EDGE + cells.shape[0], :] = part if ok is None else part * ok


def rim_lanes(width):
    out, lane = [], 0
    for row in range(RIM):
        out.append((row, lane))
        lane += width - 128 * row
    return out, lane


def pack_rim(rim_ref, lines):
    spans_, _ = rim_lanes(lines[0].shape[1])
    for line, (group, lane) in zip(lines, spans_):
        part = line[:, 128 * group :]
        rim_ref[0, :, lane : lane + part.shape[1]] = part.astype(BF)


def put_rims(pad, top_ref, bot_ref, rows):
    width = 128 * pad.shape[0]
    cols = top_ref.shape[1]
    for near, (group, lane) in enumerate(rim_lanes(width)[0]):
        for ref, line in ((top_ref, RIM - 1 - near), (bot_ref, RIM + rows + near)):
            for g in range(group, pad.shape[0]):
                at = lane + 128 * (g - group)
                pad[g, line, EDGE : EDGE + cols, :] = ref[0, :, at : at + 128].astype(F32)


def tap_row(pad, w_ref, lanes, group, row, cols, size, lines, flip):
    reach = size // 2
    total = jnp.zeros((cols, 128), F32)
    for i in lines or range(size):
        for j in range(size):
            at = i * size + j
            if flip:
                at = size * size - 1 - at
            w = w_ref[at : at + 1, lanes : lanes + 128]
            total = total + w * pad[
                group, row + i - reach, EDGE + j - reach : EDGE + j - reach + cols, :
            ]
    return total


def tap_sums(pad, grad_ref, out_ref, sums, lanes, group, size, above):
    reach = size // 2
    rows, cols = grad_ref.shape[1], grad_ref.shape[2]
    taps = size * size
    sums[:taps] = jnp.zeros((taps, 8, 128), F32)

    def step(t, carry):
        c = pl.multiple_of(t * 8, 8)
        grads = [
            grad_ref[0, r, pl.ds(c, 8), group * 128 : (group + 1) * 128].astype(F32)
            for r in range(rows)
        ]
        for j in range(size):
            got = [None] * size
            for line in range(rows + 2 * reach):
                f = pad[group, line + above - reach, pl.ds(c + EDGE + j - reach, 8), :]
                for i in range(size):
                    r = line - i
                    if 0 <= r < rows:
                        term = grads[r] * f
                        got[i] = term if got[i] is None else got[i] + term
            for i in range(size):
                sums[i * size + j] += got[i]
        return carry

    lax.fori_loop(0, cols // 8, step, 0)
    for at in range(taps):
        out_ref[at : at + 1, lanes : lanes + 128] += jnp.sum(sums[at], axis=0, keepdims=True)


def block_diagonal(wide, head):
    lane = lax.broadcasted_iota(jnp.int32, wide.shape, 1) // head
    return jnp.concatenate(
        [jnp.where(lane == h, wide, 0.0) for h in range(wide.shape[1] // head)], axis=0
    )


def diagonal_blocks(full, head):
    lane = lax.broadcasted_iota(jnp.int32, (head, full.shape[1]), 1) // head
    total = jnp.zeros((head, full.shape[1]), F32)
    for h in range(full.shape[1] // head):
        total = total + jnp.where(lane == h, full[h * head : (h + 1) * head], 0.0)
    return total


def fetch(sc, pieces, marks, lead, copy):
    place = sc.place() >> lead
    for piece, mark in zip(pieces, marks):
        for k, mask in enumerate(mark):
            copy(piece.at[k], place ^ (mask >> lead))


def rows_at(whole, block):
    return whole.at[pl.ds(pl.multiple_of(block * 16, 16), 16), :]


def taps_prep(pos_ref, three_ref, five_ref, seven_ref, taps3, w3, w5, w7):
    for i in range(3):
        for j in range(3):
            taps3[3 * i + j : 3 * i + j + 1, :] = pos_ref[i, j : j + 1, :]
            w3[3 * i + j : 3 * i + j + 1, :] = three_ref[i, j : j + 1, :]
    for i in range(5):
        for j in range(5):
            w5[5 * i + j : 5 * i + j + 1, :] = five_ref[i, j : j + 1, :128]
    for i in range(7):
        for j in range(7):
            seven = seven_ref[i, j : j + 1, :]
            low = jnp.zeros((1, 64), F32)
            if 1 <= i <= 5 and 1 <= j <= 5:
                low = five_ref[i - 1, j - 1 : j, 128:192]
            w7[7 * i + j : 7 * i + j + 1, :] = jnp.concatenate([low, seven], axis=1)


def prep_kernel(pos_ref, three_ref, five_ref, seven_ref, out_ref, up_ref, down_ref, *refs):
    taps_prep(pos_ref, three_ref, five_ref, seven_ref, *refs[:4])
    o_ref = refs[4]
    width = out_ref.shape[1]
    o_ref[0] = out_ref[...]
    for part in range(4):
        o_ref[1 + part] = up_ref[:, part * width : (part + 1) * width]
        o_ref[5 + part] = down_ref[16 * part : 16 * part + 16, :]


def first_kernel(count, *refs):
    x_first, x_last, o_ref, first_ref, last_ref = refs[count:]
    for n in range(count):
        o_ref[n] = refs[n][...]
    first_ref[...] = x_first[:, 0]
    last_ref[...] = x_last[:, 0]


def join_kernel(head, *refs):
    o_ref = refs[-1]
    parts = [ref[...].astype(F32) for ref in refs[:-1]]
    tops = [p[:, head + 1 : head + 2] for p in parts]
    top = functools.reduce(jnp.maximum, tops)
    total = functools.reduce(
        jnp.add, [p[:, : head + 1] * jnp.exp(t - top) for p, t in zip(parts, tops)]
    )
    o_ref[:, :head] = total[:, :head].astype(o_ref.dtype)
    line = lax.broadcasted_iota(jnp.int32, parts[0][:, head:].shape, 1)
    o_ref[:, head:] = jnp.where(
        line == 0, total[:, head:], jnp.where(line == 1, top, 0.0)
    ).astype(o_ref.dtype)


def norm_kernel(sc, x_ref, top_ref, bot_ref, w_ref, gain_ref, normed_ref, resid_ref, pad):
    micro = pl.program_id(0)
    rows, cols = x_ref.shape[2], x_ref.shape[3]
    clear_edges(pad)
    cols_ok = valid_cols(sc, micro, cols)
    put_row(pad, 0, top_ref[0, 0].astype(F32), cols_ok * valid_row(sc, micro, -1))
    put_row(pad, rows + 1, bot_ref[0, 0].astype(F32), cols_ok * valid_row(sc, micro, rows))

    def fill(r, carry):
        put_row(pad, r + 1, x_ref[0, 0, r].astype(F32), cols_ok * valid_row(sc, micro, r))
        return carry

    lax.fori_loop(0, rows, fill, 0)
    gain = gain_ref[...]

    def one(r, carry):
        ok = cols_ok * valid_row(sc, micro, r)
        for g in range(pad.shape[0]):
            taps = tap_row(pad, w_ref, g * 128, g, r + 1, cols, 3, None, False)
            resid_ref[0, r, :, g * 128 : (g + 1) * 128] = (
                taps + pad[g, r + 1, EDGE : EDGE + cols, :]
            ) * ok
        return carry

    lax.fori_loop(0, rows, one, 0, unroll=2)
    for r in range(0, rows, 2):
        unit, _ = unit_rows(resid_ref[0, r : r + 2].reshape(2 * cols, resid_ref.shape[3]))
        normed_ref[0, r : r + 2] = (unit * gain).astype(BF).reshape(2, cols, unit.shape[1])


def qkv_kernel(marks, lead, sc, n_ref, *refs):
    pieces = refs[: len(marks)]
    q_ref, k_ref, v_ref, sums_ref, first_ref, last_ref, whole, sem = refs[len(marks) :]
    micro = pl.program_id(0)
    rows, cols, width = n_ref.shape[1:]
    head = width // HEADS
    tokens = rows * cols

    @pl.when(micro == 0)
    def _():
        fetch(
            sc,
            pieces,
            marks,
            lead,
            lambda b, at: pltpu.make_async_copy(b, rows_at(whole, at), sem).start(),
        )
        pltpu.make_async_copy(whole, whole, sem).wait()

    normed = n_ref[0].reshape(tokens, width)
    q_ref[0] = dot(normed, whole[:, :width]).astype(BF)
    k = dot(normed, whole[:, width : 2 * width]).astype(BF)
    k_ref[0] = k
    v = dot(normed, whole[:, 2 * width :]).astype(BF)
    v_ref[0] = v.reshape(rows, cols, width)
    pack_rim(first_ref, [v[r * cols : (r + 1) * cols] for r in range(RIM)])
    pack_rim(last_ref, [v[(rows - 1 - r) * cols : (rows - r) * cols] for r in range(RIM)])
    ok = valid_rows(sc, micro, 0, rows, cols)
    keys = jnp.where(ok > 0, k.astype(F32), masked_low)
    top = jnp.max(keys, axis=0, keepdims=True)
    ew = jnp.exp(keys - top) * ok
    total = jnp.sum(ew, axis=0, keepdims=True)
    low = ew.astype(BF)
    half = 4 * head
    for b in range(width // half):
        full = dot_tn(v[:, b * half : (b + 1) * half], low[:, b * half : (b + 1) * half])
        sums_ref[0, :head, b * half : (b + 1) * half] = diagonal_blocks(full, head).astype(BF)
    line = lax.broadcasted_iota(jnp.int32, (16, width), 0)
    sums_ref[0, head:, :] = jnp.where(line == 0, total, jnp.where(line == 1, top, 0.0)).astype(BF)


def fill_rimmed(pad, source, rows, top_ref, bot_ref):
    clear_edges(pad)

    def fill(r, carry):
        put_row(pad, RIM + r, source(r).astype(F32))
        return carry

    lax.fori_loop(0, rows, fill, 0)
    put_rims(pad, top_ref, bot_ref, rows)


WINDOWS = ((0, 0, 3), (1, 0, 5), (2, 0, 7), (2, 128, 7))


def window_kernel(v_ref, *refs):
    weights, (o_ref, pad) = refs[:3], refs[3:]
    rows, cols = o_ref.shape[1], o_ref.shape[2]
    clear_edges(pad)

    def fill(r, carry):
        put_row(pad, r, v_ref[0, r].astype(F32))
        return carry

    lax.fori_loop(0, rows, fill, 0)
    for r in range(rows):
        for g, (which, lanes, size) in enumerate(WINDOWS):
            reach = size // 2
            lines = range(max(0, reach - r), min(size, rows + reach - r))
            o_ref[0, r, :, g * 128 : (g + 1) * 128] = tap_row(
                pad, weights[which], lanes, g, r, cols, size, lines, False
            )


def window_rim_kernel(part_ref, top_ref, bot_ref, *refs):
    weights, (o_ref, pad) = refs[:3], refs[3:]
    rows, cols = 2 * RIM, part_ref.shape[2]
    clear_edges(pad)
    put_rims(pad, top_ref, bot_ref, 0)
    last = part_ref.shape[1]
    for r in range(RIM):
        for row, centre in ((r, RIM + r), (last - 1 - r, RIM - 1 - r)):
            for g, (which, lanes, size) in enumerate(WINDOWS):
                reach = size // 2
                if row < RIM:
                    lines = range(0, reach - r)
                else:
                    lines = range(reach + 1 + r, size)
                part = part_ref[0, row, :, g * 128 : (g + 1) * 128]
                if lines:
                    part = part + tap_row(
                        pad, weights[which], lanes, g, centre, cols, size, lines, False
                    )
                o_ref[0, row, :, g * 128 : (g + 1) * 128] = part
    for row in range(RIM, last - RIM):
        o_ref[0, row] = part_ref[0, row]


def main_kernel(
    marks, count, lead, sc, q_ref, conv_ref, resid_ref, cot_ref, gain_ref, *refs
):
    parts, refs = refs[:count], refs[count:]
    pieces = refs[: len(marks)]
    (
        sums_ref,
        out_ref,
        act_ref,
        gh_ref,
        n2_ref,
        att_ref,
        gffn_ref,
        gproj_ref,
        gconv_ref,
        gq_ref,
        gm_ref,
        gkv_ref,
        first_ref,
        last_ref,
        ggain_ref,
        w_out,
        w_up,
        w_down,
        kvn,
        gacc,
        sem,
        up_sem,
        down_sem,
    ) = refs[len(marks) :]
    micro, tile = pl.program_id(0), pl.program_id(1)
    tokens, width = q_ref.shape[1], q_ref.shape[2]
    cols = 64
    rows = tokens // cols
    head = width // HEADS
    half = 4 * head
    scale = head**-0.5
    groups, step = w_up.shape[0], w_up.shape[2]
    per_group = w_down.shape[0] // groups

    @pl.when((micro == 0) & (tile == 0))
    def _():
        groups = w_up.shape[0]

        def to_out(b, at):
            pltpu.make_async_copy(b.at[0], rows_at(w_out, at), sem).start()

        def to_up(b, at):
            target = w_up.at[:, pl.ds(pl.multiple_of(at * 16, 16), 16), :]
            pltpu.make_async_copy(b.at[1 : 1 + groups], target, up_sem).start()

        def to_down(b, at):
            pltpu.make_async_copy(b.at[1 + groups :], w_down.at[at], down_sem).start()

        for copy in (to_out, to_up, to_down):
            fetch(sc, pieces, marks, lead, copy)
        ggain_ref[...] = jnp.zeros_like(ggain_ref)

    @pl.when(tile == 0)
    def _():
        join_kernel(head, *parts, sums_ref)
        normal = sums_ref[0, :head] / sums_ref[0, head : head + 1] * scale
        for b in range(width // half):
            kvn[b] = block_diagonal(normal[:, b * half : (b + 1) * half], head).astype(BF)
        gacc[...] = jnp.zeros_like(gacc)

    ok = valid_rows(sc, micro, tile * rows, rows, cols)
    q = q_ref[0]
    qf = q.astype(F32)
    conv = conv_ref[0]
    factor = jnp.concatenate(
        [dot_nt(q[:, b * half : (b + 1) * half], kvn[b]) for b in range(width // half)], axis=1
    )
    att = (factor + qf * conv).astype(BF)
    att_ref[0] = att

    @pl.when((micro == 0) & (tile == 0))
    def _():
        pltpu.make_async_copy(w_out, w_out, sem).wait()

    middle = resid_ref[0] + dot(att, w_out[...])
    unit, inverse = unit_rows(middle)
    gain = gain_ref[...]
    n2 = (unit * gain).astype(BF)
    n2_ref[0] = n2
    g_top = cot_ref[0].astype(F32) * ok
    g_ffn = g_top.astype(BF)
    gffn_ref[0] = g_ffn

    @pl.when((micro == 0) & (tile == 0))
    def _():
        pltpu.make_async_copy(w_up, w_up, up_sem).wait()
        pltpu.make_async_copy(w_down, w_down, down_sem).wait()

    ffn = jnp.zeros((tokens, width), F32)
    back = jnp.zeros((tokens, width), F32)
    for group in range(groups):
        c = group * step
        up = w_up[group]
        down = w_down[group * per_group : (group + 1) * per_group].reshape(step, width)
        hidden = dot(n2, up)
        cdf = 0.5 * (1.0 + lax.erf(hidden * (1.0 / math.sqrt(2.0))))
        act = (hidden * cdf).astype(BF)
        slope = cdf + hidden * jnp.exp(-0.5 * hidden * hidden) * (1.0 / math.sqrt(2.0 * math.pi))
        act_ref[0, :, c : c + step] = act
        ffn = ffn + dot(act, down)
        g_hidden = (dot_nt(g_ffn, down) * slope).astype(BF)
        gh_ref[0, :, c : c + step] = g_hidden
        back = back + dot_nt(g_hidden, up)
    out_ref[0] = ((middle + ffn) * ok).astype(BF)
    ggain_ref[...] += jnp.sum(back * unit, axis=0, keepdims=True)
    g_middle = g_top + norm_back(back, unit, inverse, gain)
    gm_ref[0] = g_middle
    g_proj = g_middle.astype(BF)
    gproj_ref[0] = g_proj
    g_att = dot_nt(g_proj, w_out[...])
    g_conv = g_att * qf
    gconv_ref[0] = g_conv

    @pl.when(tile == 0)
    def _():
        pack_rim(first_ref, [g_conv[r * cols : (r + 1) * cols] for r in range(RIM)])

    @pl.when(tile == pl.num_programs(1) - 1)
    def _():
        pack_rim(last_ref, [g_conv[(rows - 1 - r) * cols : (rows - r) * cols] for r in range(RIM)])

    low = g_att.astype(BF)
    for b in range(width // half):
        lanes = slice(b * half, (b + 1) * half)
        gq_ref[0, :, lanes] = (
            g_att[:, lanes] * conv[:, lanes] + dot(low[:, lanes], kvn[b])
        ).astype(BF)
        gacc[b] += dot_tn(low[:, lanes], q[:, lanes])

    @pl.when(tile == pl.num_programs(1) - 1)
    def _():
        for b in range(width // half):
            gkv_ref[0, :, b * half : (b + 1) * half] = (
                diagonal_blocks(gacc[b], head) * scale
            ).astype(BF)


def place_blocks(sc, lead, order, value, parts, put):
    place = sc.place() >> lead
    for slot, mask in enumerate(order):
        block = place ^ (mask >> lead)
        for part in range(parts):
            at = pl.multiple_of(block * (16 * parts) + 16 * part, 16)
            put(slot, part, value[pl.ds(at, 16), :].astype(BF))


def halves(keep_ref, send_ref, slot):
    half = keep_ref.shape[0]
    return (keep_ref if slot < half else send_ref), slot % half


def up_kernel(
    order, lead, sc, n2_ref, gh_ref, act_ref, gffn_ref, att_ref, gproj_ref, keep_ref, send_ref,
    acc, acc_down
):
    step, steps = pl.program_id(0), pl.num_programs(0)
    chunk = gh_ref.shape[1]

    def put(first):
        def one(slot, part, rows):
            ref, at = halves(keep_ref, send_ref, slot)
            ref[at, first + part] = rows

        return one

    @pl.when(step == 0)
    def _():
        acc[...] = dot_tn(att_ref[...], gproj_ref[...])
        place_blocks(sc, lead, order, acc, 1, put(0))

    acc[...] = dot_tn(n2_ref[...], gh_ref[...])
    place_blocks(sc, lead, order, acc, 1, put(1 + step))
    acc_down[pl.ds(pl.multiple_of(step * chunk, chunk), chunk), :] = dot_tn(
        act_ref[...], gffn_ref[...]
    )

    @pl.when(step == steps - 1)
    def _():
        place_blocks(sc, lead, order, acc_down, 4, put(1 + steps))


def taps_kernel(v_ref, top_ref, bot_ref, g_ref, o3, o5, o7, pad, sums):
    rows, cols = g_ref.shape[1], g_ref.shape[2]

    @pl.when(pl.program_id(0) == 0)
    def _():
        o3[...] = jnp.zeros_like(o3)
        o5[...] = jnp.zeros_like(o5)
        o7[...] = jnp.zeros_like(o7)

    fill_rimmed(pad, lambda r: v_ref[0, r], rows, top_ref, bot_ref)
    for g, (o, lanes, size) in enumerate(((o3, 0, 3), (o5, 0, 5), (o7, 0, 7), (o7, 128, 7))):
        tap_sums(pad, g_ref, o, sums, lanes, g, size, RIM)


def back_kernel(
    marks, order, count, lead, sc, n_ref, k_ref, v_ref, sums_ref, gc_ref, top_ref, bot_ref, gq_ref, resid_ref,
    gm_ref, gain_ref, w3, w5, w7, *refs
):
    gkv_parts, refs = refs[:count], refs[count:]
    pieces = refs[: len(marks)]
    (
        gu_ref, first_ref, last_ref, ggain_ref, keep_ref, send_ref,
        gqkv_ref, acc, whole, pad, gv_buf, sem,
    ) = refs[len(marks) :]
    micro = pl.program_id(0)
    rows, cols = gc_ref.shape[1], gc_ref.shape[2]
    tokens, width = k_ref.shape[1], k_ref.shape[2]
    head = width // HEADS
    half = 4 * head

    @pl.when(micro == 0)
    def _():
        fetch(
            sc,
            pieces,
            marks,
            lead,
            lambda b, at: pltpu.make_async_copy(b, rows_at(whole, at), sem).start(),
        )
        ggain_ref[...] = jnp.zeros_like(ggain_ref)

    fill_rimmed(pad, lambda r: gc_ref[0, r], rows, top_ref, bot_ref)

    def one(r, carry):
        for g, (w, lanes, size) in enumerate(((w3, 0, 3), (w5, 0, 5), (w7, 0, 7), (w7, 128, 7))):
            gv_buf[r, :, g * 128 : (g + 1) * 128] = tap_row(
                pad, w, lanes, g, r + RIM, cols, size, None, True
            )
        return carry

    lax.fori_loop(0, rows, one, 0)

    ok = valid_rows(sc, micro, 0, rows, cols)
    total = sums_ref[0, head : head + 1]
    top = sums_ref[0, head + 1 : head + 2]
    normal = sums_ref[0, :head] / total
    gkv = functools.reduce(jnp.add, [ref[0].astype(F32) for ref in gkv_parts])
    inner = jnp.sum(normal * gkv, axis=0, keepdims=True)
    probs = jnp.where(ok > 0, jnp.exp(k_ref[0].astype(F32) - top) / total, 0.0)
    low = probs.astype(BF)
    v = v_ref[0].reshape(tokens, width)
    gqkv_ref[:, :width] = gq_ref[0]
    for b in range(width // half):
        lanes = slice(b * half, (b + 1) * half)
        diag = block_diagonal(gkv[:, lanes], head).astype(BF)
        gk = probs[:, lanes] * (dot(v[:, lanes], diag) - inner[:, lanes])
        gqkv_ref[:, width + b * half : width + (b + 1) * half] = gk.astype(BF)
        gv = dot_nt(low[:, lanes], diag) + gv_buf[:, :, lanes].reshape(tokens, half)
        gqkv_ref[:, 2 * width + b * half : 2 * width + (b + 1) * half] = gv.astype(BF)

    @pl.when(micro == 0)
    def _():
        pltpu.make_async_copy(whole, whole, sem).wait()

    dy = dot_nt(gqkv_ref[...], whole[...])
    unit, inverse = unit_rows(resid_ref[0])
    ggain_ref[...] += jnp.sum(dy * unit, axis=0, keepdims=True)
    gu = (gm_ref[0] + norm_back(dy, unit, inverse, gain_ref[...])) * ok
    gu_ref[0] = gu.reshape(rows, cols, width)
    first_ref[0, 0] = gu[:cols].astype(BF)
    last_ref[0, 0] = gu[tokens - cols :].astype(BF)
    normed = n_ref[0].reshape(tokens, width)
    for c in range(0, 3 * width, width):
        part = dot_tn(normed, gqkv_ref[:, c : c + width])

        @pl.when(micro == 0)
        def _():
            acc[:, c : c + width] = part

        @pl.when(micro > 0)
        def _():
            acc[:, c : c + width] += part

    @pl.when(micro == pl.num_programs(0) - 1)
    def _():
        def put(slot, part, lines):
            ref, at = halves(keep_ref, send_ref, slot)
            ref[at] = lines

        place_blocks(sc, lead, order, acc, 1, put)


def place_seven(at, width):
    return at % 16, width + 256 * (at // 16)


def place_three(at):
    return 11 + at // 4, 128 * (at % 4)


def place_five(at, width):
    return 1 + at % 13, width + 768 + 128 * (at // 13)


def pos_grad_kernel(
    sc, x_ref, top_ref, bot_ref, gu_ref, o3, o5, o7, gain1, gain2, small_ref, pad, sums, pos, small
):
    micro = pl.program_id(0)
    rows, cols = x_ref.shape[2], x_ref.shape[3]
    width = pos.shape[1]
    clear_edges(pad)
    cols_ok = valid_cols(sc, micro, cols)

    @pl.when(micro == 0)
    def _():
        pos[...] = jnp.zeros_like(pos)

    def put(r, cells):
        put_row(pad, r + 1, cells.astype(F32), cols_ok * valid_row(sc, micro, r))

    def fill(r, carry):
        put(r, x_ref[0, 0, r])
        return carry

    lax.fori_loop(0, rows, fill, 0)
    put(-1, top_ref[0, 0])
    put(rows, bot_ref[0, 0])
    for g in range(pad.shape[0]):
        tap_sums(pad, gu_ref, pos, sums, g * 128, g, 3, 1)
    @pl.when(micro == pl.num_programs(0) - 1)
    def _():
        small[...] = jnp.zeros_like(small)
        small[:9, :width] = pos[...]
        small[9:10, :width] = gain1[...]
        small[10:11, :width] = gain2[...]
        for at in range(49):
            line, lane = place_seven(at, width)
            small[line : line + 1, lane : lane + 256] = o7[at : at + 1, :]
        for at in range(9):
            line, lane = place_three(at)
            small[line : line + 1, lane : lane + 128] = o3[at : at + 1, :]
        for at in range(25):
            line, lane = place_five(at, width)
            small[line : line + 1, lane : lane + 128] = o5[at : at + 1, :]
        small_ref[...] = small[...].astype(BF)


def start_grad_kernel(sc, gu_ref, top_ref, bot_ref, w_ref, o_ref, pad):
    micro = pl.program_id(0)
    rows, cols = gu_ref.shape[1], gu_ref.shape[2]
    clear_edges(pad)
    cols_ok = valid_cols(sc, micro, cols)

    def fill(r, carry):
        put_row(pad, 1 + r, gu_ref[0, r])
        return carry

    lax.fori_loop(0, rows, fill, 0)
    put_row(pad, 0, top_ref[0, 0].astype(F32))
    put_row(pad, rows + 1, bot_ref[0, 0].astype(F32))

    def one(r, carry):
        ok = cols_ok * valid_row(sc, micro, r)
        for g in range(pad.shape[0]):
            taps = tap_row(pad, w_ref, g * 128, g, r + 1, cols, 3, None, True)
            o_ref[0, 0, r, :, g * 128 : (g + 1) * 128] = (
                taps + pad[g, r + 1, EDGE : EDGE + cols, :]
            ) * ok
        return carry

    lax.fori_loop(0, rows, one, 0)


def add_kernel(parts, *refs):
    outs = refs[-parts:]
    ins = refs[:-parts]
    total = ins[0][...].astype(F32)
    for ref in ins[1:]:
        total = total + ref[...].astype(F32)
    for n in range(parts):
        outs[n][...] = total[n].astype(outs[n].dtype)


def sum_small(refs):
    sums = [ref[...].astype(F32) for ref in refs]
    while len(sums) > 1:
        sums = [a + b for a, b in zip(sums[::2], sums[1::2])]
    return sums[0]


def add_small_kernel(parts, count, *refs):
    ins, small, outs = refs[:count], refs[count:-parts], refs[-parts:]
    size = outs[0].shape[0] - 1
    for n in range(parts):
        for b in range(size):
            total = ins[0][n * size + b].astype(F32)
            for ref in ins[1:]:
                total = total + ref[n * size + b].astype(F32)
            outs[n][b] = total.astype(outs[n].dtype)
    if not small:
        small = [ref.at[parts * size] for ref in ins]
    low = sum_small(small).astype(BF)
    for n in range(parts):
        outs[n][size] = low.astype(outs[n].dtype)


def rest_kernel(*refs):
    out_ref, up_ref, down_ref = refs[-3:]
    total = refs[0][0]
    for ref in refs[1:-3]:
        total = total + ref[0].astype(F32)
    width = out_ref.shape[1]
    groups = up_ref.shape[1] // width
    out_ref[...] = total[0]
    for part in range(groups):
        up_ref[:, part * width : (part + 1) * width] = total[1 + part]
        down_ref[16 * part : 16 * part + 16, :] = total[1 + groups + part]


def small_kernel(s_ref, pos, three, five, seven, gain1, gain2):
    width = gain1.shape[1]
    for i in range(3):
        for j in range(3):
            at = 3 * i + j
            pos[i, j : j + 1, :] = s_ref[at : at + 1, :width]
            line, lane = place_three(at)
            three[i, j : j + 1, :] = s_ref[line : line + 1, lane : lane + 128]
    for i in range(5):
        for j in range(5):
            line, lane = place_five(5 * i + j, width)
            five[i, j : j + 1, :128] = s_ref[line : line + 1, lane : lane + 128]
            line, lane = place_seven(7 * i + j + 8, width)
            five[i, j : j + 1, 128:192] = s_ref[line : line + 1, lane : lane + 64]
    for i in range(7):
        for j in range(7):
            line, lane = place_seven(7 * i + j, width)
            seven[i, j : j + 1, :] = s_ref[line : line + 1, lane + 64 : lane + 256]
    gain1[...] = s_ref[9:10, :width]
    gain2[...] = s_ref[10:11, :width]


def ends_kernel(split, *refs):
    ins, qkv_ref, outs = refs[:4], refs[4], refs[5:]
    total = ins[0][0]
    for ref in ins[1:]:
        total = total + ref[0].astype(F32)
    qkv_ref[...] = total
    outs[-1][...] = sum_small([ref.at[1] for ref in ins])
    if split:
        small_kernel(outs[-1], *outs[:-1])


SMEM = pl.BlockSpec(memory_space=pltpu.SMEM)
VMEM = pl.BlockSpec(memory_space=pltpu.VMEM)
ANY = pl.BlockSpec(memory_space=pl.ANY)


def by_micro(shape):
    rest = tuple(shape[1:])
    return pl.BlockSpec((1,) + rest, lambda m: (m,) + (0,) * len(rest))


def whole_spec(shape):
    return pl.BlockSpec(tuple(shape), lambda *_: (0,) * len(shape))


def shaped(shape, dtype):
    return jax.ShapeDtypeStruct(tuple(shape), dtype)


def call(
    kernel, name, grid, ins, outs, scratch, micros_long, deps=(), alias=None, carry=(), rows_here=8,
    limit=None
):
    nbytes = sum(a.size * a.dtype.itemsize for _, a in ins)
    nbytes += sum(math.prod(s) * jnp.dtype(d).itemsize for _, s, d in outs)
    first, last = len(ins), len(ins) + len(deps) + len(carry)
    results = last + len(outs)

    def body(*refs):
        if ins and ins[0][0] is SMEM:
            refs = (Here(refs[0], rows_here),) + refs[1:]
        kernel(*refs[:first], *refs[last:results], *refs[results + len(carry) :])

    alias = dict(alias or {})
    for n in range(len(carry)):
        alias[first + len(deps) + n] = len(outs) + n
    return pl.pallas_call(
        body,
        name=name,
        grid=grid,
        in_specs=[s for s, _ in ins] + [ANY] * (len(deps) + len(carry)),
        out_specs=[s for s, _, _ in outs] + [ANY] * len(carry),
        out_shape=[shaped(s, d) for _, s, d in outs] + [shaped(c.shape, c.dtype) for c in carry],
        scratch_shapes=scratch,
        input_output_aliases=alias,
        cost_estimate=pl.CostEstimate(
            flops=int(micros_long * 1.15e9), bytes_accessed=int(nbytes), transcendentals=0
        ),
        compiler_params=pltpu.CompilerParams(
            vmem_limit_bytes=(limit or VMEM_MIB) * MIB, dimension_semantics=("arbitrary",) * len(grid)
        ),
    )(*[a for _, a in ins], *deps, *carry)


def gate_kernel(*refs):
    pass


def gate(values, deps):
    return call(gate_kernel, "gate", (), [], [], [], 0, deps=deps, carry=values)


def add_parts(arrays, parts, deps=(), carry=()):
    n, block = arrays[0].shape[1], tuple(arrays[0].shape[2:])
    rest = (0,) * len(block)
    return call(
        functools.partial(add_kernel, parts),
        "add_parts",
        (n,),
        [(pl.BlockSpec((parts, 1) + block, lambda i: (0, i) + rest), a) for a in arrays],
        [
            (pl.BlockSpec((1,) + block, lambda i: (i,) + rest), (n,) + block, F32 if p == 0 else BF)
            for p in range(parts)
        ],
        [],
        2,
        deps,
        carry=carry,
    )


def add_small(arrays, small, parts, deps=()):
    blocks, rows, lanes = arrays[0].shape
    shape = ((blocks if small else blocks - 1) // parts + 1, rows, lanes)
    every = list(arrays) + list(small)
    return call(
        functools.partial(add_small_kernel, parts, len(arrays)),
        "add_small",
        (1,),
        [(whole_spec(a.shape), a) for a in every],
        [(whole_spec(shape), shape, F32 if p == 0 else BF) for p in range(parts)],
        [],
        0,
        deps,
    )


def local(
    images,
    cotangent,
    extent,
    w_qkv,
    w_out,
    w_up,
    w_down,
    pos_weight,
    win_three,
    win_five,
    win_seven,
    gain_one,
    gain_two,
):
    micros, _, rows, cols, width = images.shape
    head = width // HEADS
    hidden = w_up.shape[1]
    tokens = rows * cols
    me = positions()
    lead_masks, first, second, third = plan(w_up.shape[0])
    lead = len(lead_masks)
    stages = (first, second, third)
    sc = (SMEM, extent)
    n5 = 128
    gain1, gain2 = gain_one.reshape(1, width), gain_two.reshape(1, width)
    pad_rim = pltpu.VMEM((width // 128, rows + 2 * RIM, cols + 2 * EDGE, 128), F32)
    pad_one = pltpu.VMEM((width // 128, rows + 2, cols + 2 * EDGE, 128), F32)

    flat = (micros, tokens, width)
    map_shape = (micros, rows, cols, width)
    rim_shape = (micros, cols, rim_lanes(width)[1])
    q_block = join_lead(w_qkv, lead_masks)
    joined = [join_lead(w, lead_masks) for w in (w_out, w_up, w_down)]
    block_shape = (1 + 2 * (hidden // width), 16, width)
    taps3, w3, w5, w7, r_block = call(
        prep_kernel,
        "prep",
        (1,),
        [
            (whole_spec(w.shape), w)
            for w in (pos_weight, win_three, win_five, win_seven, *joined)
        ],
        [
            (whole_spec(shape), shape, F32)
            for shape in ((9, width), (9, 128), (25, n5), (49, 256))
        ]
        + [(whole_spec(block_shape), block_shape, BF)],
        [],
        2,
    )
    windows = [(whole_spec(w.shape), w) for w in (w3, w5, w7)]

    def gather_second(own):
        return [own] + [flipped(own, m) for m in spans(second)[1:]]

    def gather_third(pieces):
        return pieces + [flipped(p, third[0]) for p in pieces]

    marks = spans(second)
    marks = marks + [m ^ third[0] for m in marks]
    r_marks = [[m ^ f for f in spans(first[::-1])] for m in marks]
    marks = [[m ^ f for f in spans(first)] for m in marks]

    def single(shape, micro):
        rest = tuple(shape[1:])
        return pl.BlockSpec((1,) + rest, lambda m: (micro,) + (0,) * len(rest))

    q_blocks = [q_block] + [flipped(q_block, m) for m in spans(first)[1:]]
    edge = (micros, 1, cols, width)

    def edge_spec(row):
        return pl.BlockSpec((micros, 1, 1, cols, width), lambda _: (0, 0, row, 0, 0))

    own_shape = (len(q_blocks),) + q_block.shape
    q_own, x_first, x_last = call(
        functools.partial(first_kernel, len(q_blocks)),
        "first",
        (1,),
        [(whole_spec(b.shape), b) for b in q_blocks]
        + [(edge_spec(0), images), (edge_spec(rows - 1), images)],
        [
            (whole_spec(own_shape), own_shape, BF),
            (whole_spec(edge), edge, BF),
            (whole_spec(edge), edge, BF),
        ],
        [],
        1,
        deps=[r_block],
    )
    x_top, x_bot = rims(x_first, x_last)
    q_pieces = gather_second(q_own)
    x_in = pl.BlockSpec((1, 1, rows, cols, width), lambda m: (m, 0, 0, 0, 0))
    r_own = r_block[None]
    for mask in first[::-1]:
        r_own = jnp.concatenate([r_own, flipped(r_own, mask)])
    normed, resid = call(
        norm_kernel,
        "norm",
        (micros,),
        [
            sc,
            (x_in, images),
            (by_micro(edge), x_top),
            (by_micro(edge), x_bot),
            (whole_spec(taps3.shape), taps3),
            (whole_spec(gain1.shape), gain1),
        ],
        [(by_micro(map_shape), map_shape, BF), (by_micro(map_shape), map_shape, F32)],
        [pad_one],
        8,
    )
    qkv_pieces = gather_third(q_pieces)
    r_pieces = list(gate([r_own] + [flipped(r_own, m) for m in second], [normed]))
    r_pieces = r_pieces + [flipped(r_pieces[1], second[1])]
    sums_shape = (micros, head + 16, width)
    q, k, v, sums, v_first, v_last = call(
        functools.partial(qkv_kernel, marks, lead),
        "qkv",
        (micros,),
        [sc, (by_micro(map_shape), normed)] + [(ANY, p) for p in qkv_pieces],
        [
            (by_micro(flat), flat, BF),
            (by_micro(flat), flat, BF),
            (by_micro(map_shape), map_shape, BF),
            (by_micro(sums_shape), sums_shape, BF),
            (by_micro(rim_shape), rim_shape, BF),
            (by_micro(rim_shape), rim_shape, BF),
        ],
        [pltpu.VMEM((width, 3 * width), BF), pltpu.SemaphoreType.DMA],
        6,
        deps=[r_own],
    )

    def join_strips(kernel, cells, stage, dtype, deps, carry=()):
        parts = [cells] + [strip_swap(cells, m) for m in spans(stage)[1:]]
        spec = whole_spec(cells.shape)
        return call(
            kernel,
            "join",
            (1,),
            [(spec, p) for p in parts],
            [(spec, cells.shape, dtype)],
            [],
            1,
            deps=deps,
            carry=carry,
        )

    near, far = strip_stages()
    v_top, v_bot = rims(v_first, v_last)
    (conv,) = call(
        window_kernel,
        "window",
        (micros,),
        [(by_micro(map_shape), v)] + windows,
        [(by_micro(map_shape), map_shape, F32)],
        [pltpu.VMEM((width // 128, rows, cols + 2 * EDGE, 128), F32)],
        6,
    )
    join = functools.partial(join_kernel, head)
    (sums,) = join_strips(join, sums, near, BF, [v_top, v_bot, conv])
    (conv,) = call(
        window_rim_kernel,
        "window_rim",
        (micros,),
        [
            (by_micro(map_shape), conv),
            (by_micro(rim_shape), v_top),
            (by_micro(rim_shape), v_bot),
        ]
        + windows,
        [(by_micro(map_shape), map_shape, F32)],
        [pltpu.VMEM((width // 128, 2 * RIM, cols + 2 * EDGE, 128), F32)],
        3,
        deps=[sums],
    )
    r_pieces = list(gate(r_pieces, [sums]))
    sums_got = [strip_swap(sums, m) for m in spans(far)[1:]]
    rest_pieces = gather_third(r_pieces)

    tile_rows = rows
    tile = tile_rows * cols
    tiles = rows // tile_rows

    def tiled(lanes):
        return pl.BlockSpec((1, tile, lanes), lambda m, t: (m, t, 0))

    def per_micro(shape):
        return pl.BlockSpec((1,) + tuple(shape[1:]), lambda m, t: (m,) + (0,) * (len(shape) - 1))

    wide = (micros, tokens, hidden)
    gkv_shape = (micros, head, width)
    outs = call(
        functools.partial(main_kernel, r_marks, 1 + len(sums_got), lead),
        "main",
        (micros, tiles),
        [
            sc,
            (tiled(width), q),
            (tiled(width), conv.reshape(flat)),
            (tiled(width), resid.reshape(flat)),
            (tiled(width), cotangent.reshape(flat)),
            (whole_spec(gain2.shape), gain2),
        ]
        + [(per_micro(sums_shape), a) for a in [sums] + sums_got]
        + [(ANY, p) for p in rest_pieces],
        [
            (per_micro(sums_shape), sums_shape, F32),
            (tiled(width), flat, BF),
            (tiled(hidden), wide, BF),
            (tiled(hidden), wide, BF),
            (tiled(width), flat, BF),
            (tiled(width), flat, BF),
            (tiled(width), flat, BF),
            (tiled(width), flat, BF),
            (tiled(width), flat, F32),
            (tiled(width), flat, BF),
            (tiled(width), flat, F32),
            (per_micro(gkv_shape), gkv_shape, BF),
            (per_micro(rim_shape), rim_shape, BF),
            (per_micro(rim_shape), rim_shape, BF),
            (whole_spec((1, width)), (1, width), F32),
        ],
        [
            pltpu.VMEM((width, width), BF),
            pltpu.VMEM((hidden // width, width, width), BF),
            pltpu.VMEM((width // 16, 4, 16, width), BF),
            pltpu.VMEM((width // (4 * head), 4 * head, 4 * head), BF),
            pltpu.VMEM((width // (4 * head), 4 * head, 4 * head), F32),
            pltpu.SemaphoreType.DMA,
            pltpu.SemaphoreType.DMA,
            pltpu.SemaphoreType.DMA,
        ],
        24,
    )
    sums, out, act, g_hidden, n2, att, g_ffn, g_proj, g_conv, gq, g_middle, gkv = outs[:12]
    gc_first, gc_last, ggain2 = outs[12:]
    g_conv = g_conv.reshape(map_shape)
    gc_top, gc_bot = rims(gc_first, gc_last)

    first, second = sum_stages(first, second)
    marked = [0]
    for stage in (first, second, third):
        marked = [o ^ m for m in spans(stage) for o in marked]
    slots = len(marked) // 2

    def flat2(a):
        return a.reshape(-1, a.shape[-1])

    def staged(block, parts):
        return block.reshape((parts, block.shape[0] // parts) + block.shape[1:])

    half_shape = (slots,) + block_shape
    ops = [flat2(a) for a in (n2, g_hidden, act, g_ffn, att, g_proj)]
    chunk = 512

    def columns(a):
        return pl.BlockSpec((a.shape[0], chunk), lambda c: (0, c))

    keep, send = call(
        functools.partial(up_kernel, marked, lead),
        "mlp_grads",
        (hidden // chunk,),
        [sc]
        + [
            (columns(a) if a.shape[1] == hidden else whole_spec(a.shape), a)
            for a in ops
        ],
        [(whole_spec(half_shape), half_shape, BF)] * 2,
        [pltpu.VMEM((width, chunk), F32), pltpu.VMEM((hidden, width), F32)],
        12,
    )
    gkv_parts = [gkv] + [strip_swap(gkv, m) for m in spans(near)[1:]]
    gkv = functools.reduce(jnp.add, [p.astype(F32) for p in gkv_parts]).astype(BF)
    (send,) = gate([send], [gkv, gc_top, gc_bot, keep])
    got = flipped(send, third[0])
    gkv_got = [strip_swap(gkv, m) for m in spans(far)[1:]]
    o3, o5, o7 = call(
        taps_kernel,
        "window_grads",
        (micros,),
        [
            (by_micro(map_shape), v),
            (by_micro(rim_shape), v_top),
            (by_micro(rim_shape), v_bot),
            (by_micro(map_shape), g_conv),
        ],
        [
            (whole_spec((9, 128)), (9, 128), F32),
            (whole_spec((25, 128)), (25, 128), F32),
            (whole_spec((49, 256)), (49, 256), F32),
        ],
        [pad_rim, pltpu.VMEM((49, 8, 128), F32)],
        6,
        deps=[send],
    )
    parts2, parts1 = len(spans(second)), len(spans(first))
    rest = add_parts([staged(keep, parts2), staged(got, parts2)], parts2, [o3] + gkv_got)
    rest_got = [flipped(o, m) for o, m in zip(rest[1:], spans(second)[1:])]

    half_shape = (slots, 16, 3 * width)
    g_u, gu_first, gu_last, ggain1, keep, send = call(
        functools.partial(back_kernel, marks, marked, 1 + len(gkv_got), lead),
        "back",
        (micros,),
        [
            sc,
            (by_micro(map_shape), normed),
            (by_micro(flat), k),
            (by_micro(map_shape), v),
            (by_micro(sums_shape), sums),
            (by_micro(map_shape), g_conv),
            (by_micro(rim_shape), gc_top),
            (by_micro(rim_shape), gc_bot),
            (by_micro(flat), gq),
            (by_micro(flat), resid.reshape(flat)),
            (by_micro(flat), g_middle),
            (whole_spec(gain1.shape), gain1),
        ]
        + windows
        + [(by_micro(gkv_shape), g) for g in [gkv] + gkv_got]
        + [(ANY, p) for p in qkv_pieces],
        [
            (by_micro(map_shape), map_shape, F32),
            (by_micro(edge), edge, BF),
            (by_micro(edge), edge, BF),
            (whole_spec((1, width)), (1, width), F32),
            (whole_spec(half_shape), half_shape, BF),
            (whole_spec(half_shape), half_shape, BF),
        ],
        [
            pltpu.VMEM((tokens, 3 * width), BF),
            pltpu.VMEM((width, 3 * width), F32),
            pltpu.VMEM((width, 3 * width), BF),
            pad_rim,
            pltpu.VMEM((rows, cols, width), F32),
            pltpu.SemaphoreType.DMA,
        ],
        15,
        deps=[rest[0]],
    )
    gu_top, gu_bot = rims(gu_first, gu_last)
    small_shape = (16, 3 * width)
    (small,) = call(
        pos_grad_kernel,
        "pos_grad",
        (micros,),
        [
            sc,
            (x_in, images),
            (by_micro(x_top.shape), x_top),
            (by_micro(x_bot.shape), x_bot),
            (by_micro(map_shape), g_u),
        ]
        + [(whole_spec(a.shape), a) for a in (o3, o5, o7, ggain1, ggain2)],
        [(whole_spec(small_shape), small_shape, BF)],
        [
            pad_one,
            pltpu.VMEM((9, 8, 128), F32),
            pltpu.VMEM((9, width), F32),
            pltpu.VMEM(small_shape, F32),
        ],
        1,
    )
    send, small_send = gate([send, small], rest_got + [gu_top, gu_bot])
    got, small_got = flipped(send, third[0]), flipped(small_send, third[0])
    rest = add_parts([staged(p, parts1) for p in [rest[0]] + rest_got], parts1)
    own = add_small([keep, got], [small_send, small_got], parts2, [rest[0]])
    own_got = [flipped(o, m) for o, m in zip(own[1:], spans(second)[1:])]
    rest_got = [flipped(o, m) for o, m in zip(rest[1:], spans(first)[1:])]
    (grad_in,) = call(
        start_grad_kernel,
        "input_grad",
        (micros,),
        [
            sc,
            (by_micro(map_shape), g_u),
            (by_micro(gu_top.shape), gu_top),
            (by_micro(gu_bot.shape), gu_bot),
            (whole_spec(taps3.shape), taps3),
        ],
        [(x_in, (micros, 1, rows, cols, width), F32)],
        [pad_one],
        3,
        deps=[own[0]],
    )
    own = [own[0]] + own_got
    own = add_small(own, [], parts1, [grad_in])
    own_got = [flipped(o, m) for o, m in zip(own[1:], spans(first)[1:])]
    own = [own[0]] + own_got
    rest = [rest[0]] + rest_got

    def lead_sum(total):
        for mask in reversed(lead_masks):
            size = total.shape[0] // 2
            low, high = total[:size], total[size:]
            bit = (me & mask) != 0
            kept, sent = jnp.where(bit, high, low), jnp.where(bit, low, high)
            total = kept + flipped(sent, mask)
        return total

    def call_whole(kernel, name, arrays, shapes, deps=()):
        return call(
            kernel,
            name,
            (1,),
            [(VMEM if n else whole_spec(a.shape), a) for n, a in enumerate(arrays)],
            [(whole_spec(shape), shape, F32) for shape in shapes],
            [],
            1,
            deps=deps,
            limit=16,
        )

    rest_shapes = [(16, width), (16, hidden), (64, width)]
    grad_out, grad_up, grad_down = call_whole(rest_kernel, "rest_sum", rest, rest_shapes, own[:1])
    small_shapes = [w.shape for w in (pos_weight, win_three, win_five, win_seven)]
    small_shapes = small_shapes + [gain1.shape] * 2
    if lead_masks:
        grad_out, grad_up, grad_down = (lead_sum(g) for g in (grad_out, grad_up, grad_down))
        grad_qkv, small = call_whole(
            functools.partial(ends_kernel, False), "last_sum", own, [small_shape] * 2
        )
        grad_qkv = lead_sum(grad_qkv)
        low = small.astype(BF)
        got = [low.astype(F32)] + [flipped(low, m).astype(F32) for m in spans(lead_masks)[1:]]
        while len(got) > 1:
            got = [a + b for a, b in zip(got[::2], got[1::2])]
        smalls = call_whole(small_kernel, "small_grads", got, small_shapes)
    else:
        grad_qkv, *smalls, _ = call_whole(
            functools.partial(ends_kernel, True),
            "last_sum",
            own,
            [small_shape] + small_shapes + [small_shape],
        )
    g_pos, g_three, g_five, g_seven, ggain1, ggain2 = smalls
    return (
        out.reshape(micros, 1, rows, cols, width),
        grad_in,
        grad_qkv,
        grad_out,
        grad_up,
        grad_down,
        g_pos,
        g_three,
        g_five,
        g_seven,
        ggain1.reshape(width),
        ggain2.reshape(width),
    )


def solution(mesh):
    in_specs = (
        P(None, "img", "strip", None, None),
        P(None, "img", "strip", None, None),
        P(None, "img", None),
        P(("img", "strip"), None),
        P(("img", "strip"), None),
        P(("img", "strip"), None),
        P(("img", "strip"), None),
        P(),
        P(),
        P(),
        P(),
        P(),
        P(),
    )
    out_specs = (
        P(None, "img", "strip", None, None),
        P(None, "img", "strip", None, None),
        P(("img", "strip"), None),
        P(("img", "strip"), None),
        P(("img", "strip"), None),
        P(("img", "strip"), None),
        P(),
        P(),
        P(),
        P(),
        P(),
        P(),
    )
    return jax.shard_map(local, mesh=mesh, in_specs=in_specs, out_specs=out_specs, check_vma=False)
```

```python
import functools
import math

import jax
import jax.numpy as jnp
from jax import lax
from jax.experimental import pallas as pl
from jax.experimental.pallas import tpu as pltpu
from jax.sharding import PartitionSpec as P

HEADS = 8
norm_eps = 1e-06
masked_low = -1e30
RIM = 3
EDGE = 8
BF = jnp.bfloat16
F32 = jnp.float32
MIB = 2**20
VMEM_MIB = 63


def positions():
    return lax.axis_index("img") * lax.axis_size("strip") + lax.axis_index("strip")


def flipped(cells, mask):
    count = lax.axis_size("img") * lax.axis_size("strip")
    return lax.ppermute(cells, ("img", "strip"), [(i, i ^ mask) for i in range(count)])


def plan(shard_rows):
    strip_bits = int(math.log2(lax.axis_size("strip")))
    img_bits = int(math.log2(lax.axis_size("img")))
    lead = 0
    while (shard_rows << lead) < 16:
        lead += 1
    free = [1 << b for b in range(lead, strip_bits)]
    img = [1 << (strip_bits + b) for b in range(1, img_bits)]
    if len(free) > 2:
        first, second = [free[0], free[2]], [free[1]] + img
    else:
        first, second = free, img
    return [1 << b for b in range(lead)], first, second, [1 << strip_bits]


def sum_stages(first, second):
    masks = sorted(first + second)
    return (masks[1:3], [masks[0]] + masks[3:]) if len(masks) == 4 else (first, second)


def spans(masks):
    out = [0]
    for mask in masks:
        out = out + [o ^ mask for o in out]
    return out


def join_lead(shard, lead):
    me = positions()
    for mask in lead:
        other = flipped(shard, mask)
        shard = jnp.where(
            (me & mask) != 0, jnp.concatenate([other, shard]), jnp.concatenate([shard, other])
        )
    return shard


def strip_swap(cells, mask):
    count = lax.axis_size("strip")
    return lax.ppermute(cells, "strip", [(i, i ^ mask) for i in range(count)])


def strip_stages():
    masks = [1 << b for b in range(int(math.log2(lax.axis_size("strip"))))]
    return [masks[:1] + masks[2:3], masks[1:2] + masks[3:]]


def rims(first, last):
    count = lax.axis_size("strip")
    above = lax.ppermute(last, "strip", [(i, i + 1) for i in range(count - 1)])
    below = lax.ppermute(first, "strip", [(i + 1, i) for i in range(count - 1)])
    return above, below


class Here:
    def __init__(self, extent_ref, strip_rows):
        self.extent = extent_ref
        self.strip_rows = strip_rows

    def place(self):
        return positions()

    def first_row(self):
        return lax.axis_index("strip") * self.strip_rows

    def valid(self, micro, which):
        return self.extent[micro, 0, which]


def dot(a, b):
    return jnp.dot(a, b, preferred_element_type=F32)


def dot_nt(a, b):
    return lax.dot_general(a, b, (((1,), (1,)), ((), ())), preferred_element_type=F32)


def dot_tn(a, b):
    return lax.dot_general(a, b, (((0,), (0,)), ((), ())), preferred_element_type=F32)


def valid_rows(sc, micro, first_row, rows, cols):
    n = rows * cols
    shift = int(math.log2(cols))
    flat = lax.broadcasted_iota(jnp.int32, (n, 1), 0)
    row = lax.shift_right_logical(flat, shift) + (sc.first_row() + first_row)
    ok = (row < sc.valid(micro, 0)) & ((flat & (cols - 1)) < sc.valid(micro, 1))
    return jnp.where(ok, 1.0, 0.0).astype(F32)


def valid_cols(sc, micro, cols):
    col = lax.broadcasted_iota(jnp.int32, (cols, 128), 0)
    return jnp.where(col < sc.valid(micro, 1), 1.0, 0.0).astype(F32)


def valid_row(sc, micro, row):
    at = sc.first_row() + row
    return jnp.where((at >= 0) & (at < sc.valid(micro, 0)), 1.0, 0.0).astype(F32)


def unit_rows(fields):
    average = jnp.mean(fields, axis=-1, keepdims=True)
    centred = fields - average
    inverse = lax.rsqrt(jnp.mean(centred * centred, axis=-1, keepdims=True) + norm_eps)
    return centred * inverse, inverse


def norm_back(dy, unit, inverse, gain):
    dyg = dy * gain
    first = jnp.mean(dyg, axis=-1, keepdims=True)
    second = jnp.mean(dyg * unit, axis=-1, keepdims=True)
    return inverse * (dyg - first - unit * second)


def clear_edges(pad):
    groups, rows, cols, _ = pad.shape
    zeros = jnp.zeros((rows, EDGE, 128), F32)
    for g in range(groups):
        pad[g, :, :EDGE, :] = zeros
        pad[g, :, cols - EDGE :, :] = zeros


def put_row(pad, row, cells, ok=None):
    for g in range(pad.shape[0]):
        part = cells[:, g * 128 : (g + 1) * 128]
        pad[g, row, EDGE : EDGE + cells.shape[0], :] = part if ok is None else part * ok


def rim_lanes(width):
    out, lane = [], 0
    for row in range(RIM):
        out.append((row, lane))
        lane += width - 128 * row
    return out, lane


def pack_rim(rim_ref, lines):
    spans_, _ = rim_lanes(lines[0].shape[1])
    for line, (group, lane) in zip(lines, spans_):
        part = line[:, 128 * group :]
        rim_ref[0, :, lane : lane + part.shape[1]] = part.astype(BF)


def put_rims(pad, top_ref, bot_ref, rows):
    width = 128 * pad.shape[0]
    cols = top_ref.shape[1]
    for near, (group, lane) in enumerate(rim_lanes(width)[0]):
        for ref, line in ((top_ref, RIM - 1 - near), (bot_ref, RIM + rows + near)):
            for g in range(group, pad.shape[0]):
                at = lane + 128 * (g - group)
                pad[g, line, EDGE : EDGE + cols, :] = ref[0, :, at : at + 128].astype(F32)


def tap_row(pad, w_ref, lanes, group, row, cols, size, lines, flip):
    reach = size // 2
    total = jnp.zeros((cols, 128), F32)
    for i in lines or range(size):
        for j in range(size):
            at = i * size + j
            if flip:
                at = size * size - 1 - at
            w = w_ref[at : at + 1, lanes : lanes + 128]
            total = total + w * pad[
                group, row + i - reach, EDGE + j - reach : EDGE + j - reach + cols, :
            ]
    return total


def tap_sums(pad, grad_ref, out_ref, sums, lanes, group, size, above):
    reach = size // 2
    rows, cols = grad_ref.shape[1], grad_ref.shape[2]
    taps = size * size
    sums[:taps] = jnp.zeros((taps, 8, 128), F32)

    def step(t, carry):
        for half in range(2):
            c = pl.multiple_of(t * 16 + half * 8, 8)
            grads = [
                grad_ref[0, r, pl.ds(c, 8), group * 128 : (group + 1) * 128].astype(F32)
                for r in range(rows)
            ]
            for j in range(size):
                part = [None] * size
                for line in range(rows + 2 * reach):
                    f = pad[group, line + above - reach, pl.ds(c + EDGE + j - reach, 8), :]
                    for i in range(size):
                        r = line - i
                        if 0 <= r < rows:
                            term = grads[r] * f
                            part[i] = term if part[i] is None else part[i] + term
                for i in range(size):
                    at = i * size + j
                    sums[at] += part[i]
        return carry

    lax.fori_loop(0, cols // 16, step, 0)
    for at in range(taps):
        out_ref[at : at + 1, lanes : lanes + 128] += jnp.sum(sums[at], axis=0, keepdims=True)


def block_diagonal(wide, head):
    lane = lax.broadcasted_iota(jnp.int32, wide.shape, 1) // head
    return jnp.concatenate(
        [jnp.where(lane == h, wide, 0.0) for h in range(wide.shape[1] // head)], axis=0
    )


def diagonal_blocks(full, head):
    lane = lax.broadcasted_iota(jnp.int32, (head, full.shape[1]), 1) // head
    total = jnp.zeros((head, full.shape[1]), F32)
    for h in range(full.shape[1] // head):
        total = total + jnp.where(lane == h, full[h * head : (h + 1) * head], 0.0)
    return total


def fetch(sc, pieces, marks, lead, copy):
    place = sc.place() >> lead
    for piece, mark in zip(pieces, marks):
        for k, mask in enumerate(mark):
            copy(piece.at[k], place ^ (mask >> lead))


def rows_at(whole, block):
    return whole.at[pl.ds(pl.multiple_of(block * 16, 16), 16), :]


def taps_prep(pos_ref, three_ref, five_ref, seven_ref, taps3, w3, w5, w7):
    for i in range(3):
        for j in range(3):
            taps3[3 * i + j : 3 * i + j + 1, :] = pos_ref[i, j : j + 1, :]
            w3[3 * i + j : 3 * i + j + 1, :] = three_ref[i, j : j + 1, :]
    for i in range(5):
        for j in range(5):
            w5[5 * i + j : 5 * i + j + 1, :] = five_ref[i, j : j + 1, :128]
    for i in range(7):
        for j in range(7):
            seven = seven_ref[i, j : j + 1, :]
            low = jnp.zeros((1, 64), F32)
            if 1 <= i <= 5 and 1 <= j <= 5:
                low = five_ref[i - 1, j - 1 : j, 128:192]
            w7[7 * i + j : 7 * i + j + 1, :] = jnp.concatenate([low, seven], axis=1)


def prep_kernel(pos_ref, three_ref, five_ref, seven_ref, out_ref, up_ref, down_ref, *refs):
    taps_prep(pos_ref, three_ref, five_ref, seven_ref, *refs[:4])
    o_ref = refs[4]
    width = out_ref.shape[1]
    o_ref[0] = out_ref[...]
    for part in range(4):
        o_ref[1 + part] = up_ref[:, part * width : (part + 1) * width]
        o_ref[5 + part] = down_ref[16 * part : 16 * part + 16, :]


def first_kernel(count, *refs):
    x_first, x_last, o_ref, first_ref, last_ref = refs[count:]
    for n in range(count):
        o_ref[n] = refs[n][...]
    first_ref[...] = x_first[:, 0]
    last_ref[...] = x_last[:, 0]


def join_kernel(head, *refs):
    o_ref = refs[-1]
    parts = [ref[...].astype(F32) for ref in refs[:-1]]
    tops = [p[:, head + 1 : head + 2] for p in parts]
    top = functools.reduce(jnp.maximum, tops)
    total = functools.reduce(
        jnp.add, [p[:, : head + 1] * jnp.exp(t - top) for p, t in zip(parts, tops)]
    )
    o_ref[:, :head] = total[:, :head].astype(o_ref.dtype)
    line = lax.broadcasted_iota(jnp.int32, parts[0][:, head:].shape, 1)
    o_ref[:, head:] = jnp.where(
        line == 0, total[:, head:], jnp.where(line == 1, top, 0.0)
    ).astype(o_ref.dtype)


def norm_kernel(sc, x_ref, top_ref, bot_ref, w_ref, gain_ref, normed_ref, resid_ref, pad):
    micro = pl.program_id(0)
    rows, cols = x_ref.shape[2], x_ref.shape[3]
    clear_edges(pad)
    cols_ok = valid_cols(sc, micro, cols)
    put_row(pad, 0, top_ref[0, 0].astype(F32), cols_ok * valid_row(sc, micro, -1))
    put_row(pad, rows + 1, bot_ref[0, 0].astype(F32), cols_ok * valid_row(sc, micro, rows))

    def fill(r, carry):
        put_row(pad, r + 1, x_ref[0, 0, r].astype(F32), cols_ok * valid_row(sc, micro, r))
        return carry

    lax.fori_loop(0, rows, fill, 0)
    gain = gain_ref[...]

    def one(r, carry):
        ok = cols_ok * valid_row(sc, micro, r)
        for g in range(pad.shape[0]):
            taps = tap_row(pad, w_ref, g * 128, g, r + 1, cols, 3, None, False)
            resid_ref[0, r, :, g * 128 : (g + 1) * 128] = (
                taps + pad[g, r + 1, EDGE : EDGE + cols, :]
            ) * ok
        return carry

    lax.fori_loop(0, rows, one, 0, unroll=2)
    for r in range(0, rows, 2):
        unit, _ = unit_rows(resid_ref[0, r : r + 2].reshape(2 * cols, resid_ref.shape[3]))
        normed_ref[0, r : r + 2] = (unit * gain).astype(BF).reshape(2, cols, unit.shape[1])


def qkv_kernel(marks, lead, sc, n_ref, *refs):
    pieces = refs[: len(marks)]
    q_ref, k_ref, v_ref, sums_ref, first_ref, last_ref, whole, sem = refs[len(marks) :]
    micro = pl.program_id(0)
    rows, cols, width = n_ref.shape[1:]
    head = width // HEADS
    tokens = rows * cols

    @pl.when(micro == 0)
    def _():
        fetch(
            sc,
            pieces,
            marks,
            lead,
            lambda b, at: pltpu.make_async_copy(b, rows_at(whole, at), sem).start(),
        )
        pltpu.make_async_copy(whole, whole, sem).wait()

    normed = n_ref[0].reshape(tokens, width)
    q_ref[0] = dot(normed, whole[:, :width]).astype(BF)
    k = dot(normed, whole[:, width : 2 * width]).astype(BF)
    k_ref[0] = k
    v = dot(normed, whole[:, 2 * width :]).astype(BF)
    v_ref[0] = v.reshape(rows, cols, width)
    pack_rim(first_ref, [v[r * cols : (r + 1) * cols] for r in range(RIM)])
    pack_rim(last_ref, [v[(rows - 1 - r) * cols : (rows - r) * cols] for r in range(RIM)])
    ok = valid_rows(sc, micro, 0, rows, cols)
    keys = jnp.where(ok > 0, k.astype(F32), masked_low)
    top = jnp.max(keys, axis=0, keepdims=True)
    ew = jnp.exp(keys - top) * ok
    total = jnp.sum(ew, axis=0, keepdims=True)
    low = ew.astype(BF)
    half = 4 * head
    for b in range(width // half):
        full = dot_tn(v[:, b * half : (b + 1) * half], low[:, b * half : (b + 1) * half])
        sums_ref[0, :head, b * half : (b + 1) * half] = diagonal_blocks(full, head).astype(BF)
    line = lax.broadcasted_iota(jnp.int32, (16, width), 0)
    sums_ref[0, head:, :] = jnp.where(line == 0, total, jnp.where(line == 1, top, 0.0)).astype(BF)


def fill_rimmed(pad, source, rows, top_ref, bot_ref):
    clear_edges(pad)

    def fill(r, carry):
        put_row(pad, RIM + r, source(r).astype(F32))
        return carry

    lax.fori_loop(0, rows, fill, 0)
    put_rims(pad, top_ref, bot_ref, rows)


WINDOWS = ((0, 0, 3), (1, 0, 5), (2, 0, 7), (2, 128, 7))


def window_kernel(v_ref, *refs):
    weights, (o_ref, pad) = refs[:3], refs[3:]
    rows, cols = o_ref.shape[1], o_ref.shape[2]
    clear_edges(pad)

    def fill(r, carry):
        put_row(pad, r, v_ref[0, r].astype(F32))
        return carry

    lax.fori_loop(0, rows, fill, 0)
    for r in range(rows):
        for g, (which, lanes, size) in enumerate(WINDOWS):
            reach = size // 2
            lines = range(max(0, reach - r), min(size, rows + reach - r))
            o_ref[0, r, :, g * 128 : (g + 1) * 128] = tap_row(
                pad, weights[which], lanes, g, r, cols, size, lines, False
            )


def window_rim_kernel(part_ref, top_ref, bot_ref, *refs):
    weights, (o_ref, pad) = refs[:3], refs[3:]
    rows, cols = 2 * RIM, part_ref.shape[2]
    clear_edges(pad)
    put_rims(pad, top_ref, bot_ref, 0)
    last = part_ref.shape[1]
    for r in range(RIM):
        for row, centre in ((r, RIM + r), (last - 1 - r, RIM - 1 - r)):
            for g, (which, lanes, size) in enumerate(WINDOWS):
                reach = size // 2
                if row < RIM:
                    lines = range(0, reach - r)
                else:
                    lines = range(reach + 1 + r, size)
                part = part_ref[0, row, :, g * 128 : (g + 1) * 128]
                if lines:
                    part = part + tap_row(
                        pad, weights[which], lanes, g, centre, cols, size, lines, False
                    )
                o_ref[0, row, :, g * 128 : (g + 1) * 128] = part
    for row in range(RIM, last - RIM):
        o_ref[0, row] = part_ref[0, row]


def main_kernel(
    marks, count, lead, sc, q_ref, conv_ref, resid_ref, cot_ref, gain_ref, *refs
):
    parts, refs = refs[:count], refs[count:]
    pieces = refs[: len(marks)]
    (
        sums_ref,
        out_ref,
        act_ref,
        gh_ref,
        n2_ref,
        att_ref,
        gffn_ref,
        gproj_ref,
        gconv_ref,
        gq_ref,
        gm_ref,
        gkv_ref,
        first_ref,
        last_ref,
        ggain_ref,
        w_out,
        w_up,
        w_down,
        kvn,
        gacc,
        sem,
        up_sem,
        down_sem,
    ) = refs[len(marks) :]
    micro, tile = pl.program_id(0), pl.program_id(1)
    tokens, width = q_ref.shape[1], q_ref.shape[2]
    cols = 64
    rows = tokens // cols
    head = width // HEADS
    half = 4 * head
    scale = head**-0.5
    groups, step = w_up.shape[0], w_up.shape[2]
    per_group = w_down.shape[0] // groups

    @pl.when((micro == 0) & (tile == 0))
    def _():
        groups = w_up.shape[0]

        def to_out(b, at):
            pltpu.make_async_copy(b.at[0], rows_at(w_out, at), sem).start()

        def to_up(b, at):
            target = w_up.at[:, pl.ds(pl.multiple_of(at * 16, 16), 16), :]
            pltpu.make_async_copy(b.at[1 : 1 + groups], target, up_sem).start()

        def to_down(b, at):
            pltpu.make_async_copy(b.at[1 + groups :], w_down.at[at], down_sem).start()

        for copy in (to_out, to_up, to_down):
            fetch(sc, pieces, marks, lead, copy)
        ggain_ref[...] = jnp.zeros_like(ggain_ref)

    @pl.when(tile == 0)
    def _():
        join_kernel(head, *parts, sums_ref)
        normal = sums_ref[0, :head] / sums_ref[0, head : head + 1] * scale
        for b in range(width // half):
            kvn[b] = block_diagonal(normal[:, b * half : (b + 1) * half], head).astype(BF)
        gacc[...] = jnp.zeros_like(gacc)

    ok = valid_rows(sc, micro, tile * rows, rows, cols)
    q = q_ref[0]
    qf = q.astype(F32)
    conv = conv_ref[0]
    factor = jnp.concatenate(
        [dot_nt(q[:, b * half : (b + 1) * half], kvn[b]) for b in range(width // half)], axis=1
    )
    att = (factor + qf * conv).astype(BF)
    att_ref[0] = att

    @pl.when((micro == 0) & (tile == 0))
    def _():
        pltpu.make_async_copy(w_out, w_out, sem).wait()

    middle = resid_ref[0] + dot(att, w_out[...])
    unit, inverse = unit_rows(middle)
    gain = gain_ref[...]
    n2 = (unit * gain).astype(BF)
    n2_ref[0] = n2
    g_top = cot_ref[0].astype(F32) * ok
    g_ffn = g_top.astype(BF)
    gffn_ref[0] = g_ffn

    @pl.when((micro == 0) & (tile == 0))
    def _():
        pltpu.make_async_copy(w_up, w_up, up_sem).wait()
        pltpu.make_async_copy(w_down, w_down, down_sem).wait()

    ffn = jnp.zeros((tokens, width), F32)
    back = jnp.zeros((tokens, width), F32)
    for group in range(groups):
        c = group * step
        up = w_up[group]
        down = w_down[group * per_group : (group + 1) * per_group].reshape(step, width)
        hidden = dot(n2, up)
        cdf = 0.5 * (1.0 + lax.erf(hidden * (1.0 / math.sqrt(2.0))))
        act = (hidden * cdf).astype(BF)
        slope = cdf + hidden * jnp.exp(-0.5 * hidden * hidden) * (1.0 / math.sqrt(2.0 * math.pi))
        act_ref[0, :, c : c + step] = act
        ffn = ffn + dot(act, down)
        g_hidden = (dot_nt(g_ffn, down) * slope).astype(BF)
        gh_ref[0, :, c : c + step] = g_hidden
        back = back + dot_nt(g_hidden, up)
    out_ref[0] = ((middle + ffn) * ok).astype(BF)
    ggain_ref[...] += jnp.sum(back * unit, axis=0, keepdims=True)
    g_middle = g_top + norm_back(back, unit, inverse, gain)
    gm_ref[0] = g_middle
    g_proj = g_middle.astype(BF)
    gproj_ref[0] = g_proj
    g_att = dot_nt(g_proj, w_out[...])
    g_conv = g_att * qf
    gconv_ref[0] = g_conv

    @pl.when(tile == 0)
    def _():
        pack_rim(first_ref, [g_conv[r * cols : (r + 1) * cols] for r in range(RIM)])

    @pl.when(tile == pl.num_programs(1) - 1)
    def _():
        pack_rim(last_ref, [g_conv[(rows - 1 - r) * cols : (rows - r) * cols] for r in range(RIM)])

    low = g_att.astype(BF)
    for b in range(width // half):
        lanes = slice(b * half, (b + 1) * half)
        gq_ref[0, :, lanes] = (
            g_att[:, lanes] * conv[:, lanes] + dot(low[:, lanes], kvn[b])
        ).astype(BF)
        gacc[b] += dot_tn(low[:, lanes], q[:, lanes])

    @pl.when(tile == pl.num_programs(1) - 1)
    def _():
        for b in range(width // half):
            gkv_ref[0, :, b * half : (b + 1) * half] = (
                diagonal_blocks(gacc[b], head) * scale
            ).astype(BF)


def place_blocks(sc, lead, order, value, parts, put):
    place = sc.place() >> lead
    for slot, mask in enumerate(order):
        block = place ^ (mask >> lead)
        for part in range(parts):
            at = pl.multiple_of(block * (16 * parts) + 16 * part, 16)
            put(slot, part, value[pl.ds(at, 16), :].astype(BF))


def halves(keep_ref, send_ref, slot):
    half = keep_ref.shape[0]
    return (keep_ref if slot < half else send_ref), slot % half


def up_kernel(
    order, lead, sc, n2_ref, gh_ref, act_ref, gffn_ref, att_ref, gproj_ref, keep_ref, send_ref,
    acc, acc_down
):
    step, steps = pl.program_id(0), pl.num_programs(0)
    chunk = gh_ref.shape[1]

    def put(first):
        def one(slot, part, rows):
            ref, at = halves(keep_ref, send_ref, slot)
            ref[at, first + part] = rows

        return one

    @pl.when(step == 0)
    def _():
        acc[...] = dot_tn(att_ref[...], gproj_ref[...])
        place_blocks(sc, lead, order, acc, 1, put(0))

    acc[...] = dot_tn(n2_ref[...], gh_ref[...])
    place_blocks(sc, lead, order, acc, 1, put(1 + step))
    acc_down[pl.ds(pl.multiple_of(step * chunk, chunk), chunk), :] = dot_tn(
        act_ref[...], gffn_ref[...]
    )

    @pl.when(step == steps - 1)
    def _():
        place_blocks(sc, lead, order, acc_down, 4, put(1 + steps))


def taps_kernel(v_ref, top_ref, bot_ref, g_ref, o3, o5, o7, pad, sums):
    rows, cols = g_ref.shape[1], g_ref.shape[2]

    @pl.when(pl.program_id(0) == 0)
    def _():
        o3[...] = jnp.zeros_like(o3)
        o5[...] = jnp.zeros_like(o5)
        o7[...] = jnp.zeros_like(o7)

    fill_rimmed(pad, lambda r: v_ref[0, r], rows, top_ref, bot_ref)
    for g, (o, lanes, size) in enumerate(((o3, 0, 3), (o5, 0, 5), (o7, 0, 7), (o7, 128, 7))):
        tap_sums(pad, g_ref, o, sums, lanes, g, size, RIM)


def back_kernel(
    marks, order, count, lead, sc, n_ref, k_ref, v_ref, sums_ref, gc_ref, top_ref, bot_ref, gq_ref, resid_ref,
    gm_ref, gain_ref, w3, w5, w7, *refs
):
    gkv_parts, refs = refs[:count], refs[count:]
    pieces = refs[: len(marks)]
    (
        gu_ref, first_ref, last_ref, ggain_ref, keep_ref, send_ref,
        gqkv_ref, acc, whole, pad, gv_buf, sem,
    ) = refs[len(marks) :]
    micro = pl.program_id(0)
    rows, cols = gc_ref.shape[1], gc_ref.shape[2]
    tokens, width = k_ref.shape[1], k_ref.shape[2]
    head = width // HEADS
    half = 4 * head

    @pl.when(micro == 0)
    def _():
        fetch(
            sc,
            pieces,
            marks,
            lead,
            lambda b, at: pltpu.make_async_copy(b, rows_at(whole, at), sem).start(),
        )
        ggain_ref[...] = jnp.zeros_like(ggain_ref)

    fill_rimmed(pad, lambda r: gc_ref[0, r], rows, top_ref, bot_ref)

    def one(r, carry):
        for g, (w, lanes, size) in enumerate(((w3, 0, 3), (w5, 0, 5), (w7, 0, 7), (w7, 128, 7))):
            gv_buf[r, :, g * 128 : (g + 1) * 128] = tap_row(
                pad, w, lanes, g, r + RIM, cols, size, None, True
            )
        return carry

    lax.fori_loop(0, rows, one, 0)

    ok = valid_rows(sc, micro, 0, rows, cols)
    total = sums_ref[0, head : head + 1]
    top = sums_ref[0, head + 1 : head + 2]
    normal = sums_ref[0, :head] / total
    gkv = functools.reduce(jnp.add, [ref[0].astype(F32) for ref in gkv_parts])
    inner = jnp.sum(normal * gkv, axis=0, keepdims=True)
    probs = jnp.where(ok > 0, jnp.exp(k_ref[0].astype(F32) - top) / total, 0.0)
    low = probs.astype(BF)
    v = v_ref[0].reshape(tokens, width)
    gqkv_ref[:, :width] = gq_ref[0]
    for b in range(width // half):
        lanes = slice(b * half, (b + 1) * half)
        diag = block_diagonal(gkv[:, lanes], head).astype(BF)
        gk = probs[:, lanes] * (dot(v[:, lanes], diag) - inner[:, lanes])
        gqkv_ref[:, width + b * half : width + (b + 1) * half] = gk.astype(BF)
        gv = dot_nt(low[:, lanes], diag) + gv_buf[:, :, lanes].reshape(tokens, half)
        gqkv_ref[:, 2 * width + b * half : 2 * width + (b + 1) * half] = gv.astype(BF)

    @pl.when(micro == 0)
    def _():
        pltpu.make_async_copy(whole, whole, sem).wait()

    dy = dot_nt(gqkv_ref[...], whole[...])
    unit, inverse = unit_rows(resid_ref[0])
    ggain_ref[...] += jnp.sum(dy * unit, axis=0, keepdims=True)
    gu = (gm_ref[0] + norm_back(dy, unit, inverse, gain_ref[...])) * ok
    gu_ref[0] = gu.reshape(rows, cols, width)
    first_ref[0, 0] = gu[:cols].astype(BF)
    last_ref[0, 0] = gu[tokens - cols :].astype(BF)
    normed = n_ref[0].reshape(tokens, width)
    for c in range(0, 3 * width, width):
        part = dot_tn(normed, gqkv_ref[:, c : c + width])

        @pl.when(micro == 0)
        def _():
            acc[:, c : c + width] = part

        @pl.when(micro > 0)
        def _():
            acc[:, c : c + width] += part

    @pl.when(micro == pl.num_programs(0) - 1)
    def _():
        def put(slot, part, lines):
            ref, at = halves(keep_ref, send_ref, slot)
            ref[at] = lines

        place_blocks(sc, lead, order, acc, 1, put)


def place_seven(at, width):
    return at % 16, width + 256 * (at // 16)


def place_three(at):
    return 11 + at // 4, 128 * (at % 4)


def place_five(at, width):
    return 1 + at % 13, width + 768 + 128 * (at // 13)


def pos_grad_kernel(
    sc, x_ref, top_ref, bot_ref, gu_ref, o3, o5, o7, gain1, gain2, small_ref, pad, sums, pos, small
):
    micro = pl.program_id(0)
    rows, cols = x_ref.shape[2], x_ref.shape[3]
    width = pos.shape[1]
    clear_edges(pad)
    cols_ok = valid_cols(sc, micro, cols)

    @pl.when(micro == 0)
    def _():
        pos[...] = jnp.zeros_like(pos)

    def put(r, cells):
        put_row(pad, r + 1, cells.astype(F32), cols_ok * valid_row(sc, micro, r))

    def fill(r, carry):
        put(r, x_ref[0, 0, r])
        return carry

    lax.fori_loop(0, rows, fill, 0)
    put(-1, top_ref[0, 0])
    put(rows, bot_ref[0, 0])
    for g in range(pad.shape[0]):
        tap_sums(pad, gu_ref, pos, sums, g * 128, g, 3, 1)
    @pl.when(micro == pl.num_programs(0) - 1)
    def _():
        small[...] = jnp.zeros_like(small)
        small[:9, :width] = pos[...]
        small[9:10, :width] = gain1[...]
        small[10:11, :width] = gain2[...]
        for at in range(49):
            line, lane = place_seven(at, width)
            small[line : line + 1, lane : lane + 256] = o7[at : at + 1, :]
        for at in range(9):
            line, lane = place_three(at)
            small[line : line + 1, lane : lane + 128] = o3[at : at + 1, :]
        for at in range(25):
            line, lane = place_five(at, width)
            small[line : line + 1, lane : lane + 128] = o5[at : at + 1, :]
        small_ref[...] = small[...].astype(BF)


def start_grad_kernel(sc, gu_ref, top_ref, bot_ref, w_ref, o_ref, pad):
    micro = pl.program_id(0)
    rows, cols = gu_ref.shape[1], gu_ref.shape[2]
    clear_edges(pad)
    cols_ok = valid_cols(sc, micro, cols)

    def fill(r, carry):
        put_row(pad, 1 + r, gu_ref[0, r])
        return carry

    lax.fori_loop(0, rows, fill, 0)
    put_row(pad, 0, top_ref[0, 0].astype(F32))
    put_row(pad, rows + 1, bot_ref[0, 0].astype(F32))

    def one(r, carry):
        ok = cols_ok * valid_row(sc, micro, r)
        for g in range(pad.shape[0]):
            taps = tap_row(pad, w_ref, g * 128, g, r + 1, cols, 3, None, True)
            o_ref[0, 0, r, :, g * 128 : (g + 1) * 128] = (
                taps + pad[g, r + 1, EDGE : EDGE + cols, :]
            ) * ok
        return carry

    lax.fori_loop(0, rows, one, 0)


def add_kernel(parts, *refs):
    outs = refs[-parts:]
    ins = refs[:-parts]
    total = ins[0][...].astype(F32)
    for ref in ins[1:]:
        total = total + ref[...].astype(F32)
    for n in range(parts):
        outs[n][...] = total[n].astype(outs[n].dtype)


def sum_small(refs):
    sums = [ref[...].astype(F32) for ref in refs]
    while len(sums) > 1:
        sums = [a + b for a, b in zip(sums[::2], sums[1::2])]
    return sums[0]


def add_small_kernel(parts, count, *refs):
    ins, small, outs = refs[:count], refs[count:-parts], refs[-parts:]
    size = outs[0].shape[0] - 1
    for n in range(parts):
        for b in range(size):
            total = ins[0][n * size + b].astype(F32)
            for ref in ins[1:]:
                total = total + ref[n * size + b].astype(F32)
            outs[n][b] = total.astype(outs[n].dtype)
    if not small:
        small = [ref.at[parts * size] for ref in ins]
    low = sum_small(small).astype(BF)
    for n in range(parts):
        outs[n][size] = low.astype(outs[n].dtype)


def rest_kernel(*refs):
    out_ref, up_ref, down_ref = refs[-3:]
    total = refs[0][0]
    for ref in refs[1:-3]:
        total = total + ref[0].astype(F32)
    width = out_ref.shape[1]
    groups = up_ref.shape[1] // width
    out_ref[...] = total[0]
    for part in range(groups):
        up_ref[:, part * width : (part + 1) * width] = total[1 + part]
        down_ref[16 * part : 16 * part + 16, :] = total[1 + groups + part]


def small_kernel(s_ref, pos, three, five, seven, gain1, gain2):
    width = gain1.shape[1]
    for i in range(3):
        for j in range(3):
            at = 3 * i + j
            pos[i, j : j + 1, :] = s_ref[at : at + 1, :width]
            line, lane = place_three(at)
            three[i, j : j + 1, :] = s_ref[line : line + 1, lane : lane + 128]
    for i in range(5):
        for j in range(5):
            line, lane = place_five(5 * i + j, width)
            five[i, j : j + 1, :128] = s_ref[line : line + 1, lane : lane + 128]
            line, lane = place_seven(7 * i + j + 8, width)
            five[i, j : j + 1, 128:192] = s_ref[line : line + 1, lane : lane + 64]
    for i in range(7):
        for j in range(7):
            line, lane = place_seven(7 * i + j, width)
            seven[i, j : j + 1, :] = s_ref[line : line + 1, lane + 64 : lane + 256]
    gain1[...] = s_ref[9:10, :width]
    gain2[...] = s_ref[10:11, :width]


def ends_kernel(split, *refs):
    ins, qkv_ref, outs = refs[:4], refs[4], refs[5:]
    total = ins[0][0]
    for ref in ins[1:]:
        total = total + ref[0].astype(F32)
    qkv_ref[...] = total
    outs[-1][...] = sum_small([ref.at[1] for ref in ins])
    if split:
        small_kernel(outs[-1], *outs[:-1])


SMEM = pl.BlockSpec(memory_space=pltpu.SMEM)
VMEM = pl.BlockSpec(memory_space=pltpu.VMEM)
ANY = pl.BlockSpec(memory_space=pl.ANY)


def by_micro(shape):
    rest = tuple(shape[1:])
    return pl.BlockSpec((1,) + rest, lambda m: (m,) + (0,) * len(rest))


def whole_spec(shape):
    return pl.BlockSpec(tuple(shape), lambda *_: (0,) * len(shape))


def shaped(shape, dtype):
    return jax.ShapeDtypeStruct(tuple(shape), dtype)


def call(
    kernel, name, grid, ins, outs, scratch, micros_long, deps=(), alias=None, carry=(), rows_here=8,
    limit=None
):
    nbytes = sum(a.size * a.dtype.itemsize for _, a in ins)
    nbytes += sum(math.prod(s) * jnp.dtype(d).itemsize for _, s, d in outs)
    first, last = len(ins), len(ins) + len(deps) + len(carry)
    results = last + len(outs)

    def body(*refs):
        if ins and ins[0][0] is SMEM:
            refs = (Here(refs[0], rows_here),) + refs[1:]
        kernel(*refs[:first], *refs[last:results], *refs[results + len(carry) :])

    alias = dict(alias or {})
    for n in range(len(carry)):
        alias[first + len(deps) + n] = len(outs) + n
    return pl.pallas_call(
        body,
        name=name,
        grid=grid,
        in_specs=[s for s, _ in ins] + [ANY] * (len(deps) + len(carry)),
        out_specs=[s for s, _, _ in outs] + [ANY] * len(carry),
        out_shape=[shaped(s, d) for _, s, d in outs] + [shaped(c.shape, c.dtype) for c in carry],
        scratch_shapes=scratch,
        input_output_aliases=alias,
        cost_estimate=pl.CostEstimate(
            flops=int(micros_long * 1.15e9), bytes_accessed=int(nbytes), transcendentals=0
        ),
        compiler_params=pltpu.CompilerParams(
            vmem_limit_bytes=(limit or VMEM_MIB) * MIB, dimension_semantics=("arbitrary",) * len(grid)
        ),
    )(*[a for _, a in ins], *deps, *carry)


def gate_kernel(*refs):
    pass


def gate(values, deps):
    return call(gate_kernel, "gate", (), [], [], [], 0, deps=deps, carry=values)


def add_parts(arrays, parts, deps=(), carry=()):
    n, block = arrays[0].shape[1], tuple(arrays[0].shape[2:])
    rest = (0,) * len(block)
    return call(
        functools.partial(add_kernel, parts),
        "add_parts",
        (n,),
        [(pl.BlockSpec((parts, 1) + block, lambda i: (0, i) + rest), a) for a in arrays],
        [
            (pl.BlockSpec((1,) + block, lambda i: (i,) + rest), (n,) + block, F32 if p == 0 else BF)
            for p in range(parts)
        ],
        [],
        2,
        deps,
        carry=carry,
    )


def add_small(arrays, small, parts, deps=()):
    blocks, rows, lanes = arrays[0].shape
    shape = ((blocks if small else blocks - 1) // parts + 1, rows, lanes)
    every = list(arrays) + list(small)
    return call(
        functools.partial(add_small_kernel, parts, len(arrays)),
        "add_small",
        (1,),
        [(whole_spec(a.shape), a) for a in every],
        [(whole_spec(shape), shape, F32 if p == 0 else BF) for p in range(parts)],
        [],
        0,
        deps,
    )


def local(
    images,
    cotangent,
    extent,
    w_qkv,
    w_out,
    w_up,
    w_down,
    pos_weight,
    win_three,
    win_five,
    win_seven,
    gain_one,
    gain_two,
):
    micros, _, rows, cols, width = images.shape
    head = width // HEADS
    hidden = w_up.shape[1]
    tokens = rows * cols
    me = positions()
    lead_masks, first, second, third = plan(w_up.shape[0])
    lead = len(lead_masks)
    stages = (first, second, third)
    sc = (SMEM, extent)
    n5 = 128
    gain1, gain2 = gain_one.reshape(1, width), gain_two.reshape(1, width)
    pad_rim = pltpu.VMEM((width // 128, rows + 2 * RIM, cols + 2 * EDGE, 128), F32)
    pad_one = pltpu.VMEM((width // 128, rows + 2, cols + 2 * EDGE, 128), F32)

    flat = (micros, tokens, width)
    map_shape = (micros, rows, cols, width)
    rim_shape = (micros, cols, rim_lanes(width)[1])
    q_block = join_lead(w_qkv, lead_masks)
    joined = [join_lead(w, lead_masks) for w in (w_out, w_up, w_down)]
    block_shape = (1 + 2 * (hidden // width), 16, width)
    taps3, w3, w5, w7, r_block = call(
        prep_kernel,
        "prep",
        (1,),
        [
            (whole_spec(w.shape), w)
            for w in (pos_weight, win_three, win_five, win_seven, *joined)
        ],
        [
            (whole_spec(shape), shape, F32)
            for shape in ((9, width), (9, 128), (25, n5), (49, 256))
        ]
        + [(whole_spec(block_shape), block_shape, BF)],
        [],
        2,
    )
    windows = [(whole_spec(w.shape), w) for w in (w3, w5, w7)]

    def gather_second(own):
        return [own] + [flipped(own, m) for m in spans(second)[1:]]

    def gather_third(pieces):
        return pieces + [flipped(p, third[0]) for p in pieces]

    marks = spans(second)
    marks = marks + [m ^ third[0] for m in marks]
    r_marks = [[m ^ f for f in spans(first[::-1])] for m in marks]
    marks = [[m ^ f for f in spans(first)] for m in marks]

    def single(shape, micro):
        rest = tuple(shape[1:])
        return pl.BlockSpec((1,) + rest, lambda m: (micro,) + (0,) * len(rest))

    q_blocks = [q_block] + [flipped(q_block, m) for m in spans(first)[1:]]
    edge = (micros, 1, cols, width)

    def edge_spec(row):
        return pl.BlockSpec((micros, 1, 1, cols, width), lambda _: (0, 0, row, 0, 0))

    own_shape = (len(q_blocks),) + q_block.shape
    q_own, x_first, x_last = call(
        functools.partial(first_kernel, len(q_blocks)),
        "first",
        (1,),
        [(VMEM if n else whole_spec(b.shape), b) for n, b in enumerate(q_blocks)]
        + [(edge_spec(0), images), (edge_spec(rows - 1), images)],
        [
            (whole_spec(own_shape), own_shape, BF),
            (whole_spec(edge), edge, BF),
            (whole_spec(edge), edge, BF),
        ],
        [],
        1,
        deps=[r_block],
        limit=16,
    )
    x_top, x_bot = rims(x_first, x_last)
    q_pieces = gather_second(q_own)
    x_in = pl.BlockSpec((1, 1, rows, cols, width), lambda m: (m, 0, 0, 0, 0))
    r_own = r_block[None]
    for mask in first[::-1]:
        r_own = jnp.concatenate([r_own, flipped(r_own, mask)])
    normed, resid = call(
        norm_kernel,
        "norm",
        (micros,),
        [
            sc,
            (x_in, images),
            (by_micro(edge), x_top),
            (by_micro(edge), x_bot),
            (whole_spec(taps3.shape), taps3),
            (whole_spec(gain1.shape), gain1),
        ],
        [(by_micro(map_shape), map_shape, BF), (by_micro(map_shape), map_shape, F32)],
        [pad_one],
        8,
    )
    qkv_pieces = gather_third(q_pieces)
    r_pieces = list(gate([r_own] + [flipped(r_own, m) for m in second], [normed]))
    r_pieces = r_pieces + [flipped(r_pieces[1], second[1])]
    sums_shape = (micros, head + 16, width)
    q, k, v, sums, v_first, v_last = call(
        functools.partial(qkv_kernel, marks, lead),
        "qkv",
        (micros,),
        [sc, (by_micro(map_shape), normed)] + [(ANY, p) for p in qkv_pieces],
        [
            (by_micro(flat), flat, BF),
            (by_micro(flat), flat, BF),
            (by_micro(map_shape), map_shape, BF),
            (by_micro(sums_shape), sums_shape, BF),
            (by_micro(rim_shape), rim_shape, BF),
            (by_micro(rim_shape), rim_shape, BF),
        ],
        [pltpu.VMEM((width, 3 * width), BF), pltpu.SemaphoreType.DMA],
        6,
        deps=[r_own],
    )

    def join_strips(kernel, cells, stage, dtype, deps, carry=()):
        parts = [cells] + [strip_swap(cells, m) for m in spans(stage)[1:]]
        spec = whole_spec(cells.shape)
        return call(
            kernel,
            "join",
            (1,),
            [(spec, p) for p in parts],
            [(spec, cells.shape, dtype)],
            [],
            1,
            deps=deps,
            carry=carry,
        )

    near, far = strip_stages()
    v_top, v_bot = rims(v_first, v_last)
    (conv,) = call(
        window_kernel,
        "window",
        (micros,),
        [(by_micro(map_shape), v)] + windows,
        [(by_micro(map_shape), map_shape, F32)],
        [pltpu.VMEM((width // 128, rows, cols + 2 * EDGE, 128), F32)],
        6,
    )
    join = functools.partial(join_kernel, head)
    (sums,) = join_strips(join, sums, near, BF, [v_top, v_bot, conv])
    (conv,) = call(
        window_rim_kernel,
        "window_rim",
        (micros,),
        [
            (by_micro(map_shape), conv),
            (by_micro(rim_shape), v_top),
            (by_micro(rim_shape), v_bot),
        ]
        + windows,
        [(by_micro(map_shape), map_shape, F32)],
        [pltpu.VMEM((width // 128, 2 * RIM, cols + 2 * EDGE, 128), F32)],
        3,
        deps=[sums],
    )
    r_pieces = list(gate(r_pieces, [sums]))
    sums_got = [strip_swap(sums, m) for m in spans(far)[1:]]
    rest_pieces = gather_third(r_pieces)

    tile_rows = rows
    tile = tile_rows * cols
    tiles = rows // tile_rows

    def tiled(lanes):
        return pl.BlockSpec((1, tile, lanes), lambda m, t: (m, t, 0))

    def per_micro(shape):
        return pl.BlockSpec((1,) + tuple(shape[1:]), lambda m, t: (m,) + (0,) * (len(shape) - 1))

    wide = (micros, tokens, hidden)
    gkv_shape = (micros, head, width)
    outs = call(
        functools.partial(main_kernel, r_marks, 1 + len(sums_got), lead),
        "main",
        (micros, tiles),
        [
            sc,
            (tiled(width), q),
            (tiled(width), conv.reshape(flat)),
            (tiled(width), resid.reshape(flat)),
            (tiled(width), cotangent.reshape(flat)),
            (whole_spec(gain2.shape), gain2),
        ]
        + [(per_micro(sums_shape), a) for a in [sums] + sums_got]
        + [(ANY, p) for p in rest_pieces],
        [
            (per_micro(sums_shape), sums_shape, F32),
            (tiled(width), flat, BF),
            (tiled(hidden), wide, BF),
            (tiled(hidden), wide, BF),
            (tiled(width), flat, BF),
            (tiled(width), flat, BF),
            (tiled(width), flat, BF),
            (tiled(width), flat, BF),
            (tiled(width), flat, F32),
            (tiled(width), flat, BF),
            (tiled(width), flat, F32),
            (per_micro(gkv_shape), gkv_shape, BF),
            (per_micro(rim_shape), rim_shape, BF),
            (per_micro(rim_shape), rim_shape, BF),
            (whole_spec((1, width)), (1, width), F32),
        ],
        [
            pltpu.VMEM((width, width), BF),
            pltpu.VMEM((hidden // width, width, width), BF),
            pltpu.VMEM((width // 16, 4, 16, width), BF),
            pltpu.VMEM((width // (4 * head), 4 * head, 4 * head), BF),
            pltpu.VMEM((width // (4 * head), 4 * head, 4 * head), F32),
            pltpu.SemaphoreType.DMA,
            pltpu.SemaphoreType.DMA,
            pltpu.SemaphoreType.DMA,
        ],
        24,
    )
    sums, out, act, g_hidden, n2, att, g_ffn, g_proj, g_conv, gq, g_middle, gkv = outs[:12]
    gc_first, gc_last, ggain2 = outs[12:]
    g_conv = g_conv.reshape(map_shape)
    gc_top, gc_bot = rims(gc_first, gc_last)

    first, second = sum_stages(first, second)
    marked = [0]
    for stage in (first, second, third):
        marked = [o ^ m for m in spans(stage) for o in marked]
    slots = len(marked) // 2

    def flat2(a):
        return a.reshape(-1, a.shape[-1])

    def staged(block, parts):
        return block.reshape((parts, block.shape[0] // parts) + block.shape[1:])

    half_shape = (slots,) + block_shape
    ops = [flat2(a) for a in (n2, g_hidden, act, g_ffn, att, g_proj)]
    chunk = 512

    def columns(a):
        return pl.BlockSpec((a.shape[0], chunk), lambda c: (0, c))

    keep, send = call(
        functools.partial(up_kernel, marked, lead),
        "mlp_grads",
        (hidden // chunk,),
        [sc]
        + [
            (columns(a) if a.shape[1] == hidden else whole_spec(a.shape), a)
            for a in ops
        ],
        [(whole_spec(half_shape), half_shape, BF)] * 2,
        [pltpu.VMEM((width, chunk), F32), pltpu.VMEM((hidden, width), F32)],
        12,
    )
    gkv_parts = [gkv] + [strip_swap(gkv, m) for m in spans(near)[1:]]
    gkv = functools.reduce(jnp.add, [p.astype(F32) for p in gkv_parts]).astype(BF)
    (send,) = gate([send], [gkv, gc_top, gc_bot, keep])
    got = flipped(send, third[0])
    gkv_got = [strip_swap(gkv, m) for m in spans(far)[1:]]
    o3, o5, o7 = call(
        taps_kernel,
        "window_grads",
        (micros,),
        [
            (by_micro(map_shape), v),
            (by_micro(rim_shape), v_top),
            (by_micro(rim_shape), v_bot),
            (by_micro(map_shape), g_conv),
        ],
        [
            (whole_spec((9, 128)), (9, 128), F32),
            (whole_spec((25, 128)), (25, 128), F32),
            (whole_spec((49, 256)), (49, 256), F32),
        ],
        [pad_rim, pltpu.VMEM((49, 8, 128), F32)],
        6,
        deps=[send],
    )
    parts2, parts1 = len(spans(second)), len(spans(first))
    rest = add_parts([staged(keep, parts2), staged(got, parts2)], parts2, [o3] + gkv_got)
    rest_got = [flipped(o, m) for o, m in zip(rest[1:], spans(second)[1:])]

    half_shape = (slots, 16, 3 * width)
    g_u, gu_first, gu_last, ggain1, keep, send = call(
        functools.partial(back_kernel, marks, marked, 1 + len(gkv_got), lead),
        "back",
        (micros,),
        [
            sc,
            (by_micro(map_shape), normed),
            (by_micro(flat), k),
            (by_micro(map_shape), v),
            (by_micro(sums_shape), sums),
            (by_micro(map_shape), g_conv),
            (by_micro(rim_shape), gc_top),
            (by_micro(rim_shape), gc_bot),
            (by_micro(flat), gq),
            (by_micro(flat), resid.reshape(flat)),
            (by_micro(flat), g_middle),
            (whole_spec(gain1.shape), gain1),
        ]
        + windows
        + [(by_micro(gkv_shape), g) for g in [gkv] + gkv_got]
        + [(ANY, p) for p in qkv_pieces],
        [
            (by_micro(map_shape), map_shape, F32),
            (by_micro(edge), edge, BF),
            (by_micro(edge), edge, BF),
            (whole_spec((1, width)), (1, width), F32),
            (whole_spec(half_shape), half_shape, BF),
            (whole_spec(half_shape), half_shape, BF),
        ],
        [
            pltpu.VMEM((tokens, 3 * width), BF),
            pltpu.VMEM((width, 3 * width), F32),
            pltpu.VMEM((width, 3 * width), BF),
            pad_rim,
            pltpu.VMEM((rows, cols, width), F32),
            pltpu.SemaphoreType.DMA,
        ],
        15,
        deps=[rest[0]],
    )
    gu_top, gu_bot = rims(gu_first, gu_last)
    small_shape = (16, 3 * width)
    (small,) = call(
        pos_grad_kernel,
        "pos_grad",
        (micros,),
        [
            sc,
            (x_in, images),
            (by_micro(x_top.shape), x_top),
            (by_micro(x_bot.shape), x_bot),
            (by_micro(map_shape), g_u),
        ]
        + [(whole_spec(a.shape), a) for a in (o3, o5, o7, ggain1, ggain2)],
        [(whole_spec(small_shape), small_shape, BF)],
        [
            pad_one,
            pltpu.VMEM((9, 8, 128), F32),
            pltpu.VMEM((9, width), F32),
            pltpu.VMEM(small_shape, F32),
        ],
        1,
    )
    send, small_send = gate([send, small], rest_got + [gu_top, gu_bot])
    got, small_got = flipped(send, third[0]), flipped(small_send, third[0])
    rest = add_parts([staged(p, parts1) for p in [rest[0]] + rest_got], parts1)
    own = add_small([keep, got], [small_send, small_got], parts2, [rest[0]])
    own_got = [flipped(o, m) for o, m in zip(own[1:], spans(second)[1:])]
    rest_got = [flipped(o, m) for o, m in zip(rest[1:], spans(first)[1:])]
    (grad_in,) = call(
        start_grad_kernel,
        "input_grad",
        (micros,),
        [
            sc,
            (by_micro(map_shape), g_u),
            (by_micro(gu_top.shape), gu_top),
            (by_micro(gu_bot.shape), gu_bot),
            (whole_spec(taps3.shape), taps3),
        ],
        [(x_in, (micros, 1, rows, cols, width), F32)],
        [pad_one],
        3,
        deps=[own[0]],
    )
    own = [own[0]] + own_got
    own = add_small(own, [], parts1, [grad_in])
    own_got = [flipped(o, m) for o, m in zip(own[1:], spans(first)[1:])]
    own = [own[0]] + own_got
    rest = [rest[0]] + rest_got

    def lead_sum(total):
        for mask in reversed(lead_masks):
            size = total.shape[0] // 2
            low, high = total[:size], total[size:]
            bit = (me & mask) != 0
            kept, sent = jnp.where(bit, high, low), jnp.where(bit, low, high)
            total = kept + flipped(sent, mask)
        return total

    def call_whole(kernel, name, arrays, shapes, deps=()):
        return call(
            kernel,
            name,
            (1,),
            [(VMEM if n else whole_spec(a.shape), a) for n, a in enumerate(arrays)],
            [(whole_spec(shape), shape, F32) for shape in shapes],
            [],
            1,
            deps=deps,
            limit=16,
        )

    rest_shapes = [(16, width), (16, hidden), (64, width)]
    grad_out, grad_up, grad_down = call_whole(rest_kernel, "rest_sum", rest, rest_shapes, own[:1])
    small_shapes = [w.shape for w in (pos_weight, win_three, win_five, win_seven)]
    small_shapes = small_shapes + [gain1.shape] * 2
    if lead_masks:
        grad_out, grad_up, grad_down = (lead_sum(g) for g in (grad_out, grad_up, grad_down))
        grad_qkv, small = call_whole(
            functools.partial(ends_kernel, False), "last_sum", own, [small_shape] * 2
        )
        grad_qkv = lead_sum(grad_qkv)
        low = small.astype(BF)
        got = [low.astype(F32)] + [flipped(low, m).astype(F32) for m in spans(lead_masks)[1:]]
        while len(got) > 1:
            got = [a + b for a, b in zip(got[::2], got[1::2])]
        smalls = call_whole(small_kernel, "small_grads", got, small_shapes)
    else:
        grad_qkv, *smalls, _ = call_whole(
            functools.partial(ends_kernel, True),
            "last_sum",
            own,
            [small_shape] + small_shapes + [small_shape],
        )
    g_pos, g_three, g_five, g_seven, ggain1, ggain2 = smalls
    return (
        out.reshape(micros, 1, rows, cols, width),
        grad_in,
        grad_qkv,
        grad_out,
        grad_up,
        grad_down,
        g_pos,
        g_three,
        g_five,
        g_seven,
        ggain1.reshape(width),
        ggain2.reshape(width),
    )


def solution(mesh):
    in_specs = (
        P(None, "img", "strip", None, None),
        P(None, "img", "strip", None, None),
        P(None, "img", None),
        P(("img", "strip"), None),
        P(("img", "strip"), None),
        P(("img", "strip"), None),
        P(("img", "strip"), None),
        P(),
        P(),
        P(),
        P(),
        P(),
        P(),
    )
    out_specs = (
        P(None, "img", "strip", None, None),
        P(None, "img", "strip", None, None),
        P(("img", "strip"), None),
        P(("img", "strip"), None),
        P(("img", "strip"), None),
        P(("img", "strip"), None),
        P(),
        P(),
        P(),
        P(),
        P(),
        P(),
    )
    return jax.shard_map(local, mesh=mesh, in_specs=in_specs, out_specs=out_specs, check_vma=False)
```

```python
import functools
import math

import jax
import jax.numpy as jnp
from jax import lax
from jax.experimental import pallas as pl
from jax.experimental.pallas import tpu as pltpu
from jax.sharding import PartitionSpec as P

HEADS = 8
norm_eps = 1e-06
masked_low = -1e30
RIM = 3
EDGE = 8
BF = jnp.bfloat16
F32 = jnp.float32
MIB = 2**20
VMEM_MIB = 63


def positions():
    return lax.axis_index("img") * lax.axis_size("strip") + lax.axis_index("strip")


def flipped(cells, mask):
    count = lax.axis_size("img") * lax.axis_size("strip")
    return lax.ppermute(cells, ("img", "strip"), [(i, i ^ mask) for i in range(count)])


def plan(shard_rows):
    strip_bits = int(math.log2(lax.axis_size("strip")))
    img_bits = int(math.log2(lax.axis_size("img")))
    lead = 0
    while (shard_rows << lead) < 16:
        lead += 1
    free = [1 << b for b in range(lead, strip_bits)]
    img = [1 << (strip_bits + b) for b in range(1, img_bits)]
    if len(free) > 2:
        first, second = [free[0], free[2]], [free[1]] + img
    else:
        first, second = free, img
    return [1 << b for b in range(lead)], first, second, [1 << strip_bits]


def sum_stages(first, second):
    masks = sorted(first + second)
    return (masks[1:3], [masks[0]] + masks[3:]) if len(masks) == 4 else (first, second)


def spans(masks):
    out = [0]
    for mask in masks:
        out = out + [o ^ mask for o in out]
    return out


def join_lead(shard, lead):
    me = positions()
    for mask in lead:
        other = flipped(shard, mask)
        shard = jnp.where(
            (me & mask) != 0, jnp.concatenate([other, shard]), jnp.concatenate([shard, other])
        )
    return shard


def strip_swap(cells, mask):
    count = lax.axis_size("strip")
    return lax.ppermute(cells, "strip", [(i, i ^ mask) for i in range(count)])


def strip_stages():
    masks = [1 << b for b in range(int(math.log2(lax.axis_size("strip"))))]
    return [masks[:1] + masks[2:3], masks[1:2] + masks[3:]]


def rims(first, last):
    count = lax.axis_size("strip")
    above = lax.ppermute(last, "strip", [(i, i + 1) for i in range(count - 1)])
    below = lax.ppermute(first, "strip", [(i + 1, i) for i in range(count - 1)])
    return above, below


class Here:
    def __init__(self, extent_ref, strip_rows):
        self.extent = extent_ref
        self.strip_rows = strip_rows

    def place(self):
        return positions()

    def first_row(self):
        return lax.axis_index("strip") * self.strip_rows

    def valid(self, micro, which):
        return self.extent[micro, 0, which]


def dot(a, b):
    return jnp.dot(a, b, preferred_element_type=F32)


def dot_nt(a, b):
    return lax.dot_general(a, b, (((1,), (1,)), ((), ())), preferred_element_type=F32)


def dot_tn(a, b):
    return lax.dot_general(a, b, (((0,), (0,)), ((), ())), preferred_element_type=F32)


def valid_rows(sc, micro, first_row, rows, cols):
    n = rows * cols
    shift = int(math.log2(cols))
    flat = lax.broadcasted_iota(jnp.int32, (n, 1), 0)
    row = lax.shift_right_logical(flat, shift) + (sc.first_row() + first_row)
    ok = (row < sc.valid(micro, 0)) & ((flat & (cols - 1)) < sc.valid(micro, 1))
    return jnp.where(ok, 1.0, 0.0).astype(F32)


def valid_cols(sc, micro, cols):
    col = lax.broadcasted_iota(jnp.int32, (cols, 128), 0)
    return jnp.where(col < sc.valid(micro, 1), 1.0, 0.0).astype(F32)


def valid_row(sc, micro, row):
    at = sc.first_row() + row
    return jnp.where((at >= 0) & (at < sc.valid(micro, 0)), 1.0, 0.0).astype(F32)


def unit_rows(fields):
    average = jnp.mean(fields, axis=-1, keepdims=True)
    centred = fields - average
    inverse = lax.rsqrt(jnp.mean(centred * centred, axis=-1, keepdims=True) + norm_eps)
    return centred * inverse, inverse


def norm_back(dy, unit, inverse, gain):
    dyg = dy * gain
    first = jnp.mean(dyg, axis=-1, keepdims=True)
    second = jnp.mean(dyg * unit, axis=-1, keepdims=True)
    return inverse * (dyg - first - unit * second)


def clear_edges(pad):
    groups, rows, cols, _ = pad.shape
    zeros = jnp.zeros((rows, EDGE, 128), F32)
    for g in range(groups):
        pad[g, :, :EDGE, :] = zeros
        pad[g, :, cols - EDGE :, :] = zeros


def put_row(pad, row, cells, ok=None):
    for g in range(pad.shape[0]):
        part = cells[:, g * 128 : (g + 1) * 128]
        pad[g, row, EDGE : EDGE + cells.shape[0], :] = part if ok is None else part * ok


def rim_lanes(width):
    out, lane = [], 0
    for row in range(RIM):
        out.append((row, lane))
        lane += width - 128 * row
    return out, lane


def pack_rim(rim_ref, lines):
    spans_, _ = rim_lanes(lines[0].shape[1])
    for line, (group, lane) in zip(lines, spans_):
        part = line[:, 128 * group :]
        rim_ref[0, :, lane : lane + part.shape[1]] = part.astype(BF)


def put_rims(pad, top_ref, bot_ref, rows):
    width = 128 * pad.shape[0]
    cols = top_ref.shape[1]
    for near, (group, lane) in enumerate(rim_lanes(width)[0]):
        for ref, line in ((top_ref, RIM - 1 - near), (bot_ref, RIM + rows + near)):
            for g in range(group, pad.shape[0]):
                at = lane + 128 * (g - group)
                pad[g, line, EDGE : EDGE + cols, :] = ref[0, :, at : at + 128].astype(F32)


def tap_row(pad, w_ref, lanes, group, row, cols, size, lines, flip):
    reach = size // 2
    total = jnp.zeros((cols, 128), F32)
    for i in lines or range(size):
        for j in range(size):
            at = i * size + j
            if flip:
                at = size * size - 1 - at
            w = w_ref[at : at + 1, lanes : lanes + 128]
            total = total + w * pad[
                group, row + i - reach, EDGE + j - reach : EDGE + j - reach + cols, :
            ]
    return total


def tap_sums(pad, grad_ref, out_ref, sums, lanes, group, size, above):
    reach = size // 2
    rows, cols = grad_ref.shape[1], grad_ref.shape[2]
    taps = size * size
    sums[:taps] = jnp.zeros((taps, 8, 128), F32)

    def step(t, carry):
        for half in range(2):
            c = pl.multiple_of(t * 16 + half * 8, 8)
            grads = [
                grad_ref[0, r, pl.ds(c, 8), group * 128 : (group + 1) * 128].astype(F32)
                for r in range(rows)
            ]
            for j in range(size):
                part = [None] * size
                for line in range(rows + 2 * reach):
                    f = pad[group, line + above - reach, pl.ds(c + EDGE + j - reach, 8), :]
                    for i in range(size):
                        r = line - i
                        if 0 <= r < rows:
                            term = grads[r] * f
                            part[i] = term if part[i] is None else part[i] + term
                for i in range(size):
                    at = i * size + j
                    sums[at] += part[i]
        return carry

    lax.fori_loop(0, cols // 16, step, 0)
    for at in range(taps):
        out_ref[at : at + 1, lanes : lanes + 128] += jnp.sum(sums[at], axis=0, keepdims=True)


def block_diagonal(wide, head):
    lane = lax.broadcasted_iota(jnp.int32, wide.shape, 1) // head
    return jnp.concatenate(
        [jnp.where(lane == h, wide, 0.0) for h in range(wide.shape[1] // head)], axis=0
    )


def diagonal_blocks(full, head):
    lane = lax.broadcasted_iota(jnp.int32, (head, full.shape[1]), 1) // head
    total = jnp.zeros((head, full.shape[1]), F32)
    for h in range(full.shape[1] // head):
        total = total + jnp.where(lane == h, full[h * head : (h + 1) * head], 0.0)
    return total


def fetch(sc, pieces, marks, lead, copy):
    place = sc.place() >> lead
    for piece, mark in zip(pieces, marks):
        for k, mask in enumerate(mark):
            copy(piece.at[k], place ^ (mask >> lead))


def rows_at(whole, block):
    return whole.at[pl.ds(pl.multiple_of(block * 16, 16), 16), :]


def taps_prep(pos_ref, three_ref, five_ref, seven_ref, taps3, w3, w5, w7):
    for i in range(3):
        for j in range(3):
            taps3[3 * i + j : 3 * i + j + 1, :] = pos_ref[i, j : j + 1, :]
            w3[3 * i + j : 3 * i + j + 1, :] = three_ref[i, j : j + 1, :]
    for i in range(5):
        for j in range(5):
            w5[5 * i + j : 5 * i + j + 1, :] = five_ref[i, j : j + 1, :128]
    for i in range(7):
        for j in range(7):
            seven = seven_ref[i, j : j + 1, :]
            low = jnp.zeros((1, 64), F32)
            if 1 <= i <= 5 and 1 <= j <= 5:
                low = five_ref[i - 1, j - 1 : j, 128:192]
            w7[7 * i + j : 7 * i + j + 1, :] = jnp.concatenate([low, seven], axis=1)


def prep_kernel(pos_ref, three_ref, five_ref, seven_ref, out_ref, up_ref, down_ref, *refs):
    taps_prep(pos_ref, three_ref, five_ref, seven_ref, *refs[:4])
    o_ref = refs[4]
    width = out_ref.shape[1]
    o_ref[0] = out_ref[...]
    for part in range(4):
        o_ref[1 + part] = up_ref[:, part * width : (part + 1) * width]
        o_ref[5 + part] = down_ref[16 * part : 16 * part + 16, :]


def first_kernel(count, *refs):
    x_first, x_last, o_ref, first_ref, last_ref = refs[count:]
    for n in range(count):
        o_ref[n] = refs[n][...]
    first_ref[...] = x_first[:, 0]
    last_ref[...] = x_last[:, 0]


def join_kernel(head, *refs):
    o_ref = refs[-1]
    parts = [ref[...].astype(F32) for ref in refs[:-1]]
    tops = [p[:, head + 1 : head + 2] for p in parts]
    top = functools.reduce(jnp.maximum, tops)
    total = functools.reduce(
        jnp.add, [p[:, : head + 1] * jnp.exp(t - top) for p, t in zip(parts, tops)]
    )
    o_ref[:, :head] = total[:, :head].astype(o_ref.dtype)
    line = lax.broadcasted_iota(jnp.int32, parts[0][:, head:].shape, 1)
    o_ref[:, head:] = jnp.where(
        line == 0, total[:, head:], jnp.where(line == 1, top, 0.0)
    ).astype(o_ref.dtype)


def norm_kernel(sc, x_ref, top_ref, bot_ref, w_ref, gain_ref, normed_ref, resid_ref, pad):
    micro = pl.program_id(0)
    rows, cols = x_ref.shape[2], x_ref.shape[3]
    clear_edges(pad)
    cols_ok = valid_cols(sc, micro, cols)
    put_row(pad, 0, top_ref[0, 0].astype(F32), cols_ok * valid_row(sc, micro, -1))
    put_row(pad, rows + 1, bot_ref[0, 0].astype(F32), cols_ok * valid_row(sc, micro, rows))

    def fill(r, carry):
        put_row(pad, r + 1, x_ref[0, 0, r].astype(F32), cols_ok * valid_row(sc, micro, r))
        return carry

    lax.fori_loop(0, rows, fill, 0)
    gain = gain_ref[...]

    def one(r, carry):
        ok = cols_ok * valid_row(sc, micro, r)
        for g in range(pad.shape[0]):
            taps = tap_row(pad, w_ref, g * 128, g, r + 1, cols, 3, None, False)
            resid_ref[0, r, :, g * 128 : (g + 1) * 128] = (
                taps + pad[g, r + 1, EDGE : EDGE + cols, :]
            ) * ok
        return carry

    lax.fori_loop(0, rows, one, 0, unroll=2)
    for r in range(0, rows, 2):
        unit, _ = unit_rows(resid_ref[0, r : r + 2].reshape(2 * cols, resid_ref.shape[3]))
        normed_ref[0, r : r + 2] = (unit * gain).astype(BF).reshape(2, cols, unit.shape[1])


def qkv_kernel(marks, lead, sc, n_ref, *refs):
    pieces = refs[: len(marks)]
    q_ref, k_ref, v_ref, sums_ref, first_ref, last_ref, whole, sem = refs[len(marks) :]
    micro = pl.program_id(0)
    rows, cols, width = n_ref.shape[1:]
    head = width // HEADS
    tokens = rows * cols

    @pl.when(micro == 0)
    def _():
        fetch(
            sc,
            pieces,
            marks,
            lead,
            lambda b, at: pltpu.make_async_copy(b, rows_at(whole, at), sem).start(),
        )
        pltpu.make_async_copy(whole, whole, sem).wait()

    normed = n_ref[0].reshape(tokens, width)
    q_ref[0] = dot(normed, whole[:, :width]).astype(BF)
    k = dot(normed, whole[:, width : 2 * width]).astype(BF)
    k_ref[0] = k
    v = dot(normed, whole[:, 2 * width :]).astype(BF)
    v_ref[0] = v.reshape(rows, cols, width)
    pack_rim(first_ref, [v[r * cols : (r + 1) * cols] for r in range(RIM)])
    pack_rim(last_ref, [v[(rows - 1 - r) * cols : (rows - r) * cols] for r in range(RIM)])
    ok = valid_rows(sc, micro, 0, rows, cols)
    keys = jnp.where(ok > 0, k.astype(F32), masked_low)
    top = jnp.max(keys, axis=0, keepdims=True)
    ew = jnp.exp(keys - top) * ok
    total = jnp.sum(ew, axis=0, keepdims=True)
    low = ew.astype(BF)
    half = 4 * head
    for b in range(width // half):
        full = dot_tn(v[:, b * half : (b + 1) * half], low[:, b * half : (b + 1) * half])
        sums_ref[0, :head, b * half : (b + 1) * half] = diagonal_blocks(full, head).astype(BF)
    line = lax.broadcasted_iota(jnp.int32, (16, width), 0)
    sums_ref[0, head:, :] = jnp.where(line == 0, total, jnp.where(line == 1, top, 0.0)).astype(BF)


def fill_rimmed(pad, source, rows, top_ref, bot_ref):
    clear_edges(pad)

    def fill(r, carry):
        put_row(pad, RIM + r, source(r).astype(F32))
        return carry

    lax.fori_loop(0, rows, fill, 0)
    put_rims(pad, top_ref, bot_ref, rows)


WINDOWS = ((0, 0, 3), (1, 0, 5), (2, 0, 7), (2, 128, 7))


def window_kernel(v_ref, *refs):
    weights, (o_ref, pad) = refs[:3], refs[3:]
    rows, cols = o_ref.shape[1], o_ref.shape[2]
    clear_edges(pad)

    def fill(r, carry):
        put_row(pad, r, v_ref[0, r].astype(F32))
        return carry

    lax.fori_loop(0, rows, fill, 0)
    for r in range(rows):
        for g, (which, lanes, size) in enumerate(WINDOWS):
            reach = size // 2
            lines = range(max(0, reach - r), min(size, rows + reach - r))
            o_ref[0, r, :, g * 128 : (g + 1) * 128] = tap_row(
                pad, weights[which], lanes, g, r, cols, size, lines, False
            )


def window_rim_kernel(part_ref, top_ref, bot_ref, *refs):
    weights, (o_ref, pad) = refs[:3], refs[3:]
    rows, cols = 2 * RIM, part_ref.shape[2]
    clear_edges(pad)
    put_rims(pad, top_ref, bot_ref, 0)
    last = part_ref.shape[1]
    for r in range(RIM):
        for row, centre in ((r, RIM + r), (last - 1 - r, RIM - 1 - r)):
            for g, (which, lanes, size) in enumerate(WINDOWS):
                reach = size // 2
                if row < RIM:
                    lines = range(0, reach - r)
                else:
                    lines = range(reach + 1 + r, size)
                part = part_ref[0, row, :, g * 128 : (g + 1) * 128]
                if lines:
                    part = part + tap_row(
                        pad, weights[which], lanes, g, centre, cols, size, lines, False
                    )
                o_ref[0, row, :, g * 128 : (g + 1) * 128] = part
    for row in range(RIM, last - RIM):
        o_ref[0, row] = part_ref[0, row]


def main_kernel(
    marks, count, lead, sc, q_ref, conv_ref, resid_ref, cot_ref, gain_ref, *refs
):
    parts, refs = refs[:count], refs[count:]
    pieces = refs[: len(marks)]
    (
        sums_ref,
        out_ref,
        act_ref,
        gh_ref,
        n2_ref,
        att_ref,
        gffn_ref,
        gproj_ref,
        gconv_ref,
        gq_ref,
        gm_ref,
        gkv_ref,
        first_ref,
        last_ref,
        ggain_ref,
        w_out,
        w_up,
        w_down,
        kvn,
        gacc,
        sem,
        up_sem,
        down_sem,
    ) = refs[len(marks) :]
    micro, tile = pl.program_id(0), pl.program_id(1)
    tokens, width = q_ref.shape[1], q_ref.shape[2]
    cols = 64
    rows = tokens // cols
    head = width // HEADS
    half = 4 * head
    scale = head**-0.5
    groups, step = w_up.shape[0], w_up.shape[2]
    per_group = w_down.shape[0] // groups

    @pl.when((micro == 0) & (tile == 0))
    def _():
        groups = w_up.shape[0]

        def to_out(b, at):
            pltpu.make_async_copy(b.at[0], rows_at(w_out, at), sem).start()

        def to_up(b, at):
            target = w_up.at[:, pl.ds(pl.multiple_of(at * 16, 16), 16), :]
            pltpu.make_async_copy(b.at[1 : 1 + groups], target, up_sem).start()

        def to_down(b, at):
            pltpu.make_async_copy(b.at[1 + groups :], w_down.at[at], down_sem).start()

        for copy in (to_out, to_up, to_down):
            fetch(sc, pieces, marks, lead, copy)
        ggain_ref[...] = jnp.zeros_like(ggain_ref)

    @pl.when(tile == 0)
    def _():
        join_kernel(head, *parts, sums_ref)
        normal = sums_ref[0, :head] / sums_ref[0, head : head + 1] * scale
        for b in range(width // half):
            kvn[b] = block_diagonal(normal[:, b * half : (b + 1) * half], head).astype(BF)
        gacc[...] = jnp.zeros_like(gacc)

    ok = valid_rows(sc, micro, tile * rows, rows, cols)
    q = q_ref[0]
    qf = q.astype(F32)
    conv = conv_ref[0]
    factor = jnp.concatenate(
        [dot_nt(q[:, b * half : (b + 1) * half], kvn[b]) for b in range(width // half)], axis=1
    )
    att = (factor + qf * conv).astype(BF)
    att_ref[0] = att

    @pl.when((micro == 0) & (tile == 0))
    def _():
        pltpu.make_async_copy(w_out, w_out, sem).wait()

    middle = resid_ref[0] + dot(att, w_out[...])
    unit, inverse = unit_rows(middle)
    gain = gain_ref[...]
    n2 = (unit * gain).astype(BF)
    n2_ref[0] = n2
    g_top = cot_ref[0].astype(F32) * ok
    g_ffn = g_top.astype(BF)
    gffn_ref[0] = g_ffn

    @pl.when((micro == 0) & (tile == 0))
    def _():
        pltpu.make_async_copy(w_up, w_up, up_sem).wait()
        pltpu.make_async_copy(w_down, w_down, down_sem).wait()

    ffn = jnp.zeros((tokens, width), F32)
    back = jnp.zeros((tokens, width), F32)
    for group in range(groups):
        c = group * step
        up = w_up[group]
        down = w_down[group * per_group : (group + 1) * per_group].reshape(step, width)
        hidden = dot(n2, up)
        cdf = 0.5 * (1.0 + lax.erf(hidden * (1.0 / math.sqrt(2.0))))
        act = (hidden * cdf).astype(BF)
        slope = cdf + hidden * jnp.exp(-0.5 * hidden * hidden) * (1.0 / math.sqrt(2.0 * math.pi))
        act_ref[0, :, c : c + step] = act
        ffn = ffn + dot(act, down)
        g_hidden = (dot_nt(g_ffn, down) * slope).astype(BF)
        gh_ref[0, :, c : c + step] = g_hidden
        back = back + dot_nt(g_hidden, up)
    out_ref[0] = ((middle + ffn) * ok).astype(BF)
    ggain_ref[...] += jnp.sum(back * unit, axis=0, keepdims=True)
    g_middle = g_top + norm_back(back, unit, inverse, gain)
    gm_ref[0] = g_middle
    g_proj = g_middle.astype(BF)
    gproj_ref[0] = g_proj
    g_att = dot_nt(g_proj, w_out[...])
    g_conv = g_att * qf
    gconv_ref[0] = g_conv

    @pl.when(tile == 0)
    def _():
        pack_rim(first_ref, [g_conv[r * cols : (r + 1) * cols] for r in range(RIM)])

    @pl.when(tile == pl.num_programs(1) - 1)
    def _():
        pack_rim(last_ref, [g_conv[(rows - 1 - r) * cols : (rows - r) * cols] for r in range(RIM)])

    low = g_att.astype(BF)
    for b in range(width // half):
        lanes = slice(b * half, (b + 1) * half)
        gq_ref[0, :, lanes] = (
            g_att[:, lanes] * conv[:, lanes] + dot(low[:, lanes], kvn[b])
        ).astype(BF)
        gacc[b] += dot_tn(low[:, lanes], q[:, lanes])

    @pl.when(tile == pl.num_programs(1) - 1)
    def _():
        for b in range(width // half):
            gkv_ref[0, :, b * half : (b + 1) * half] = (
                diagonal_blocks(gacc[b], head) * scale
            ).astype(BF)


def place_blocks(sc, lead, order, value, parts, put):
    place = sc.place() >> lead
    for slot, mask in enumerate(order):
        block = place ^ (mask >> lead)
        for part in range(parts):
            at = pl.multiple_of(block * (16 * parts) + 16 * part, 16)
            put(slot, part, value[pl.ds(at, 16), :].astype(BF))


def halves(keep_ref, send_ref, slot):
    half = keep_ref.shape[0]
    return (keep_ref if slot < half else send_ref), slot % half


def up_kernel(
    order, lead, sc, n2_ref, gh_ref, act_ref, gffn_ref, att_ref, gproj_ref, keep_ref, send_ref,
    acc, acc_down
):
    step, steps = pl.program_id(0), pl.num_programs(0)
    chunk = gh_ref.shape[1]

    def put(first):
        def one(slot, part, rows):
            ref, at = halves(keep_ref, send_ref, slot)
            ref[at, first + part] = rows

        return one

    @pl.when(step == 0)
    def _():
        acc[...] = dot_tn(att_ref[...], gproj_ref[...])
        place_blocks(sc, lead, order, acc, 1, put(0))

    acc[...] = dot_tn(n2_ref[...], gh_ref[...])
    place_blocks(sc, lead, order, acc, 1, put(1 + step))
    acc_down[pl.ds(pl.multiple_of(step * chunk, chunk), chunk), :] = dot_tn(
        act_ref[...], gffn_ref[...]
    )

    @pl.when(step == steps - 1)
    def _():
        place_blocks(sc, lead, order, acc_down, 4, put(1 + steps))


def taps_kernel(v_ref, top_ref, bot_ref, g_ref, o3, o5, o7, pad, sums):
    rows, cols = g_ref.shape[1], g_ref.shape[2]

    @pl.when(pl.program_id(0) == 0)
    def _():
        o3[...] = jnp.zeros_like(o3)
        o5[...] = jnp.zeros_like(o5)
        o7[...] = jnp.zeros_like(o7)

    fill_rimmed(pad, lambda r: v_ref[0, r], rows, top_ref, bot_ref)
    for g, (o, lanes, size) in enumerate(((o3, 0, 3), (o5, 0, 5), (o7, 0, 7), (o7, 128, 7))):
        tap_sums(pad, g_ref, o, sums, lanes, g, size, RIM)


def back_kernel(
    marks, order, count, lead, sc, n_ref, k_ref, v_ref, sums_ref, gc_ref, top_ref, bot_ref, gq_ref, resid_ref,
    gm_ref, gain_ref, w3, w5, w7, *refs
):
    gkv_parts, refs = refs[:count], refs[count:]
    pieces = refs[: len(marks)]
    (
        gu_ref, first_ref, last_ref, ggain_ref, keep_ref, send_ref,
        gqkv_ref, acc, whole, pad, gv_buf, sem,
    ) = refs[len(marks) :]
    micro = pl.program_id(0)
    rows, cols = gc_ref.shape[1], gc_ref.shape[2]
    tokens, width = k_ref.shape[1], k_ref.shape[2]
    head = width // HEADS
    half = 4 * head

    @pl.when(micro == 0)
    def _():
        fetch(
            sc,
            pieces,
            marks,
            lead,
            lambda b, at: pltpu.make_async_copy(b, rows_at(whole, at), sem).start(),
        )
        ggain_ref[...] = jnp.zeros_like(ggain_ref)

    fill_rimmed(pad, lambda r: gc_ref[0, r], rows, top_ref, bot_ref)

    def one(r, carry):
        for g, (w, lanes, size) in enumerate(((w3, 0, 3), (w5, 0, 5), (w7, 0, 7), (w7, 128, 7))):
            gv_buf[r, :, g * 128 : (g + 1) * 128] = tap_row(
                pad, w, lanes, g, r + RIM, cols, size, None, True
            )
        return carry

    lax.fori_loop(0, rows, one, 0)

    ok = valid_rows(sc, micro, 0, rows, cols)
    total = sums_ref[0, head : head + 1]
    top = sums_ref[0, head + 1 : head + 2]
    normal = sums_ref[0, :head] / total
    gkv = functools.reduce(jnp.add, [ref[0].astype(F32) for ref in gkv_parts])
    inner = jnp.sum(normal * gkv, axis=0, keepdims=True)
    probs = jnp.where(ok > 0, jnp.exp(k_ref[0].astype(F32) - top) / total, 0.0)
    low = probs.astype(BF)
    v = v_ref[0].reshape(tokens, width)
    gqkv_ref[:, :width] = gq_ref[0]
    for b in range(width // half):
        lanes = slice(b * half, (b + 1) * half)
        diag = block_diagonal(gkv[:, lanes], head).astype(BF)
        gk = probs[:, lanes] * (dot(v[:, lanes], diag) - inner[:, lanes])
        gqkv_ref[:, width + b * half : width + (b + 1) * half] = gk.astype(BF)
        gv = dot_nt(low[:, lanes], diag) + gv_buf[:, :, lanes].reshape(tokens, half)
        gqkv_ref[:, 2 * width + b * half : 2 * width + (b + 1) * half] = gv.astype(BF)

    @pl.when(micro == 0)
    def _():
        pltpu.make_async_copy(whole, whole, sem).wait()

    dy = dot_nt(gqkv_ref[...], whole[...])
    unit, inverse = unit_rows(resid_ref[0])
    ggain_ref[...] += jnp.sum(dy * unit, axis=0, keepdims=True)
    gu = (gm_ref[0] + norm_back(dy, unit, inverse, gain_ref[...])) * ok
    gu_ref[0] = gu.reshape(rows, cols, width)
    first_ref[0, 0] = gu[:cols].astype(BF)
    last_ref[0, 0] = gu[tokens - cols :].astype(BF)
    normed = n_ref[0].reshape(tokens, width)
    for c in range(0, 3 * width, width):
        part = dot_tn(normed, gqkv_ref[:, c : c + width])

        @pl.when(micro == 0)
        def _():
            acc[:, c : c + width] = part

        @pl.when(micro > 0)
        def _():
            acc[:, c : c + width] += part

    @pl.when(micro == pl.num_programs(0) - 1)
    def _():
        def put(slot, part, lines):
            ref, at = halves(keep_ref, send_ref, slot)
            ref[at] = lines

        place_blocks(sc, lead, order, acc, 1, put)


def place_seven(at, width):
    return at % 16, width + 256 * (at // 16)


def place_three(at):
    return 11 + at // 4, 128 * (at % 4)


def place_five(at, width):
    return 1 + at % 13, width + 768 + 128 * (at // 13)


def pos_grad_kernel(
    sc, x_ref, top_ref, bot_ref, gu_ref, o3, o5, o7, gain1, gain2, small_ref, pad, sums, pos, small
):
    micro = pl.program_id(0)
    rows, cols = x_ref.shape[2], x_ref.shape[3]
    width = pos.shape[1]
    clear_edges(pad)
    cols_ok = valid_cols(sc, micro, cols)

    @pl.when(micro == 0)
    def _():
        pos[...] = jnp.zeros_like(pos)

    def put(r, cells):
        put_row(pad, r + 1, cells.astype(F32), cols_ok * valid_row(sc, micro, r))

    def fill(r, carry):
        put(r, x_ref[0, 0, r])
        return carry

    lax.fori_loop(0, rows, fill, 0)
    put(-1, top_ref[0, 0])
    put(rows, bot_ref[0, 0])
    for g in range(pad.shape[0]):
        tap_sums(pad, gu_ref, pos, sums, g * 128, g, 3, 1)
    @pl.when(micro == pl.num_programs(0) - 1)
    def _():
        small[...] = jnp.zeros_like(small)
        small[:9, :width] = pos[...]
        small[9:10, :width] = gain1[...]
        small[10:11, :width] = gain2[...]
        for at in range(49):
            line, lane = place_seven(at, width)
            small[line : line + 1, lane : lane + 256] = o7[at : at + 1, :]
        for at in range(9):
            line, lane = place_three(at)
            small[line : line + 1, lane : lane + 128] = o3[at : at + 1, :]
        for at in range(25):
            line, lane = place_five(at, width)
            small[line : line + 1, lane : lane + 128] = o5[at : at + 1, :]
        small_ref[...] = small[...].astype(BF)


def start_grad_kernel(sc, gu_ref, top_ref, bot_ref, w_ref, o_ref, pad):
    micro = pl.program_id(0)
    rows, cols = gu_ref.shape[1], gu_ref.shape[2]
    clear_edges(pad)
    cols_ok = valid_cols(sc, micro, cols)

    def fill(r, carry):
        put_row(pad, 1 + r, gu_ref[0, r])
        return carry

    lax.fori_loop(0, rows, fill, 0)
    put_row(pad, 0, top_ref[0, 0].astype(F32))
    put_row(pad, rows + 1, bot_ref[0, 0].astype(F32))

    def one(r, carry):
        ok = cols_ok * valid_row(sc, micro, r)
        for g in range(pad.shape[0]):
            taps = tap_row(pad, w_ref, g * 128, g, r + 1, cols, 3, None, True)
            o_ref[0, 0, r, :, g * 128 : (g + 1) * 128] = (
                taps + pad[g, r + 1, EDGE : EDGE + cols, :]
            ) * ok
        return carry

    lax.fori_loop(0, rows, one, 0)


def add_kernel(parts, *refs):
    outs = refs[-parts:]
    ins = refs[:-parts]
    total = ins[0][...].astype(F32)
    for ref in ins[1:]:
        total = total + ref[...].astype(F32)
    for n in range(parts):
        outs[n][...] = total[n].astype(outs[n].dtype)


def sum_small(refs):
    sums = [ref[...].astype(F32) for ref in refs]
    while len(sums) > 1:
        sums = [a + b for a, b in zip(sums[::2], sums[1::2])]
    return sums[0]


def add_small_kernel(parts, count, *refs):
    ins, small, outs = refs[:count], refs[count:-parts], refs[-parts:]
    size = outs[0].shape[0] - 1
    for n in range(parts):
        for b in range(size):
            total = ins[0][n * size + b].astype(F32)
            for ref in ins[1:]:
                total = total + ref[n * size + b].astype(F32)
            outs[n][b] = total.astype(outs[n].dtype)
    if not small:
        small = [ref.at[parts * size] for ref in ins]
    low = sum_small(small).astype(BF)
    for n in range(parts):
        outs[n][size] = low.astype(outs[n].dtype)


def rest_kernel(*refs):
    out_ref, up_ref, down_ref = refs[-3:]
    total = refs[0][0]
    for ref in refs[1:-3]:
        total = total + ref[0].astype(F32)
    width = out_ref.shape[1]
    groups = up_ref.shape[1] // width
    out_ref[...] = total[0]
    for part in range(groups):
        up_ref[:, part * width : (part + 1) * width] = total[1 + part]
        down_ref[16 * part : 16 * part + 16, :] = total[1 + groups + part]


def small_kernel(s_ref, pos, three, five, seven, gain1, gain2):
    width = gain1.shape[1]
    for i in range(3):
        for j in range(3):
            at = 3 * i + j
            pos[i, j : j + 1, :] = s_ref[at : at + 1, :width]
            line, lane = place_three(at)
            three[i, j : j + 1, :] = s_ref[line : line + 1, lane : lane + 128]
    for i in range(5):
        for j in range(5):
            line, lane = place_five(5 * i + j, width)
            five[i, j : j + 1, :128] = s_ref[line : line + 1, lane : lane + 128]
            line, lane = place_seven(7 * i + j + 8, width)
            five[i, j : j + 1, 128:192] = s_ref[line : line + 1, lane : lane + 64]
    for i in range(7):
        for j in range(7):
            line, lane = place_seven(7 * i + j, width)
            seven[i, j : j + 1, :] = s_ref[line : line + 1, lane + 64 : lane + 256]
    gain1[...] = s_ref[9:10, :width]
    gain2[...] = s_ref[10:11, :width]


def ends_kernel(split, *refs):
    ins, qkv_ref, outs = refs[:4], refs[4], refs[5:]
    total = ins[0][0]
    for ref in ins[1:]:
        total = total + ref[0].astype(F32)
    qkv_ref[...] = total
    outs[-1][...] = sum_small([ref.at[1] for ref in ins])
    if split:
        small_kernel(outs[-1], *outs[:-1])


SMEM = pl.BlockSpec(memory_space=pltpu.SMEM)
VMEM = pl.BlockSpec(memory_space=pltpu.VMEM)
ANY = pl.BlockSpec(memory_space=pl.ANY)


def by_micro(shape):
    rest = tuple(shape[1:])
    return pl.BlockSpec((1,) + rest, lambda m: (m,) + (0,) * len(rest))


def whole_spec(shape):
    return pl.BlockSpec(tuple(shape), lambda *_: (0,) * len(shape))


def shaped(shape, dtype):
    return jax.ShapeDtypeStruct(tuple(shape), dtype)


def call(
    kernel, name, grid, ins, outs, scratch, micros_long, deps=(), alias=None, carry=(), rows_here=8,
    limit=None
):
    nbytes = sum(a.size * a.dtype.itemsize for _, a in ins)
    nbytes += sum(math.prod(s) * jnp.dtype(d).itemsize for _, s, d in outs)
    first, last = len(ins), len(ins) + len(deps) + len(carry)
    results = last + len(outs)

    def body(*refs):
        if ins and ins[0][0] is SMEM:
            refs = (Here(refs[0], rows_here),) + refs[1:]
        kernel(*refs[:first], *refs[last:results], *refs[results + len(carry) :])

    alias = dict(alias or {})
    for n in range(len(carry)):
        alias[first + len(deps) + n] = len(outs) + n
    return pl.pallas_call(
        body,
        name=name,
        grid=grid,
        in_specs=[s for s, _ in ins] + [ANY] * (len(deps) + len(carry)),
        out_specs=[s for s, _, _ in outs] + [ANY] * len(carry),
        out_shape=[shaped(s, d) for _, s, d in outs] + [shaped(c.shape, c.dtype) for c in carry],
        scratch_shapes=scratch,
        input_output_aliases=alias,
        cost_estimate=pl.CostEstimate(
            flops=int(micros_long * 1.15e9), bytes_accessed=int(nbytes), transcendentals=0
        ),
        compiler_params=pltpu.CompilerParams(
            vmem_limit_bytes=(limit or VMEM_MIB) * MIB, dimension_semantics=("arbitrary",) * len(grid)
        ),
    )(*[a for _, a in ins], *deps, *carry)


def gate_kernel(*refs):
    pass


def gate(values, deps):
    return call(gate_kernel, "gate", (), [], [], [], 0, deps=deps, carry=values)


def add_parts(arrays, parts, deps=(), carry=()):
    n, block = arrays[0].shape[1], tuple(arrays[0].shape[2:])
    per = 2 if n % 2 == 0 else 1
    rest = (0,) * len(block)
    return call(
        functools.partial(add_kernel, parts),
        "add_parts",
        (n // per,),
        [(pl.BlockSpec((parts, per) + block, lambda i: (0, i) + rest), a) for a in arrays],
        [
            (
                pl.BlockSpec((per,) + block, lambda i: (i,) + rest),
                (n,) + block,
                F32 if p == 0 and n == 1 else BF,
            )
            for p in range(parts)
        ],
        [],
        2,
        deps,
        carry=carry,
    )


def add_small(arrays, small, parts, deps=()):
    blocks, rows, lanes = arrays[0].shape
    shape = ((blocks if small else blocks - 1) // parts + 1, rows, lanes)
    every = list(arrays) + list(small)
    return call(
        functools.partial(add_small_kernel, parts, len(arrays)),
        "add_small",
        (1,),
        [(whole_spec(a.shape), a) for a in every],
        [(whole_spec(shape), shape, F32 if p == 0 else BF) for p in range(parts)],
        [],
        0,
        deps,
    )


def local(
    images,
    cotangent,
    extent,
    w_qkv,
    w_out,
    w_up,
    w_down,
    pos_weight,
    win_three,
    win_five,
    win_seven,
    gain_one,
    gain_two,
):
    micros, _, rows, cols, width = images.shape
    head = width // HEADS
    hidden = w_up.shape[1]
    tokens = rows * cols
    me = positions()
    lead_masks, first, second, third = plan(w_up.shape[0])
    lead = len(lead_masks)
    stages = (first, second, third)
    sc = (SMEM, extent)
    n5 = 128
    gain1, gain2 = gain_one.reshape(1, width), gain_two.reshape(1, width)
    pad_rim = pltpu.VMEM((width // 128, rows + 2 * RIM, cols + 2 * EDGE, 128), F32)
    pad_one = pltpu.VMEM((width // 128, rows + 2, cols + 2 * EDGE, 128), F32)

    flat = (micros, tokens, width)
    map_shape = (micros, rows, cols, width)
    rim_shape = (micros, cols, rim_lanes(width)[1])
    q_block = join_lead(w_qkv, lead_masks)
    joined = [join_lead(w, lead_masks) for w in (w_out, w_up, w_down)]
    block_shape = (1 + 2 * (hidden // width), 16, width)
    taps3, w3, w5, w7, r_block = call(
        prep_kernel,
        "prep",
        (1,),
        [
            (whole_spec(w.shape), w)
            for w in (pos_weight, win_three, win_five, win_seven, *joined)
        ],
        [
            (whole_spec(shape), shape, F32)
            for shape in ((9, width), (9, 128), (25, n5), (49, 256))
        ]
        + [(whole_spec(block_shape), block_shape, BF)],
        [],
        2,
    )
    windows = [(whole_spec(w.shape), w) for w in (w3, w5, w7)]

    def gather_second(own):
        return [own] + [flipped(own, m) for m in spans(second)[1:]]

    def gather_third(pieces):
        return pieces + [flipped(p, third[0]) for p in pieces]

    marks = spans(second)
    marks = marks + [m ^ third[0] for m in marks]
    r_marks = [[m ^ f for f in spans(first[::-1])] for m in marks]
    marks = [[m ^ f for f in spans(first)] for m in marks]

    def single(shape, micro):
        rest = tuple(shape[1:])
        return pl.BlockSpec((1,) + rest, lambda m: (micro,) + (0,) * len(rest))

    q_blocks = [q_block] + [flipped(q_block, m) for m in spans(first)[1:]]
    edge = (micros, 1, cols, width)

    def edge_spec(row):
        return pl.BlockSpec((micros, 1, 1, cols, width), lambda _: (0, 0, row, 0, 0))

    own_shape = (len(q_blocks),) + q_block.shape
    q_own, x_first, x_last = call(
        functools.partial(first_kernel, len(q_blocks)),
        "first",
        (1,),
        [(VMEM if n else whole_spec(b.shape), b) for n, b in enumerate(q_blocks)]
        + [(edge_spec(0), images), (edge_spec(rows - 1), images)],
        [
            (whole_spec(own_shape), own_shape, BF),
            (whole_spec(edge), edge, BF),
            (whole_spec(edge), edge, BF),
        ],
        [],
        1,
        deps=[r_block],
        limit=16,
    )
    x_top, x_bot = rims(x_first, x_last)
    q_pieces = gather_second(q_own)
    x_in = pl.BlockSpec((1, 1, rows, cols, width), lambda m: (m, 0, 0, 0, 0))
    r_own = r_block[None]
    for mask in first[::-1]:
        r_own = jnp.concatenate([r_own, flipped(r_own, mask)])
    normed, resid = call(
        norm_kernel,
        "norm",
        (micros,),
        [
            sc,
            (x_in, images),
            (by_micro(edge), x_top),
            (by_micro(edge), x_bot),
            (whole_spec(taps3.shape), taps3),
            (whole_spec(gain1.shape), gain1),
        ],
        [(by_micro(map_shape), map_shape, BF), (by_micro(map_shape), map_shape, F32)],
        [pad_one],
        8,
    )
    qkv_pieces = gather_third(q_pieces)
    r_pieces = list(gate([r_own] + [flipped(r_own, m) for m in second], [normed]))
    r_pieces = r_pieces + [flipped(r_pieces[1], second[1])]
    sums_shape = (micros, head + 16, width)
    q, k, v, sums, v_first, v_last = call(
        functools.partial(qkv_kernel, marks, lead),
        "qkv",
        (micros,),
        [sc, (by_micro(map_shape), normed)] + [(ANY, p) for p in qkv_pieces],
        [
            (by_micro(flat), flat, BF),
            (by_micro(flat), flat, BF),
            (by_micro(map_shape), map_shape, BF),
            (by_micro(sums_shape), sums_shape, BF),
            (by_micro(rim_shape), rim_shape, BF),
            (by_micro(rim_shape), rim_shape, BF),
        ],
        [pltpu.VMEM((width, 3 * width), BF), pltpu.SemaphoreType.DMA],
        6,
        deps=[r_own],
    )

    def join_strips(kernel, cells, stage, dtype, deps, carry=()):
        parts = [cells] + [strip_swap(cells, m) for m in spans(stage)[1:]]
        spec = whole_spec(cells.shape)
        return call(
            kernel,
            "join",
            (1,),
            [(spec, p) for p in parts],
            [(spec, cells.shape, dtype)],
            [],
            1,
            deps=deps,
            carry=carry,
        )

    near, far = strip_stages()
    v_top, v_bot = rims(v_first, v_last)
    (conv,) = call(
        window_kernel,
        "window",
        (micros,),
        [(by_micro(map_shape), v)] + windows,
        [(by_micro(map_shape), map_shape, F32)],
        [pltpu.VMEM((width // 128, rows, cols + 2 * EDGE, 128), F32)],
        6,
    )
    join = functools.partial(join_kernel, head)
    (sums,) = join_strips(join, sums, near, BF, [v_top, v_bot, conv])
    (conv,) = call(
        window_rim_kernel,
        "window_rim",
        (micros,),
        [
            (by_micro(map_shape), conv),
            (by_micro(rim_shape), v_top),
            (by_micro(rim_shape), v_bot),
        ]
        + windows,
        [(by_micro(map_shape), map_shape, F32)],
        [pltpu.VMEM((width // 128, 2 * RIM, cols + 2 * EDGE, 128), F32)],
        3,
        deps=[sums],
    )
    r_pieces = list(gate(r_pieces, [sums]))
    sums_got = [strip_swap(sums, m) for m in spans(far)[1:]]
    rest_pieces = gather_third(r_pieces)

    tile_rows = rows
    tile = tile_rows * cols
    tiles = rows // tile_rows

    def tiled(lanes):
        return pl.BlockSpec((1, tile, lanes), lambda m, t: (m, t, 0))

    def per_micro(shape):
        return pl.BlockSpec((1,) + tuple(shape[1:]), lambda m, t: (m,) + (0,) * (len(shape) - 1))

    wide = (micros, tokens, hidden)
    gkv_shape = (micros, head, width)
    outs = call(
        functools.partial(main_kernel, r_marks, 1 + len(sums_got), lead),
        "main",
        (micros, tiles),
        [
            sc,
            (tiled(width), q),
            (tiled(width), conv.reshape(flat)),
            (tiled(width), resid.reshape(flat)),
            (tiled(width), cotangent.reshape(flat)),
            (whole_spec(gain2.shape), gain2),
        ]
        + [(per_micro(sums_shape), a) for a in [sums] + sums_got]
        + [(ANY, p) for p in rest_pieces],
        [
            (per_micro(sums_shape), sums_shape, F32),
            (tiled(width), flat, BF),
            (tiled(hidden), wide, BF),
            (tiled(hidden), wide, BF),
            (tiled(width), flat, BF),
            (tiled(width), flat, BF),
            (tiled(width), flat, BF),
            (tiled(width), flat, BF),
            (tiled(width), flat, F32),
            (tiled(width), flat, BF),
            (tiled(width), flat, F32),
            (per_micro(gkv_shape), gkv_shape, BF),
            (per_micro(rim_shape), rim_shape, BF),
            (per_micro(rim_shape), rim_shape, BF),
            (whole_spec((1, width)), (1, width), F32),
        ],
        [
            pltpu.VMEM((width, width), BF),
            pltpu.VMEM((hidden // width, width, width), BF),
            pltpu.VMEM((width // 16, 4, 16, width), BF),
            pltpu.VMEM((width // (4 * head), 4 * head, 4 * head), BF),
            pltpu.VMEM((width // (4 * head), 4 * head, 4 * head), F32),
            pltpu.SemaphoreType.DMA,
            pltpu.SemaphoreType.DMA,
            pltpu.SemaphoreType.DMA,
        ],
        24,
    )
    sums, out, act, g_hidden, n2, att, g_ffn, g_proj, g_conv, gq, g_middle, gkv = outs[:12]
    gc_first, gc_last, ggain2 = outs[12:]
    g_conv = g_conv.reshape(map_shape)
    gc_top, gc_bot = rims(gc_first, gc_last)

    first, second = sum_stages(first, second)
    marked = [0]
    for stage in (first, second, third):
        marked = [o ^ m for m in spans(stage) for o in marked]
    slots = len(marked) // 2

    def flat2(a):
        return a.reshape(-1, a.shape[-1])

    def staged(block, parts):
        return block.reshape((parts, block.shape[0] // parts) + block.shape[1:])

    half_shape = (slots,) + block_shape
    ops = [flat2(a) for a in (n2, g_hidden, act, g_ffn, att, g_proj)]
    chunk = 512

    def columns(a):
        return pl.BlockSpec((a.shape[0], chunk), lambda c: (0, c))

    keep, send = call(
        functools.partial(up_kernel, marked, lead),
        "mlp_grads",
        (hidden // chunk,),
        [sc]
        + [
            (columns(a) if a.shape[1] == hidden else whole_spec(a.shape), a)
            for a in ops
        ],
        [(whole_spec(half_shape), half_shape, BF)] * 2,
        [pltpu.VMEM((width, chunk), F32), pltpu.VMEM((hidden, width), F32)],
        12,
    )
    gkv_parts = [gkv] + [strip_swap(gkv, m) for m in spans(near)[1:]]
    gkv = functools.reduce(jnp.add, [p.astype(F32) for p in gkv_parts]).astype(BF)
    (send,) = gate([send], [gkv, gc_top, gc_bot, keep])
    got = flipped(send, third[0])
    gkv_got = [strip_swap(gkv, m) for m in spans(far)[1:]]
    o3, o5, o7 = call(
        taps_kernel,
        "window_grads",
        (micros,),
        [
            (by_micro(map_shape), v),
            (by_micro(rim_shape), v_top),
            (by_micro(rim_shape), v_bot),
            (by_micro(map_shape), g_conv),
        ],
        [
            (whole_spec((9, 128)), (9, 128), F32),
            (whole_spec((25, 128)), (25, 128), F32),
            (whole_spec((49, 256)), (49, 256), F32),
        ],
        [pad_rim, pltpu.VMEM((49, 8, 128), F32)],
        6,
        deps=[send],
    )
    parts2, parts1 = len(spans(second)), len(spans(first))
    rest = add_parts([staged(keep, parts2), staged(got, parts2)], parts2, [o3] + gkv_got)
    rest_got = [flipped(o, m) for o, m in zip(rest[1:], spans(second)[1:])]

    half_shape = (slots, 16, 3 * width)
    g_u, gu_first, gu_last, ggain1, keep, send = call(
        functools.partial(back_kernel, marks, marked, 1 + len(gkv_got), lead),
        "back",
        (micros,),
        [
            sc,
            (by_micro(map_shape), normed),
            (by_micro(flat), k),
            (by_micro(map_shape), v),
            (by_micro(sums_shape), sums),
            (by_micro(map_shape), g_conv),
            (by_micro(rim_shape), gc_top),
            (by_micro(rim_shape), gc_bot),
            (by_micro(flat), gq),
            (by_micro(flat), resid.reshape(flat)),
            (by_micro(flat), g_middle),
            (whole_spec(gain1.shape), gain1),
        ]
        + windows
        + [(by_micro(gkv_shape), g) for g in [gkv] + gkv_got]
        + [(ANY, p) for p in qkv_pieces],
        [
            (by_micro(map_shape), map_shape, F32),
            (by_micro(edge), edge, BF),
            (by_micro(edge), edge, BF),
            (whole_spec((1, width)), (1, width), F32),
            (whole_spec(half_shape), half_shape, BF),
            (whole_spec(half_shape), half_shape, BF),
        ],
        [
            pltpu.VMEM((tokens, 3 * width), BF),
            pltpu.VMEM((width, 3 * width), F32),
            pltpu.VMEM((width, 3 * width), BF),
            pad_rim,
            pltpu.VMEM((rows, cols, width), F32),
            pltpu.SemaphoreType.DMA,
        ],
        15,
        deps=[rest[0]],
    )
    gu_top, gu_bot = rims(gu_first, gu_last)
    small_shape = (16, 3 * width)
    (small,) = call(
        pos_grad_kernel,
        "pos_grad",
        (micros,),
        [
            sc,
            (x_in, images),
            (by_micro(x_top.shape), x_top),
            (by_micro(x_bot.shape), x_bot),
            (by_micro(map_shape), g_u),
        ]
        + [(whole_spec(a.shape), a) for a in (o3, o5, o7, ggain1, ggain2)],
        [(whole_spec(small_shape), small_shape, BF)],
        [
            pad_one,
            pltpu.VMEM((9, 8, 128), F32),
            pltpu.VMEM((9, width), F32),
            pltpu.VMEM(small_shape, F32),
        ],
        1,
    )
    send, small_send = gate([send, small], rest_got + [gu_top, gu_bot])
    got, small_got = flipped(send, third[0]), flipped(small_send, third[0])
    rest = add_parts([staged(p, parts1) for p in [rest[0]] + rest_got], parts1)
    own = add_small([keep, got], [small_send, small_got], parts2, [rest[0]])
    own_got = [flipped(o, m) for o, m in zip(own[1:], spans(second)[1:])]
    rest_got = [flipped(o, m) for o, m in zip(rest[1:], spans(first)[1:])]
    (grad_in,) = call(
        start_grad_kernel,
        "input_grad",
        (micros,),
        [
            sc,
            (by_micro(map_shape), g_u),
            (by_micro(gu_top.shape), gu_top),
            (by_micro(gu_bot.shape), gu_bot),
            (whole_spec(taps3.shape), taps3),
        ],
        [(x_in, (micros, 1, rows, cols, width), F32)],
        [pad_one],
        3,
        deps=[own[0]],
    )
    own = [own[0]] + own_got
    own = add_small(own, [], parts1, [grad_in])
    own_got = [flipped(o, m) for o, m in zip(own[1:], spans(first)[1:])]
    own = [own[0]] + own_got
    rest = [rest[0]] + rest_got

    def lead_sum(total):
        for mask in reversed(lead_masks):
            size = total.shape[0] // 2
            low, high = total[:size], total[size:]
            bit = (me & mask) != 0
            kept, sent = jnp.where(bit, high, low), jnp.where(bit, low, high)
            total = kept + flipped(sent, mask)
        return total

    def call_whole(kernel, name, arrays, shapes, deps=()):
        return call(
            kernel,
            name,
            (1,),
            [(VMEM if n else whole_spec(a.shape), a) for n, a in enumerate(arrays)],
            [(whole_spec(shape), shape, F32) for shape in shapes],
            [],
            1,
            deps=deps,
            limit=16,
        )

    rest_shapes = [(16, width), (16, hidden), (64, width)]
    grad_out, grad_up, grad_down = call_whole(rest_kernel, "rest_sum", rest, rest_shapes, own[:1])
    small_shapes = [w.shape for w in (pos_weight, win_three, win_five, win_seven)]
    small_shapes = small_shapes + [gain1.shape] * 2
    if lead_masks:
        grad_out, grad_up, grad_down = (lead_sum(g) for g in (grad_out, grad_up, grad_down))
        grad_qkv, small = call_whole(
            functools.partial(ends_kernel, False), "last_sum", own, [small_shape] * 2
        )
        grad_qkv = lead_sum(grad_qkv)
        low = small.astype(BF)
        got = [low.astype(F32)] + [flipped(low, m).astype(F32) for m in spans(lead_masks)[1:]]
        while len(got) > 1:
            got = [a + b for a, b in zip(got[::2], got[1::2])]
        smalls = call_whole(small_kernel, "small_grads", got, small_shapes)
    else:
        grad_qkv, *smalls, _ = call_whole(
            functools.partial(ends_kernel, True),
            "last_sum",
            own,
            [small_shape] + small_shapes + [small_shape],
        )
    g_pos, g_three, g_five, g_seven, ggain1, ggain2 = smalls
    return (
        out.reshape(micros, 1, rows, cols, width),
        grad_in,
        grad_qkv,
        grad_out,
        grad_up,
        grad_down,
        g_pos,
        g_three,
        g_five,
        g_seven,
        ggain1.reshape(width),
        ggain2.reshape(width),
    )


def solution(mesh):
    in_specs = (
        P(None, "img", "strip", None, None),
        P(None, "img", "strip", None, None),
        P(None, "img", None),
        P(("img", "strip"), None),
        P(("img", "strip"), None),
        P(("img", "strip"), None),
        P(("img", "strip"), None),
        P(),
        P(),
        P(),
        P(),
        P(),
        P(),
    )
    out_specs = (
        P(None, "img", "strip", None, None),
        P(None, "img", "strip", None, None),
        P(("img", "strip"), None),
        P(("img", "strip"), None),
        P(("img", "strip"), None),
        P(("img", "strip"), None),
        P(),
        P(),
        P(),
        P(),
        P(),
        P(),
    )
    return jax.shard_map(local, mesh=mesh, in_specs=in_specs, out_specs=out_specs, check_vma=False)
```
